256 devices in a mesh: grp: 4 (over y), slab: 64 (over z, x, core).
Axes of the slice: x: 4, y: 4, z: 8, core: 2. Of those that a mesh axis runs over, the one named last changes fastest.
Arguments:
- base_field: bfloat16 [64, 128, 128, 128], P(None, 'slab'), may hold values from -6 to 6
- cotangent: bfloat16 [4, 64, 128, 128, 128], P('grp', None, 'slab'), may hold values from -6 to 6
- w_spec: bfloat16 [16, 256, 64, 128], P('grp', 'slab'), may hold values from -0.75 to 0.75
- w_local: bfloat16 [64, 64], replicated, may hold values from -0.75 to 0.75
- bias: float32 [64], replicated, may hold values from -3 to 3
- direction: int32 [64, 30], replicated, may hold values from 0 to 1073741823
- shift: int32 [4, 64], P('grp'), may hold values from 0 to 1073741823
Outputs:
- output: bfloat16 [4, 64, 128, 128, 128], P('grp', None, 'slab')
- d_spec: float32 [16, 256, 64, 128], P('grp', 'slab')
- d_local: float32 [64, 64], replicated
- d_bias: float32 [64], replicated
The draws below stay inside these ranges and needn't reach their ends.
All inputs are finite; a program needn't handle non-finite values.
Results may differ from the reference program's by a relative error of at most 0.024.
Values may be sent and summed in bfloat16 or wider, within the bound.
A program may use at most 128 MiB of HBM per device.

```python
import math
import jax
import jax.numpy as jnp
from jax import lax

CH = 64
NY = 128
NZ = 128
MODES = 16
BITS = 30
NX = 128
N_GRP = 4


def touch_ends(result, key, smallest, high):
    shape = result.shape
    index_at = [jax.random.randint(jax.random.fold_in(key, axis), (), 0, shape[axis]) for axis in range(len(shape))]
    result = result.at[tuple(index_at)].set(smallest)
    longest = shape.index(max(shape))
    index_at[longest] = (index_at[longest] + 1) % shape[longest]
    return result.at[tuple(index_at)].set(high)


def steps_of(key, extent, split, low, largest):
    level = 1.0
    for position, parts in split:
        draws = jax.random.uniform(jax.random.fold_in(jax.random.fold_in(key, 6), position), (parts,), jnp.float32, low / len(split), largest / len(split))
        level = level * jnp.repeat(jnp.exp(draws), extent[position] // parts).reshape((-1,) + (1,) * (len(extent) - 1 - position))
    return level


def noise(own_key, dims, spread, reach, split=(), held_as=jnp.bfloat16):
    drawn = spread * jax.random.normal(own_key, dims, jnp.float32)
    if split:
        drawn = drawn * steps_of(own_key, dims, split, -0.22, 0.18)
    return jnp.clip(drawn, -reach, reach).astype(held_as)


def setup_inputs(seed: int = 0) -> dict:
    arg_keys = jax.random.split(jax.random.key(seed), 8)
    return {
        "base_field": noise(arg_keys[0], (CH, NX, NY, NZ), 1.0, 6.0, ((1, 64),)),
        "cotangent": noise(arg_keys[1], (N_GRP, CH, NX, NY, NZ), 1.0, 6.0, ((0, 4), (2, 64))),
        "w_spec": noise(arg_keys[2], (MODES, MODES * MODES, CH, 2 * CH), CH ** -0.5, 0.75, ((0, 4), (1, 64))),
        "w_local": noise(arg_keys[3], (CH, CH), CH ** -0.5, 0.75),
        "bias": noise(arg_keys[4], (CH,), 0.5, 3.0, (), jnp.float32),
        "direction": touch_ends(jax.random.randint(arg_keys[5], (CH, BITS), 0, 1073741824), jax.random.fold_in(arg_keys[5], 1), 0, 1073741823).astype(jnp.int32),
        "shift": touch_ends(jax.random.randint(arg_keys[6], (N_GRP, CH), 0, 1073741824), jax.random.fold_in(arg_keys[6], 1), 0, 1073741823).astype(jnp.int32),
    }


def wave_tables(mode_count, length, half):
    mode_ids = jnp.arange(mode_count, dtype=jnp.int32)
    if half:
        kept_ids = mode_ids
    else:
        kept_ids = jnp.where(mode_ids < mode_count // 2, mode_ids, length - mode_count + mode_ids)
    points = jnp.arange(length, dtype=jnp.int32)
    phases = kept_ids[:, None] * points[None, :] % length
    angles = 2.0 * math.pi / length * phases.astype(jnp.float32)
    return (jnp.cos(angles), jnp.sin(angles))

def z_tables(mode_count, length):
    cos_z, sin_z = wave_tables(mode_count, length, True)
    weight_k = jnp.where(jnp.arange(mode_count) == 0, 1.0, 2.0).astype(jnp.float32)[:, None]
    forward = jnp.concatenate([cos_z, -sin_z], 0).T.astype(jnp.bfloat16)
    backward = jnp.concatenate([weight_k * cos_z, -weight_k * sin_z], 0).T.astype(jnp.bfloat16)
    inverse = jnp.stack([weight_k * cos_z, -weight_k * sin_z], 1).astype(jnp.bfloat16)
    return (forward, backward, inverse)

def along_yz(values, table_z, cos_y, sin_y):
    channels, rows_x, span_y, span_z = values.shape
    mode_count = cos_y.shape[0]
    along_z = jnp.dot(values.reshape(-1, span_z), table_z, preferred_element_type=jnp.float32)
    along_z = along_z.astype(jnp.bfloat16).reshape(channels, rows_x, span_y, 2 * mode_count)
    cos_part = jnp.einsum('cxyk,jy->xjkc', along_z.astype(jnp.float32), cos_y.astype(jnp.float32))
    sin_part = jnp.einsum('cxyk,jy->xjkc', along_z.astype(jnp.float32), sin_y.astype(jnp.float32))
    real_part = cos_part[:, :, :mode_count] + sin_part[:, :, mode_count:]
    imag_part = cos_part[:, :, mode_count:] - sin_part[:, :, :mode_count]
    joined = jnp.concatenate([real_part, imag_part], -1)
    return joined.reshape(rows_x, mode_count * mode_count, 2 * channels).astype(jnp.bfloat16)

def along_x(pencil, cos_x, sin_x, factor):
    channels = pencil.shape[2] // 2
    flat_rows = pencil.reshape(pencil.shape[0], -1)
    cos_part = jnp.dot(cos_x, flat_rows, preferred_element_type=jnp.float32).reshape(-1, pencil.shape[1], pencil.shape[2])
    sin_part = jnp.dot(sin_x, flat_rows, preferred_element_type=jnp.float32).reshape(-1, pencil.shape[1], pencil.shape[2])
    real_part = cos_part[..., :channels] + sin_part[..., channels:]
    imag_part = cos_part[..., channels:] - sin_part[..., :channels]
    return (jnp.concatenate([real_part, imag_part], -1) * factor).astype(jnp.bfloat16)

def mix_modes(spectrum, weights):
    channels = weights.shape[2]
    cos_part = jnp.einsum('kmc,kmcd->kmd', spectrum[..., :channels].astype(jnp.float32), weights.astype(jnp.float32))
    sin_part = jnp.einsum('kmc,kmcd->kmd', spectrum[..., channels:].astype(jnp.float32), weights.astype(jnp.float32))
    real_part = cos_part[..., :channels] - sin_part[..., channels:]
    imag_part = cos_part[..., channels:] + sin_part[..., :channels]
    return jnp.concatenate([real_part, imag_part], -1).astype(jnp.bfloat16)

def synth_x(spectrum, cos_x, sin_x):
    channels = spectrum.shape[2] // 2
    flat_rows = spectrum.reshape(spectrum.shape[0], -1)
    cos_part = jnp.dot(cos_x.T, flat_rows, preferred_element_type=jnp.float32).reshape(-1, spectrum.shape[1], spectrum.shape[2])
    sin_part = jnp.dot(sin_x.T, flat_rows, preferred_element_type=jnp.float32).reshape(-1, spectrum.shape[1], spectrum.shape[2])
    real_part = cos_part[..., :channels] - sin_part[..., channels:]
    imag_part = cos_part[..., channels:] + sin_part[..., :channels]
    return jnp.concatenate([real_part, imag_part], -1).astype(jnp.bfloat16)

def synth_yz(spectrum, cos_y, sin_y, inverse_z, factor):
    rows_x = spectrum.shape[0]
    channels = spectrum.shape[2] // 2
    mode_count = cos_y.shape[0]
    grid_modes = spectrum.reshape(rows_x, mode_count, mode_count, 2 * channels).astype(jnp.float32)
    cos_part = jnp.einsum('xjkd,jy->xykd', grid_modes, cos_y.astype(jnp.float32))
    sin_part = jnp.einsum('xjkd,jy->xykd', grid_modes, sin_y.astype(jnp.float32))
    real_part = cos_part[..., :channels] - sin_part[..., channels:]
    imag_part = cos_part[..., channels:] + sin_part[..., :channels]
    stacked = jnp.stack([real_part, imag_part], 3).astype(jnp.bfloat16)
    return jnp.einsum('xykrc,krz->cxyz', stacked.astype(jnp.float32), inverse_z.astype(jnp.float32)) * factor

def outer_modes(left_modes, right_modes):
    channels = left_modes.shape[-1] // 2
    left_re = left_modes[..., :channels].astype(jnp.float32)
    left_im = left_modes[..., channels:].astype(jnp.float32)
    right_re = right_modes[..., :channels].astype(jnp.float32)
    right_im = right_modes[..., channels:].astype(jnp.float32)
    first_half = jnp.einsum('kmc,kmd->kmcd', left_re, right_re) + jnp.einsum('kmc,kmd->kmcd', left_im, right_im)
    second_half = jnp.einsum('kmc,kmd->kmcd', left_re, right_im) - jnp.einsum('kmc,kmd->kmcd', left_im, right_re)
    return jnp.concatenate([first_half, second_half], -1)

def reference(base_field, cotangent, w_spec, w_local, bias, direction, shift):
    cos_y, sin_y = wave_tables(MODES, NY, False)
    cos_y, sin_y = (cos_y.astype(jnp.bfloat16), sin_y.astype(jnp.bfloat16))
    cos_x, sin_x = wave_tables(MODES, NX, False)
    cos_x, sin_x = (cos_x.astype(jnp.bfloat16), sin_x.astype(jnp.bfloat16))
    forward_z, backward_z, inverse_z = z_tables(MODES, NZ)
    fwd_scale = 1.0 / math.sqrt(NX * NY * NZ)
    inv_scale = 1.0 / math.sqrt(MODES ** 3)
    grad_scale = 1.0 / math.sqrt(N_GRP * NX * NY * NZ)
    outputs = []
    d_spec = jnp.zeros(w_spec.shape, jnp.float32)
    d_local = jnp.zeros((CH, CH), jnp.float32)
    d_bias = jnp.zeros((CH,), jnp.float32)
    for sample_id in range(N_GRP):
        number = sample_id + 1
        gray_code = number ^ number >> 1
        mixed_bits = jnp.zeros((CH,), jnp.int32)
        for bit_pos in range(BITS):
            if gray_code >> bit_pos & 1:
                mixed_bits = jnp.bitwise_xor(mixed_bits, direction[:, bit_pos])
        sobol_point = jnp.bitwise_xor(mixed_bits, shift[sample_id]).astype(jnp.float32) * 2.0 ** (-30)
        inputs = (base_field.astype(jnp.float32) * (0.5 + sobol_point)[:, None, None, None]).astype(jnp.bfloat16)
        modes_u = along_x(along_yz(inputs, forward_z, cos_y, sin_y), cos_x, sin_x, fwd_scale)
        mixed_modes = mix_modes(modes_u, w_spec)
        spectral = synth_yz(synth_x(mixed_modes, cos_x, sin_x), cos_y, sin_y, inverse_z, inv_scale)
        flat_inputs = inputs.reshape(CH, -1)
        local_term = jnp.dot(w_local, flat_inputs, preferred_element_type=jnp.float32).reshape(spectral.shape)
        pre_act = spectral + local_term + bias[:, None, None, None]
        outputs.append(jax.nn.gelu(pre_act).astype(jnp.bfloat16))
        _, pullback = jax.vjp(jax.nn.gelu, pre_act)
        cotan_pre = pullback(cotangent[sample_id].astype(jnp.float32) * grad_scale)[0].astype(jnp.bfloat16)
        flat_cotan = cotan_pre.reshape(CH, -1)
        d_local = d_local + jnp.dot(flat_cotan, flat_inputs.T, preferred_element_type=jnp.float32)
        d_bias = d_bias + lax.optimization_barrier(jnp.sum(flat_cotan.astype(jnp.float32), axis=1))
        modes_g = along_x(along_yz(cotan_pre, backward_z, cos_y, sin_y), cos_x, sin_x, 1.0)
        d_spec = d_spec + outer_modes(modes_u, modes_g)
    return (jnp.stack(outputs, 0), d_spec, d_local, d_bias)
```

```python
from functools import reduce
import math

import jax
import jax.numpy as jnp
import ml_dtypes
import numpy as np
from jax import lax
from jax.experimental import pallas as pl
from jax.experimental.pallas import tpu as pltpu
from jax.sharding import PartitionSpec as P

CH = 64
NX = 128
NY = 128
NZ = 128
MODES = 16
BITS = 30
N_GRP = 4
N_SLAB = 64
N_LOW = 8
N_Z = 8
MESH = pl.DeviceIdType.MESH
F32 = jnp.float32
BF16 = jnp.bfloat16
MIB = 1024 * 1024


def waves(length, half):
    ids = np.arange(MODES)
    if not half:
        ids = np.where(ids < MODES // 2, ids, length - MODES + ids)
    angles = 2.0 * math.pi / length * (ids[:, None] * np.arange(length)[None, :] % length)
    return np.cos(angles), np.sin(angles)


def as_bf16(table):
    return np.asarray(table, np.float32).astype(ml_dtypes.bfloat16)


def table_ty():
    cos_y, sin_y = waves(NY, False)
    out = np.zeros((2, 2, MODES, 2, NY))
    for c2 in range(2):
        out[0, c2, :, c2] = cos_y
        out[1, c2, :, c2] = sin_y
    return as_bf16(out.reshape(64, 256))


def weights_z(backward):
    return np.where(np.arange(MODES) == 0, 1.0, 2.0 if backward else 1.0)[:, None]


def table_zt(backward):
    cos_z, sin_z = waves(NZ, True)
    weight = weights_z(backward)
    cos_z = (weight * cos_z).reshape(4, 4, NZ)
    sin_z = (weight * sin_z).reshape(4, 4, NZ)
    out = np.zeros((2, 4, 2, 4, 2, 2, NZ))
    for x in range(2):
        out[0, :, x, :, 0, x] = cos_z
        out[0, :, x, :, 1, x] = -sin_z
        out[1, :, x, :, 0, x] = -sin_z
        out[1, :, x, :, 1, x] = -cos_z
    return as_bf16(out.reshape(64, 512))


def table_tx():
    cos_x, sin_x = waves(NX, False)
    out = np.zeros((2, MODES, 4, NX, 4))
    for m in range(4):
        out[0, :, m, :, m] = cos_x
        out[1, :, m, :, m] = sin_x
    return as_bf16(out.reshape(128, 512))


def table_ey():
    cos_y, sin_y = waves(NY, False)
    out = np.zeros((2, NY, 2, 2, MODES))
    for c2 in range(2):
        out[c2, :, c2, 0] = cos_y.T
        out[c2, :, c2, 1] = -sin_y.T
    return as_bf16(out.reshape(256, 64))


def table_ez():
    cos_z, sin_z = waves(NZ, True)
    weight = weights_z(True) / math.sqrt(MODES**3)
    cos_z = (weight * cos_z).reshape(4, 4, NZ)
    sin_z = (weight * sin_z).reshape(4, 4, NZ)
    out = np.zeros((2, 4, 2, 4, 2, 2, NZ))
    for x in range(2):
        out[0, :, x, :, 0, x] = cos_z
        out[1, :, x, :, 0, x] = -sin_z
        out[0, :, x, :, 1, x] = sin_z
        out[1, :, x, :, 1, x] = cos_z
    return as_bf16(out.reshape(64, 512))


def lane_sign(rows, first, second):
    lane = lax.broadcasted_iota(jnp.int32, (rows, 128), 1)
    return jnp.where(lane < 64, first, second).astype(F32)


def turned(rows, first, second):
    return pltpu.roll(rows, 64, 1) * lane_sign(rows.shape[0], first, second)


def nt_dot(left, right, precision=None):
    return lax.dot_general(
        left, right, (((1,), (1,)), ((), ())), preferred_element_type=F32, precision=precision
    )


def fetch_field(field, held, sems):
    for part in range(8):
        rows = pl.ds(8 * part, 8)
        pltpu.make_async_copy(field.at[rows], held.at[rows], sems.at[part]).start()


def analyse(field, held, sems, ty_ref, zt_ref, along_y, slab_modes):

    def channels(part, carry):
        rows = pl.ds(8 * part, 8)
        pltpu.make_async_copy(field.at[rows], held.at[rows], sems.at[part]).wait()
        for pair in range(4):
            first = 8 * part + 2 * pair
            cells = jnp.concatenate(
                [
                    jnp.concatenate([held[first + c2, 0], held[first + c2, 1]], 1)
                    for c2 in range(2)
                ],
                0,
            )
            got = jnp.dot(ty_ref[...], cells, preferred_element_type=F32)
            for cs in range(2):
                for c2 in range(2):
                    at = cs * 32 + c2 * 16
                    for x in range(2):
                        start = (2 * cs + x) * 1024 + first + c2
                        along_y[pl.ds(start, 16, stride=64), :] = got[
                            at : at + 16, x * 128 : x * 128 + 128
                        ]
        return carry

    lax.fori_loop(0, 8, channels, 0)
    for quarter in range(4):
        rows = jnp.concatenate(
            [
                along_y[part * 1024 + quarter * 256 : part * 1024 + quarter * 256 + 256, :]
                for part in range(4)
            ],
            1,
        ).astype(BF16)
        got = nt_dot(zt_ref[...], rows)
        for jy in range(4):
            real = got[0:32, jy * 64 : jy * 64 + 64]
            imag = got[32:64, jy * 64 : jy * 64 + 64]
            owner = (quarter * 4 + jy) * 4
            slab_modes[owner : owner + 4] = (
                jnp.concatenate([real, imag], 1).reshape(4, 8, 128).astype(BF16)
            )


def greet(barrier, me, grp):
    def tell(step, carry):
        pl.semaphore_signal(
            barrier, inc=1, device_id={"slab": lax.rem(me + step, N_SLAB)}, device_id_type=MESH
        )
        return carry

    lax.fori_loop(1, N_SLAB, tell, 0)
    for step in range(1, N_GRP):
        pl.semaphore_signal(
            barrier, inc=1, device_id={"grp": lax.rem(grp + step, N_GRP)}, device_id_type=MESH
        )


def send_all(source, target, send_sem, recv_sem, me):
    low = lax.rem(me, N_LOW)
    z = me // N_LOW
    for dz in (4, 3, 5, 2, 6, 1, 7, 0):

        def go(step, carry):
            other = lax.rem(z + dz, N_Z) * N_LOW + lax.rem(low + step, N_LOW)
            pltpu.make_async_remote_copy(
                src_ref=source.at[other],
                dst_ref=target.at[me],
                send_sem=send_sem,
                recv_sem=recv_sem,
                device_id={"slab": other},
                device_id_type=MESH,
            ).start()
            return carry

        lax.fori_loop(1 if dz == 0 else 0, N_LOW, go, 0)
    target[pl.ds(me, 1)] = source[pl.ds(me, 1)]


def wait_blocks(source, target, send_sem, recv_sem, count, me):
    pltpu.make_async_remote_copy(
        src_ref=source.at[pl.ds(0, count)],
        dst_ref=target.at[pl.ds(0, count)],
        send_sem=send_sem,
        recv_sem=recv_sem,
        device_id={"slab": me},
        device_id_type=MESH,
    ).wait()


def send_grp(source, target, send_sem, recv_sem, grp, by_target):
    for step in range(1, N_GRP):
        other = lax.rem(grp + step, N_GRP)
        pltpu.make_async_remote_copy(
            src_ref=source.at[other] if by_target else source.at[grp],
            dst_ref=target.at[grp],
            send_sem=send_sem,
            recv_sem=recv_sem,
            device_id={"grp": other},
            device_id_type=MESH,
        ).start()


def x_modes(pencil, tx_ref):
    rows = pencil[...].astype(F32).reshape(512, 128).astype(BF16)
    both = jnp.dot(tx_ref[...], rows, preferred_element_type=F32)
    return both[:64] + turned(both[64:], 1.0, -1.0)


def spectral_kernel(
    field, w_ref, wl_ref, scale_ref, ty_ref, zt_ref, tx_ref, txb_ref,
    grid_modes, own_modes, scales, kron_ref,
    held, along_y, slab_modes, pencil, mixed, gathered, back, landed, all_modes, scale_own, scale_all, w_two,
    field_sems, send_sems, recv_sems,
):
    me = lax.axis_index("slab")
    grp = lax.axis_index("grp")
    barrier = pltpu.get_barrier_semaphore()
    fetch_field(field, held, field_sems)
    greet(barrier, me, grp)
    analyse(field, held, field_sems, ty_ref, zt_ref, along_y, slab_modes)
    scale_own[grp] = scale_ref[...]
    scale_all[grp] = scale_ref[...]
    pl.semaphore_wait(barrier, N_SLAB - 1 + N_GRP - 1)
    send_all(slab_modes, pencil, send_sems.at[0], recv_sems.at[0], me)
    send_grp(scale_own, scale_all, send_sems.at[1], recv_sems.at[1], grp, False)
    for k in range(16):
        block = w_ref[k].astype(F32)
        w_two[k * 128 : k * 128 + 64, :] = w_ref[k]
        w_two[k * 128 + 64 : k * 128 + 128, :] = turned(block, -1.0, 1.0).astype(BF16)
    local = (wl_ref[...].astype(F32) * scale_ref[0:1, 0:64]).astype(BF16)
    pick = (
        lax.broadcasted_iota(jnp.int32, (64, 512), 0)
        == lax.broadcasted_iota(jnp.int32, (64, 512), 1) // 8
    )
    wide = jnp.dot(local, pick.astype(F32).astype(BF16), preferred_element_type=F32).astype(BF16)
    row_pick = (
        lax.broadcasted_iota(jnp.int32, (64, 64), 0) // 8
        == lax.broadcasted_iota(jnp.int32, (64, 64), 1)
    )
    same = (
        lax.broadcasted_iota(jnp.int32, (64, 512), 0) % 8
        == lax.broadcasted_iota(jnp.int32, (64, 512), 1) % 8
    )
    row_ids = lax.broadcasted_iota(jnp.int32, (64, 64), 0) // 8
    col_ids = lax.broadcasted_iota(jnp.int32, (64, 64), 1)
    for octet in range(8):
        rows_of = (row_ids + 8 * octet == col_ids).astype(F32).astype(BF16)
        tall = jnp.dot(rows_of, wide, preferred_element_type=F32)
        kron_ref[octet * 64 : octet * 64 + 64, :] = jnp.where(same, tall, 0.0).astype(BF16)
    pltpu.make_async_remote_copy(
        src_ref=scale_own.at[pl.ds(0, N_GRP - 1)],
        dst_ref=scale_all.at[pl.ds(0, N_GRP - 1)],
        send_sem=send_sems.at[1],
        recv_sem=recv_sems.at[1],
        device_id={"slab": me},
        device_id_type=MESH,
    ).wait()
    scales[...] = scale_all[...]
    wait_blocks(slab_modes, pencil, send_sems.at[0], recv_sems.at[0], N_SLAB - 1, me)
    all_modes[...] = x_modes(pencil, tx_ref) * (1.0 / math.sqrt(NX * NY * NZ))
    own = all_modes[pl.ds(pl.multiple_of(16 * grp, 16), 16), :]
    own_modes[...] = own
    shifted = jnp.concatenate([own * scale_all[s, 0:1, :] for s in range(N_GRP)], 0)
    row_mode = lax.broadcasted_iota(jnp.int32, (64, 128), 0) % 16
    spread = jnp.concatenate(
        [jnp.where(row_mode == k, shifted, 0.0).astype(BF16) for k in range(16)], 1
    )
    mixed[...] = (
        jnp.dot(spread, w_two[...], preferred_element_type=F32).astype(BF16).reshape(4, 16, 128)
    )
    send_grp(mixed, gathered, send_sems.at[2], recv_sems.at[2], grp, True)
    gathered[pl.ds(grp, 1)] = mixed[pl.ds(grp, 1)]
    wait_blocks(mixed, gathered, send_sems.at[2], recv_sems.at[2], N_GRP - 1, me)
    full = gathered[...].reshape(64, 128)
    both = jnp.concatenate([full, turned(full.astype(F32), -1.0, 1.0).astype(BF16)], 0)
    cells = jnp.dot(txb_ref[...], both, preferred_element_type=F32)
    back[...] = cells.reshape(64, 8, 128).astype(BF16)
    send_all(back, landed, send_sems.at[3], recv_sems.at[3], me)
    wait_blocks(back, landed, send_sems.at[3], recv_sems.at[3], N_SLAB - 1, me)
    grid_modes[...] = landed[...]


def spectral_call(field, w_spec, w_local, scale_rows):
    vmem = pl.BlockSpec(memory_space=pltpu.VMEM)
    return pl.pallas_call(
        spectral_kernel,
        out_shape=(
            jax.ShapeDtypeStruct((64, 8, 128), BF16),
            jax.ShapeDtypeStruct((16, 128), F32),
            jax.ShapeDtypeStruct((4, 8, 128), F32),
            jax.ShapeDtypeStruct((512, 512), BF16),
        ),
        in_specs=[pl.BlockSpec(memory_space=pl.ANY)] + [vmem] * 7,
        out_specs=(vmem,) * 4,
        scratch_shapes=[
            pltpu.VMEM((64, 2, 128, 128), BF16),
            pltpu.VMEM((4096, 128), F32),
            pltpu.VMEM((64, 8, 128), BF16),
            pltpu.VMEM((64, 8, 128), BF16),
            pltpu.VMEM((4, 16, 128), BF16),
            pltpu.VMEM((4, 16, 128), BF16),
            pltpu.VMEM((64, 8, 128), BF16),
            pltpu.VMEM((64, 8, 128), BF16),
            pltpu.VMEM((64, 128), F32),
            pltpu.VMEM((4, 8, 128), F32),
            pltpu.VMEM((4, 8, 128), F32),
            pltpu.VMEM((2048, 128), BF16),
            pltpu.SemaphoreType.DMA((8,)),
            pltpu.SemaphoreType.DMA((4,)),
            pltpu.SemaphoreType.DMA((4,)),
        ],
        compiler_params=pltpu.CompilerParams(
            collective_id=0, has_side_effects=True, vmem_limit_bytes=32 * MIB
        ),
    )(
        field, w_spec, w_local, scale_rows,
        table_ty(), table_zt(False), table_tx(), np.ascontiguousarray(table_tx().T),
    )


GELU_K = math.sqrt(2.0 / math.pi)
GELU_A = GELU_K * 0.044715


def cells_kernel(
    grid_modes, kron_ref, bias_ref, scale_ref, ey_ref, ez_ref, field_ref, cotan_ref,
    out_ref, cotan_pre_ref, sums_ref,
    along_z, spectral, local, field_rows, cotan_rows, grad, bias_sum,
):
    step = pl.program_id(0)
    grad_scale = 1.0 / math.sqrt(N_GRP * NX * NY * NZ)

    @pl.when(step == 0)
    def _():
        grad[...] = jnp.zeros_like(grad)
        bias_sum[...] = jnp.zeros_like(bias_sum)
        for quarter in range(4):
            rows = grid_modes[quarter * 16 : quarter * 16 + 16].astype(F32).reshape(128, 128)
            turn = rows.T
            per_c = jnp.concatenate(
                [
                    jnp.concatenate(
                        [turn[0:64, jy * 32 : jy * 32 + 32], turn[64:128, jy * 32 : jy * 32 + 32]],
                        1,
                    )
                    for jy in range(4)
                ],
                0,
            ).astype(BF16)
            got = jnp.dot(per_c, ez_ref[...], preferred_element_type=F32)
            for jy in range(4):
                for cs in range(2):
                    for x in range(2):
                        start = x * 2048 + cs * 16 + quarter * 4 + jy
                        lane = cs * 256 + x * 128
                        along_z[pl.ds(start, 64, stride=32), :] = got[
                            jy * 64 : jy * 64 + 64, lane : lane + 128
                        ]

        def pair(index, carry):
            rows = jnp.concatenate(
                [
                    along_z[pl.ds(pl.multiple_of(x * 2048 + 64 * index, 64), 64), :]
                    for x in range(2)
                ],
                1,
            ).astype(BF16)
            got = jnp.dot(ey_ref[...], rows, preferred_element_type=F32)
            spectral[2 * index] = got[:128] + bias_ref[2 * index]
            spectral[2 * index + 1] = got[128:] + bias_ref[2 * index + 1]
            return carry

        lax.fori_loop(0, 32, pair, 0)

    halves = []
    for x in range(2):
        halves.append(field_ref[:, x].astype(F32))
    for half in range(2):
        rows = jnp.concatenate(
            [part[:, 8 * half : 8 * half + 8].reshape(512, 128) for part in halves], 1
        ).astype(BF16)
        field_rows[:, half * 256 : half * 256 + 256] = rows
        got = jnp.dot(kron_ref[...], rows, preferred_element_type=F32)
        local[:, 8 * half : 8 * half + 8, :] = got.reshape(64, 8, 256)

    def few(index, carry):
        at = pl.ds(4 * index, 4)
        y_at = pl.ds(pl.multiple_of(16 * step, 16), 16)
        sums = jnp.zeros((4, 8, 128), F32)
        for x in range(2):
            lanes = slice(x * 128, x * 128 + 128)
            pre = local[at, :, lanes] + spectral[at, y_at, lanes]
            square = pre * pre
            half_tanh = 0.5 + 0.5 * jnp.tanh(pre * (GELU_K + GELU_A * square))
            out_ref[at, x] = (pre * half_tanh).astype(BF16)
            slope = half_tanh * (
                1.0
                + (1.0 - half_tanh) * (pre * (2.0 * GELU_K + 6.0 * GELU_A * square))
            )
            cotan = (slope * (cotan_ref[at, x].astype(F32) * grad_scale)).astype(BF16)
            cotan_pre_ref[at, x] = cotan
            wide = cotan.astype(F32)
            for half in range(2):
                rows = wide[:, 8 * half : 8 * half + 8]
                sums = sums + rows
                cotan_rows[
                    pl.ds(pl.multiple_of(32 * index, 32), 32),
                    half * 256 + x * 128 : half * 256 + x * 128 + 128,
                ] = rows.reshape(32, 128).astype(BF16)
        bias_sum[at] += sums
        return carry

    lax.fori_loop(0, 16, few, 0)
    grad[...] += nt_dot(cotan_rows[...], field_rows[...])

    @pl.when(step == pl.num_programs(0) - 1)
    def _():
        same = (
            lax.broadcasted_iota(jnp.int32, (512, 512), 0) % 8
            == lax.broadcasted_iota(jnp.int32, (512, 512), 1) % 8
        )
        per_c = jnp.sum(jnp.where(same, grad[...], 0.0).reshape(64, 8, 512), axis=1)
        pick = (
            lax.broadcasted_iota(jnp.int32, (512, 64), 0) // 8
            == lax.broadcasted_iota(jnp.int32, (512, 64), 1)
        ).astype(F32)
        d_local = jnp.dot(
            per_c, pick, preferred_element_type=F32, precision=lax.Precision.HIGHEST
        )
        d_local = d_local * scale_ref[0:1, 0:64]
        lanes = jnp.sum(bias_sum[...], axis=1)
        d_bias = nt_dot(jnp.ones((8, 128), F32), lanes, lax.Precision.HIGHEST)
        side = jnp.concatenate([d_bias, jnp.zeros((56, 64), F32)], 0)
        sums_ref[...] = jnp.concatenate([d_local, side], 1).reshape(8, 8, 128)


def cells_call(grid_modes, kron, bias, scale_rows, field, cotangent):
    vmem = pl.BlockSpec(memory_space=pltpu.VMEM)
    block = pl.BlockSpec((64, 2, 16, 128), lambda step: (0, 0, step, 0))
    cells = 64 * 2 * 128 * 128
    return pl.pallas_call(
        cells_kernel,
        grid=(8,),
        out_shape=(
            jax.ShapeDtypeStruct((64, 2, 128, 128), BF16),
            jax.ShapeDtypeStruct((64, 2, 128, 128), BF16),
            jax.ShapeDtypeStruct((8, 8, 128), F32),
        ),
        in_specs=[
            vmem, vmem, pl.BlockSpec(memory_space=pltpu.SMEM), vmem, vmem, vmem, block, block,
        ],
        out_specs=(block, block, pl.BlockSpec((8, 8, 128), lambda step: (0, 0, 0))),
        scratch_shapes=[
            pltpu.VMEM((4096, 128), F32),
            pltpu.VMEM((64, 128, 256), F32),
            pltpu.VMEM((64, 16, 256), F32),
            pltpu.VMEM((512, 512), BF16),
            pltpu.VMEM((512, 512), BF16),
            pltpu.VMEM((512, 512), F32),
            pltpu.VMEM((64, 8, 128), F32),
        ],
        compiler_params=pltpu.CompilerParams(vmem_limit_bytes=40 * MIB),
        cost_estimate=pl.CostEstimate(
            flops=cells * 64 * 8 * 4, bytes_accessed=cells * 8, transcendentals=cells
        ),
    )(grid_modes, kron, bias, scale_rows, table_ey(), table_ez(), field, cotangent)


def gradient_kernel(
    cotan, sums_ref, ty_ref, zt_ref, tx_ref,
    modes_out, sums_out,
    held, along_y, slab_modes, pencil, modes, gathered, own_sums, first, second, second_own, third,
    field_sems, send_sems, recv_sems,
):
    me = lax.axis_index("slab")
    grp = lax.axis_index("grp")
    low = lax.rem(me, N_LOW)
    z = me // N_LOW
    barrier = pltpu.get_barrier_semaphore()
    fetch_field(cotan, held, field_sems)
    greet(barrier, me, grp)
    for g_step in range(1, N_GRP):

        def tell(step, carry):
            pl.semaphore_signal(
                barrier,
                inc=1,
                device_id={
                    "grp": lax.rem(grp + g_step, N_GRP),
                    "slab": z * N_LOW + lax.rem(low + step, N_LOW),
                },
                device_id_type=MESH,
            )
            return carry

        lax.fori_loop(1, N_LOW, tell, 0)
    analyse(cotan, held, field_sems, ty_ref, zt_ref, along_y, slab_modes)
    own_sums[...] = sums_ref[...]
    pl.semaphore_wait(barrier, N_SLAB - 1 + N_GRP - 1 + (N_GRP - 1) * (N_LOW - 1))

    def scatter(step, carry):
        other = lax.rem(z + step, N_Z)
        pltpu.make_async_remote_copy(
            src_ref=own_sums.at[other],
            dst_ref=first.at[z],
            send_sem=send_sems.at[1],
            recv_sem=recv_sems.at[1],
            device_id={"slab": other * N_LOW + low},
            device_id_type=MESH,
        ).start()
        return carry

    lax.fori_loop(1, N_Z, scatter, 0)
    first[pl.ds(z, 1)] = own_sums[pl.ds(z, 1)]
    send_all(slab_modes, pencil, send_sems.at[0], recv_sems.at[0], me)
    wait_blocks(own_sums, first, send_sems.at[1], recv_sems.at[1], N_Z - 1, me)
    part = jnp.sum(first[...], axis=0, keepdims=True)
    mine = grp * N_LOW + low
    second[pl.ds(mine, 1)] = part
    second_own[...] = part
    for g_step in range(N_GRP):

        def spread(step, carry):
            pltpu.make_async_remote_copy(
                src_ref=second_own.at[0],
                dst_ref=second.at[mine],
                send_sem=send_sems.at[2],
                recv_sem=recv_sems.at[2],
                device_id={
                    "grp": lax.rem(grp + g_step, N_GRP),
                    "slab": z * N_LOW + lax.rem(low + step, N_LOW),
                },
                device_id_type=MESH,
            ).start()
            return carry

        lax.fori_loop(1 if g_step == 0 else 0, N_LOW, spread, 0)
    wait_blocks(slab_modes, pencil, send_sems.at[0], recv_sems.at[0], N_SLAB - 1, me)
    modes[...] = x_modes(pencil, tx_ref).astype(BF16).reshape(4, 16, 128)
    send_grp(modes, gathered, send_sems.at[3], recv_sems.at[3], grp, True)
    gathered[pl.ds(grp, 1)] = modes[pl.ds(grp, 1)]
    wait_blocks(second, second, send_sems.at[2], recv_sems.at[2], N_GRP * N_LOW - 1, me)
    third[pl.ds(z, 1)] = jnp.sum(second[...], axis=0, keepdims=True)

    def collect(step, carry):
        other = lax.rem(z + step, N_Z)
        pltpu.make_async_remote_copy(
            src_ref=third.at[z],
            dst_ref=third.at[z],
            send_sem=send_sems.at[4],
            recv_sem=recv_sems.at[4],
            device_id={"slab": other * N_LOW + low},
            device_id_type=MESH,
        ).start()
        return carry

    lax.fori_loop(1, N_Z, collect, 0)
    wait_blocks(modes, gathered, send_sems.at[3], recv_sems.at[3], N_GRP - 1, me)
    modes_out[...] = gathered[...]
    wait_blocks(third, third, send_sems.at[4], recv_sems.at[4], N_Z - 1, me)
    sums_out[...] = third[...]


def gradient_call(cotan, sums):
    vmem = pl.BlockSpec(memory_space=pltpu.VMEM)
    return pl.pallas_call(
        gradient_kernel,
        out_shape=(
            jax.ShapeDtypeStruct((4, 16, 128), BF16),
            jax.ShapeDtypeStruct((8, 8, 128), F32),
        ),
        in_specs=[pl.BlockSpec(memory_space=pl.ANY)] + [vmem] * 4,
        out_specs=(vmem,) * 2,
        scratch_shapes=[
            pltpu.VMEM((64, 2, 128, 128), BF16),
            pltpu.VMEM((4096, 128), F32),
            pltpu.VMEM((64, 8, 128), BF16),
            pltpu.VMEM((64, 8, 128), BF16),
            pltpu.VMEM((4, 16, 128), BF16),
            pltpu.VMEM((4, 16, 128), BF16),
            pltpu.VMEM((8, 8, 128), F32),
            pltpu.VMEM((8, 8, 128), F32),
            pltpu.VMEM((32, 8, 128), F32),
            pltpu.VMEM((1, 8, 128), F32),
            pltpu.VMEM((8, 8, 128), F32),
            pltpu.SemaphoreType.DMA((8,)),
            pltpu.SemaphoreType.DMA((5,)),
            pltpu.SemaphoreType.DMA((5,)),
        ],
        compiler_params=pltpu.CompilerParams(
            collective_id=1, has_side_effects=True, vmem_limit_bytes=32 * MIB
        ),
    )(cotan, sums, table_ty(), table_zt(True), table_tx())


def weights_kernel(modes_g, own_modes, scales, sums_ref, d_spec, d_local, d_bias):
    own = own_modes[...]
    shifted = jnp.concatenate([own * scales[s, 0:1, :] for s in range(N_GRP)], 0)
    columns = shifted.T
    rows = modes_g[...].astype(F32).reshape(64, 128)
    other = turned(rows, 1.0, -1.0)
    for k in range(16):
        total = jnp.zeros((64, 128), F32)
        for s in range(N_GRP):
            at = s * 16 + k
            total = total + columns[0:64, at : at + 1] * rows[at : at + 1]
            total = total + columns[64:128, at : at + 1] * other[at : at + 1]
        d_spec[k] = total
    sums = sums_ref[...].reshape(64, 128)
    d_local[...] = sums[:, 0:64]
    d_bias[...] = sums[0:1, 64:128]


def weights_call(modes_g, own_modes, scales, sums):
    vmem = pl.BlockSpec(memory_space=pltpu.VMEM)
    return pl.pallas_call(
        weights_kernel,
        out_shape=(
            jax.ShapeDtypeStruct((16, 64, 128), F32),
            jax.ShapeDtypeStruct((64, 64), F32),
            jax.ShapeDtypeStruct((1, 64), F32),
        ),
        in_specs=[vmem] * 4,
        out_specs=(vmem,) * 3,
    )(modes_g, own_modes, scales, sums)


def shards(base_field, cotangent, w_spec, w_local, bias, direction, shift):
    number = lax.axis_index("grp") + 1
    gray_code = jnp.bitwise_xor(number, number >> 1)
    picked = [
        jnp.where(gray_code >> bit_pos & 1 == 1, direction[:, bit_pos], 0)
        for bit_pos in range(BITS)
    ]
    mixed_bits = reduce(jnp.bitwise_xor, picked)
    sobol_point = jnp.bitwise_xor(mixed_bits, shift[0]).astype(F32) * 2.0 ** (-30)
    scale = 0.5 + sobol_point
    scale_rows = jnp.broadcast_to(jnp.concatenate([scale, scale])[None, :], (8, 128))
    grid_modes, own_modes, scales, kron = spectral_call(
        base_field, w_spec.reshape(16, 64, 128), w_local, scale_rows
    )
    output, cotan_pre, sums = cells_call(
        grid_modes, kron, bias, scale_rows, base_field, cotangent[0]
    )
    modes_g, total = gradient_call(cotan_pre, sums)
    d_spec, d_local, d_bias = weights_call(modes_g, own_modes, scales, total)
    return (output[None], d_spec.reshape(4, 4, 64, 128), d_local, d_bias.reshape(64))


def solution(mesh):
    return jax.shard_map(
        shards,
        mesh=mesh,
        in_specs=(
            P(None, "slab", None, None),
            P("grp", None, "slab", None, None),
            P("grp", "slab", None, None),
            P(),
            P(),
            P(),
            P("grp", None),
        ),
        out_specs=(P("grp", None, "slab", None, None), P("grp", "slab", None, None), P(), P()),
        check_vma=False,
    )
```

```python
from functools import reduce
import math

import jax
import jax.numpy as jnp
import ml_dtypes
import numpy as np
from jax import lax
from jax.experimental import pallas as pl
from jax.experimental.pallas import tpu as pltpu
from jax.sharding import PartitionSpec as P

CH = 64
NX = 128
NY = 128
NZ = 128
MODES = 16
BITS = 30
N_GRP = 4
N_SLAB = 64
N_LOW = 8
N_Z = 8
MESH = pl.DeviceIdType.MESH
F32 = jnp.float32
BF16 = jnp.bfloat16
MIB = 1024 * 1024


def waves(length, half):
    ids = np.arange(MODES)
    if not half:
        ids = np.where(ids < MODES // 2, ids, length - MODES + ids)
    angles = 2.0 * math.pi / length * (ids[:, None] * np.arange(length)[None, :] % length)
    return np.cos(angles), np.sin(angles)


def as_bf16(table):
    return np.asarray(table, np.float32).astype(ml_dtypes.bfloat16)


def table_ty():
    cos_y, sin_y = waves(NY, False)
    out = np.zeros((2, 2, MODES, 2, NY))
    for c2 in range(2):
        out[0, c2, :, c2] = cos_y
        out[1, c2, :, c2] = sin_y
    return as_bf16(out.reshape(64, 256))


def weights_z(backward):
    return np.where(np.arange(MODES) == 0, 1.0, 2.0 if backward else 1.0)[:, None]


def table_zt(backward):
    cos_z, sin_z = waves(NZ, True)
    weight = weights_z(backward)
    cos_z = (weight * cos_z).reshape(4, 4, NZ)
    sin_z = (weight * sin_z).reshape(4, 4, NZ)
    out = np.zeros((2, 4, 2, 4, 2, 2, NZ))
    for x in range(2):
        out[0, :, x, :, 0, x] = cos_z
        out[0, :, x, :, 1, x] = -sin_z
        out[1, :, x, :, 0, x] = -sin_z
        out[1, :, x, :, 1, x] = -cos_z
    return as_bf16(out.reshape(64, 512))


def table_tx():
    cos_x, sin_x = waves(NX, False)
    out = np.zeros((2, MODES, 4, NX, 4))
    for m in range(4):
        out[0, :, m, :, m] = cos_x
        out[1, :, m, :, m] = sin_x
    return as_bf16(out.reshape(128, 512))


def table_ey():
    cos_y, sin_y = waves(NY, False)
    out = np.zeros((2, NY, 2, 2, MODES))
    for c2 in range(2):
        out[c2, :, c2, 0] = cos_y.T
        out[c2, :, c2, 1] = -sin_y.T
    return as_bf16(out.reshape(256, 64))


def table_ez():
    cos_z, sin_z = waves(NZ, True)
    weight = weights_z(True) / math.sqrt(MODES**3)
    cos_z = (weight * cos_z).reshape(4, 4, NZ)
    sin_z = (weight * sin_z).reshape(4, 4, NZ)
    out = np.zeros((2, 4, 2, 4, 2, 2, NZ))
    for x in range(2):
        out[0, :, x, :, 0, x] = cos_z
        out[1, :, x, :, 0, x] = -sin_z
        out[0, :, x, :, 1, x] = sin_z
        out[1, :, x, :, 1, x] = cos_z
    return as_bf16(out.reshape(64, 512))


def lane_sign(rows, first, second):
    lane = lax.broadcasted_iota(jnp.int32, (rows, 128), 1)
    return jnp.where(lane < 64, first, second).astype(F32)


def turned(rows, first, second):
    return pltpu.roll(rows, 64, 1) * lane_sign(rows.shape[0], first, second)


def nt_dot(left, right, precision=None):
    return lax.dot_general(
        left, right, (((1,), (1,)), ((), ())), preferred_element_type=F32, precision=precision
    )


def fetch_field(field, held, sems):
    for part in range(8):
        rows = pl.ds(8 * part, 8)
        pltpu.make_async_copy(field.at[rows], held.at[rows], sems.at[part]).start()


def wait_field(field, held, sems, part):
    rows = pl.ds(8 * part, 8)
    pltpu.make_async_copy(field.at[rows], held.at[rows], sems.at[part]).wait()


def store_along_y(along_y, got, first):
    for cs in range(2):
        for c2 in range(2):
            at = cs * 32 + c2 * 16
            for x in range(2):
                start = (2 * cs + x) * 1024 + first + c2
                along_y[pl.ds(start, 16, stride=64), :] = got[
                    at : at + 16, x * 128 : x * 128 + 128
                ]


def along_z_modes(along_y, zt_ref, slab_modes):
    for quarter in range(4):
        rows = jnp.concatenate(
            [
                along_y[part * 1024 + quarter * 256 : part * 1024 + quarter * 256 + 256, :]
                for part in range(4)
            ],
            1,
        ).astype(BF16)
        got = nt_dot(zt_ref[...], rows)
        for jy in range(4):
            real = got[0:32, jy * 64 : jy * 64 + 64]
            imag = got[32:64, jy * 64 : jy * 64 + 64]
            owner = (quarter * 4 + jy) * 4
            slab_modes[owner : owner + 4] = (
                jnp.concatenate([real, imag], 1).reshape(4, 8, 128).astype(BF16)
            )


def greet(barrier, me, grp):
    def tell(step, carry):
        pl.semaphore_signal(
            barrier, inc=1, device_id={"slab": lax.rem(me + step, N_SLAB)}, device_id_type=MESH
        )
        return carry

    lax.fori_loop(1, N_SLAB, tell, 0)
    for step in range(1, N_GRP):
        pl.semaphore_signal(
            barrier, inc=1, device_id={"grp": lax.rem(grp + step, N_GRP)}, device_id_type=MESH
        )


def send_all(source, target, send_sem, recv_sem, me):
    low = lax.rem(me, N_LOW)
    z = me // N_LOW
    for dz in (4, 3, 5, 2, 6, 1, 7, 0):

        def go(step, carry):
            other = lax.rem(z + dz, N_Z) * N_LOW + lax.rem(low + step, N_LOW)
            pltpu.make_async_remote_copy(
                src_ref=source.at[other],
                dst_ref=target.at[me],
                send_sem=send_sem,
                recv_sem=recv_sem,
                device_id={"slab": other},
                device_id_type=MESH,
            ).start()
            return carry

        lax.fori_loop(1 if dz == 0 else 0, N_LOW, go, 0)
    target[pl.ds(me, 1)] = source[pl.ds(me, 1)]


def wait_blocks(source, target, send_sem, recv_sem, count, me):
    pltpu.make_async_remote_copy(
        src_ref=source.at[pl.ds(0, count)],
        dst_ref=target.at[pl.ds(0, count)],
        send_sem=send_sem,
        recv_sem=recv_sem,
        device_id={"slab": me},
        device_id_type=MESH,
    ).wait()


def send_grp(source, target, send_sem, recv_sem, grp, by_target):
    for step in range(1, N_GRP):
        other = lax.rem(grp + step, N_GRP)
        pltpu.make_async_remote_copy(
            src_ref=source.at[other] if by_target else source.at[grp],
            dst_ref=target.at[grp],
            send_sem=send_sem,
            recv_sem=recv_sem,
            device_id={"grp": other},
            device_id_type=MESH,
        ).start()


def x_modes(pencil, tx_ref):
    rows = pencil[...].astype(F32).reshape(512, 128).astype(BF16)
    both = jnp.dot(tx_ref[...], rows, preferred_element_type=F32)
    return both[:64] + turned(both[64:], 1.0, -1.0)


GELU_K = math.sqrt(2.0 / math.pi)
GELU_A = GELU_K * 0.044715
GRAD_SCALE = 1.0 / math.sqrt(N_GRP * NX * NY * NZ)


def local_step(part, held, kron, field_rows, local):
    y_at = pl.multiple_of(16 * part, 16)
    halves = [held[:, x, pl.ds(y_at, 16), :].astype(F32) for x in range(2)]
    for half in range(2):
        rows = jnp.concatenate(
            [block[:, 8 * half : 8 * half + 8].reshape(512, 128) for block in halves], 1
        ).astype(BF16)
        field_rows[part, :, half * 256 : half * 256 + 256] = rows
        got = jnp.dot(kron[...], rows, preferred_element_type=F32)
        local[:, pl.ds(pl.multiple_of(y_at + 8 * half, 8), 8), :] = got.reshape(64, 8, 256)


def fill_kron(wl_ref, scale_row, kron):
    local = (wl_ref[...].astype(F32) * scale_row[0:1, 0:64]).astype(BF16)
    pick = (
        lax.broadcasted_iota(jnp.int32, (64, 512), 0)
        == lax.broadcasted_iota(jnp.int32, (64, 512), 1) // 8
    )
    wide = jnp.dot(local, pick.astype(F32).astype(BF16), preferred_element_type=F32).astype(BF16)
    same = (
        lax.broadcasted_iota(jnp.int32, (64, 512), 0) % 8
        == lax.broadcasted_iota(jnp.int32, (64, 512), 1) % 8
    )
    row_ids = lax.broadcasted_iota(jnp.int32, (64, 64), 0) // 8
    col_ids = lax.broadcasted_iota(jnp.int32, (64, 64), 1)
    for octet in range(8):
        rows_of = (row_ids + 8 * octet == col_ids).astype(F32).astype(BF16)
        tall = jnp.dot(rows_of, wide, preferred_element_type=F32)
        kron[octet * 64 : octet * 64 + 64, :] = jnp.where(same, tall, 0.0).astype(BF16)


def fill_along_z(landed, ez_ref, along_z):
    for quarter in range(4):
        rows = landed[quarter * 16 : quarter * 16 + 16].astype(F32).reshape(128, 128)
        turn = rows.T
        per_c = jnp.concatenate(
            [
                jnp.concatenate(
                    [turn[0:64, jy * 32 : jy * 32 + 32], turn[64:128, jy * 32 : jy * 32 + 32]], 1
                )
                for jy in range(4)
            ],
            0,
        ).astype(BF16)
        got = jnp.dot(per_c, ez_ref[...], preferred_element_type=F32)
        for jy in range(4):
            for cs in range(2):
                for x in range(2):
                    start = x * 2048 + cs * 16 + quarter * 4 + jy
                    lane = cs * 256 + x * 128
                    along_z[pl.ds(start, 64, stride=32), :] = got[
                        jy * 64 : jy * 64 + 64, lane : lane + 128
                    ]


def cells_step(
    index, along_z, local, bias_ref, cotan_in, ey_ref, ty_ref, out_held, cotan_rows, bias_sum, along_y
):
    rows = jnp.concatenate(
        [along_z[pl.ds(pl.multiple_of(x * 2048 + 64 * index, 64), 64), :] for x in range(2)], 1
    ).astype(BF16)
    got = jnp.dot(ey_ref[...], rows, preferred_element_type=F32)
    cells = []
    for c2 in range(2):
        channel = 2 * index + c2
        both = []
        for x in range(2):
            lanes = slice(x * 128, x * 128 + 128)
            pre = got[c2 * 128 : c2 * 128 + 128, lanes] + (
                local[channel, :, lanes] + bias_ref[channel]
            )
            square = pre * pre
            half_tanh = 0.5 + 0.5 * jnp.tanh(pre * (GELU_K + GELU_A * square))
            out_held[channel, x] = (pre * half_tanh).astype(BF16)
            slope = half_tanh + half_tanh * (1.0 - half_tanh) * (
                pre * (2.0 * GELU_K + 6.0 * GELU_A * square)
            )
            both.append(slope * (cotan_in[channel, x].astype(F32) * GRAD_SCALE))
        total = both[0] + both[1]
        bias_sum[channel] = jnp.sum(total.reshape(16, 8, 128), axis=0)
        cells.append(both)
    for y8 in range(16):
        for x in range(2):
            block = jnp.concatenate(
                [cells[c2][x][8 * y8 : 8 * y8 + 8] for c2 in range(2)], 0
            ).astype(BF16)
            lane = (y8 % 2) * 256 + x * 128
            cotan_rows[
                y8 // 2, pl.ds(pl.multiple_of(16 * index, 16), 16), lane : lane + 128
            ] = block
    wide = jnp.concatenate([jnp.concatenate(both, 1) for both in cells], 0).astype(BF16)
    store_along_y(
        along_y, jnp.dot(ty_ref[...], wide, preferred_element_type=F32), 2 * index
    )


def sums_of(grad, bias_sum, scale_row):
    same = (
        lax.broadcasted_iota(jnp.int32, (512, 512), 0) % 8
        == lax.broadcasted_iota(jnp.int32, (512, 512), 1) % 8
    )
    per_c = jnp.sum(jnp.where(same, grad, 0.0).reshape(64, 8, 512), axis=1)
    pick = (
        lax.broadcasted_iota(jnp.int32, (512, 64), 0) // 8
        == lax.broadcasted_iota(jnp.int32, (512, 64), 1)
    ).astype(F32)
    d_local = jnp.dot(per_c, pick, preferred_element_type=F32, precision=lax.Precision.HIGHEST)
    d_local = d_local * scale_row[0:1, 0:64]
    lanes = jnp.sum(bias_sum[...], axis=1)
    d_bias = nt_dot(jnp.ones((8, 128), F32), lanes, lax.Precision.HIGHEST)
    side = jnp.concatenate([d_bias, jnp.zeros((56, 64), F32)], 0)
    return jnp.concatenate([d_local, side], 1).reshape(8, 8, 128)


def layer_kernel(
    field, cotan, w_hbm, wl_hbm, scale_hbm, bias_ref,
    ty_hbm, ztf_hbm, ztb_hbm, tx_hbm, txb_hbm, ey_hbm, ez_hbm,
    out_hbm, modes_out, own_modes, scales, sums_out,
    ty_ref, ztf_ref, ztb_ref, tx_ref, txb_ref, ey_ref, ez_ref, w_ref, wl_ref, scale_ref,
    held, cotan_in, out_held, field_rows, cotan_rows, local, along_y, along_z, kron, w_two,
    slab_modes, pencil, mixed, gathered, back, landed, slab_g, pencil_g, mixed_g, gathered_g,
    all_modes, scale_own, scale_all, bias_sum, own_sums, first, second, second_own, third,
    field_sems, cotan_sems, table_sems, out_sems, send_sems, recv_sems,
):
    me = lax.axis_index("slab")
    grp = lax.axis_index("grp")
    low = lax.rem(me, N_LOW)
    z = me // N_LOW
    barrier = pltpu.get_barrier_semaphore()
    small = [
        (ty_hbm, ty_ref), (ztf_hbm, ztf_ref), (scale_hbm, scale_ref), (wl_hbm, wl_ref),
        (w_hbm, w_ref), (tx_hbm, tx_ref), (txb_hbm, txb_ref), (ey_hbm, ey_ref),
        (ez_hbm, ez_ref), (ztb_hbm, ztb_ref),
    ]
    copies = [
        pltpu.make_async_copy(source, target, table_sems.at[at])
        for at, (source, target) in enumerate(small)
    ]
    for copy in copies[:2]:
        copy.start()
    fetch_field(field, held, field_sems)
    for copy in copies[2:]:
        copy.start()
    fetch_field(cotan, cotan_in, cotan_sems)
    greet(barrier, me, grp)
    for g_step in range(1, N_GRP):

        def tell(step, carry):
            pl.semaphore_signal(
                barrier,
                inc=1,
                device_id={
                    "grp": lax.rem(grp + g_step, N_GRP),
                    "slab": lax.rem(z + step, N_Z) * N_LOW + low,
                },
                device_id_type=MESH,
            )
            return carry

        lax.fori_loop(1, N_Z, tell, 0)

    copies[0].wait()

    def channels(part, carry):
        wait_field(field, held, field_sems, part)
        for pair in range(4):
            first_c = 8 * part + 2 * pair
            rows = jnp.concatenate(
                [
                    jnp.concatenate([held[first_c + c2, 0], held[first_c + c2, 1]], 1)
                    for c2 in range(2)
                ],
                0,
            )
            store_along_y(
                along_y, jnp.dot(ty_ref[...], rows, preferred_element_type=F32), first_c
            )
        return carry

    lax.fori_loop(0, 8, channels, 0)
    copies[1].wait()
    along_z_modes(along_y, ztf_ref, slab_modes)
    copies[2].wait()
    scale_own[grp] = scale_ref[...]
    scale_all[grp] = scale_ref[...]
    pl.semaphore_wait(barrier, N_SLAB - 1 + N_GRP - 1 + (N_GRP - 1) * (N_Z - 1))
    send_all(slab_modes, pencil, send_sems.at[0], recv_sems.at[0], me)
    send_grp(scale_own, scale_all, send_sems.at[1], recv_sems.at[1], grp, False)

    copies[3].wait()
    copies[4].wait()
    for k in range(16):
        block = w_ref[k].astype(F32)
        w_two[k * 128 : k * 128 + 64, :] = w_ref[k]
        w_two[k * 128 + 64 : k * 128 + 128, :] = turned(block, -1.0, 1.0).astype(BF16)
    fill_kron(wl_ref, scale_ref[...], kron)

    def local_some(part, carry):
        local_step(part, held, kron, field_rows, local)
        return carry

    lax.fori_loop(0, 3, local_some, 0)
    pltpu.make_async_remote_copy(
        src_ref=scale_own.at[pl.ds(0, N_GRP - 1)],
        dst_ref=scale_all.at[pl.ds(0, N_GRP - 1)],
        send_sem=send_sems.at[1],
        recv_sem=recv_sems.at[1],
        device_id={"slab": me},
        device_id_type=MESH,
    ).wait()
    scales[...] = scale_all[...]
    copies[5].wait()
    copies[6].wait()
    wait_blocks(slab_modes, pencil, send_sems.at[0], recv_sems.at[0], N_SLAB - 1, me)

    all_modes[...] = x_modes(pencil, tx_ref) * (1.0 / math.sqrt(NX * NY * NZ))
    own = all_modes[pl.ds(pl.multiple_of(16 * grp, 16), 16), :]
    own_modes[...] = own
    shifted = jnp.concatenate([own * scale_all[s, 0:1, :] for s in range(N_GRP)], 0)
    row_mode = lax.broadcasted_iota(jnp.int32, (64, 128), 0) % 16
    spread = jnp.concatenate(
        [jnp.where(row_mode == k, shifted, 0.0).astype(BF16) for k in range(16)], 1
    )
    mixed[...] = (
        jnp.dot(spread, w_two[...], preferred_element_type=F32).astype(BF16).reshape(4, 16, 128)
    )
    send_grp(mixed, gathered, send_sems.at[2], recv_sems.at[2], grp, True)
    gathered[pl.ds(grp, 1)] = mixed[pl.ds(grp, 1)]
    lax.fori_loop(3, 5, local_some, 0)
    wait_blocks(mixed, gathered, send_sems.at[2], recv_sems.at[2], N_GRP - 1, me)
    full = gathered[...].reshape(64, 128)
    both = jnp.concatenate([full, turned(full.astype(F32), -1.0, 1.0).astype(BF16)], 0)
    back[...] = (
        jnp.dot(txb_ref[...], both, preferred_element_type=F32).reshape(64, 8, 128).astype(BF16)
    )
    send_all(back, landed, send_sems.at[3], recv_sems.at[3], me)
    lax.fori_loop(5, 8, local_some, 0)
    for copy in copies[7:]:
        copy.wait()
    for part in range(8):
        wait_field(cotan, cotan_in, cotan_sems, part)
    wait_blocks(back, landed, send_sems.at[3], recv_sems.at[3], N_SLAB - 1, me)

    fill_along_z(landed, ez_ref, along_z)

    def some_cells(part, carry):
        for pair in range(2):
            cells_step(
                2 * part + pair, along_z, local, bias_ref, cotan_in, ey_ref, ty_ref, out_held,
                cotan_rows, bias_sum, along_y,
            )
        return carry

    def cells_part(part, carry):
        lax.fori_loop(2 * part, 2 * part + 2, some_cells, 0)
        rows = pl.ds(8 * part, 8)
        pltpu.make_async_copy(out_held.at[rows], out_hbm.at[rows], out_sems.at[part]).start()
        return carry

    lax.fori_loop(0, 8, cells_part, 0)

    grad = jnp.zeros((512, 512), F32)
    for part in range(8):
        grad = grad + nt_dot(cotan_rows[part], field_rows[part])
    own_sums[...] = sums_of(grad, bias_sum, scale_ref[...])

    def scatter(step, carry):
        other = lax.rem(low + step, N_LOW)
        pltpu.make_async_remote_copy(
            src_ref=own_sums.at[other],
            dst_ref=first.at[low],
            send_sem=send_sems.at[4],
            recv_sem=recv_sems.at[4],
            device_id={"slab": z * N_LOW + other},
            device_id_type=MESH,
        ).start()
        return carry

    lax.fori_loop(1, N_LOW, scatter, 0)
    first[pl.ds(low, 1)] = own_sums[pl.ds(low, 1)]
    along_z_modes(along_y, ztb_ref, slab_g)
    send_all(slab_g, pencil_g, send_sems.at[5], recv_sems.at[5], me)
    wait_blocks(own_sums, first, send_sems.at[4], recv_sems.at[4], N_LOW - 1, me)
    part_sum = jnp.sum(first[...], axis=0, keepdims=True)
    mine = grp * N_Z + z
    second[pl.ds(mine, 1)] = part_sum
    second_own[...] = part_sum
    for g_step in (2, 1, 3, 0):

        def spread_sum(step, carry):
            pltpu.make_async_remote_copy(
                src_ref=second_own.at[0],
                dst_ref=second.at[mine],
                send_sem=send_sems.at[6],
                recv_sem=recv_sems.at[6],
                device_id={
                    "grp": lax.rem(grp + g_step, N_GRP),
                    "slab": lax.rem(z + step, N_Z) * N_LOW + low,
                },
                device_id_type=MESH,
            ).start()
            return carry

        lax.fori_loop(1 if g_step == 0 else 0, N_Z, spread_sum, 0)
    wait_blocks(slab_g, pencil_g, send_sems.at[5], recv_sems.at[5], N_SLAB - 1, me)
    mixed_g[...] = x_modes(pencil_g, tx_ref).astype(BF16).reshape(4, 16, 128)
    send_grp(mixed_g, gathered_g, send_sems.at[7], recv_sems.at[7], grp, True)
    gathered_g[pl.ds(grp, 1)] = mixed_g[pl.ds(grp, 1)]
    wait_blocks(second, second, send_sems.at[6], recv_sems.at[6], N_GRP * N_Z - 1, me)
    third[pl.ds(low, 1)] = jnp.sum(second[...], axis=0, keepdims=True)

    def collect(step, carry):
        pltpu.make_async_remote_copy(
            src_ref=third.at[low],
            dst_ref=third.at[low],
            send_sem=send_sems.at[8],
            recv_sem=recv_sems.at[8],
            device_id={"slab": z * N_LOW + lax.rem(low + step, N_LOW)},
            device_id_type=MESH,
        ).start()
        return carry

    lax.fori_loop(1, N_LOW, collect, 0)
    wait_blocks(mixed_g, gathered_g, send_sems.at[7], recv_sems.at[7], N_GRP - 1, me)
    modes_out[...] = gathered_g[...]
    for part in range(8):
        rows = pl.ds(8 * part, 8)
        pltpu.make_async_copy(out_held.at[rows], out_hbm.at[rows], out_sems.at[part]).wait()
    wait_blocks(third, third, send_sems.at[8], recv_sems.at[8], N_LOW - 1, me)
    sums_out[...] = third[...]


def layer_call(field, cotangent, w_spec, w_local, scale_rows, bias):
    vmem = pl.BlockSpec(memory_space=pltpu.VMEM)
    hbm = pl.BlockSpec(memory_space=pl.ANY)
    tables = (
        table_ty(), table_zt(False), table_zt(True), table_tx(),
        np.ascontiguousarray(table_tx().T), table_ey(), table_ez(),
    )
    cells = (64, 2, 128, 128)
    blocks = pltpu.VMEM((64, 8, 128), BF16)
    quads = pltpu.VMEM((4, 16, 128), BF16)
    return pl.pallas_call(
        layer_kernel,
        out_shape=(
            jax.ShapeDtypeStruct(cells, BF16),
            jax.ShapeDtypeStruct((4, 16, 128), BF16),
            jax.ShapeDtypeStruct((16, 128), F32),
            jax.ShapeDtypeStruct((4, 8, 128), F32),
            jax.ShapeDtypeStruct((8, 8, 128), F32),
        ),
        in_specs=[hbm] * 5 + [pl.BlockSpec(memory_space=pltpu.SMEM)] + [hbm] * 7,
        out_specs=(hbm,) + (vmem,) * 4,
        scratch_shapes=[pltpu.VMEM(table.shape, BF16) for table in tables]
        + [
            pltpu.VMEM((16, 64, 128), BF16),
            pltpu.VMEM((64, 64), BF16),
            pltpu.VMEM((8, 128), F32),
            pltpu.VMEM(cells, BF16),
            pltpu.VMEM(cells, BF16),
            pltpu.VMEM(cells, BF16),
            pltpu.VMEM((8, 512, 512), BF16),
            pltpu.VMEM((8, 512, 512), BF16),
            pltpu.VMEM((64, 128, 256), F32),
            pltpu.VMEM((4096, 128), F32),
            pltpu.VMEM((4096, 128), F32),
            pltpu.VMEM((512, 512), BF16),
            pltpu.VMEM((2048, 128), BF16),
            blocks, blocks, quads, quads, blocks, blocks, blocks, blocks, quads, quads,
            pltpu.VMEM((64, 128), F32),
            pltpu.VMEM((4, 8, 128), F32),
            pltpu.VMEM((4, 8, 128), F32),
            pltpu.VMEM((64, 8, 128), F32),
            pltpu.VMEM((8, 8, 128), F32),
            pltpu.VMEM((8, 8, 128), F32),
            pltpu.VMEM((32, 8, 128), F32),
            pltpu.VMEM((1, 8, 128), F32),
            pltpu.VMEM((8, 8, 128), F32),
            pltpu.SemaphoreType.DMA((8,)),
            pltpu.SemaphoreType.DMA((8,)),
            pltpu.SemaphoreType.DMA((10,)),
            pltpu.SemaphoreType.DMA((8,)),
            pltpu.SemaphoreType.DMA((9,)),
            pltpu.SemaphoreType.DMA((9,)),
        ],
        compiler_params=pltpu.CompilerParams(
            collective_id=0, has_side_effects=True, vmem_limit_bytes=58 * MIB
        ),
    )(field, cotangent, w_spec, w_local, scale_rows, bias, *tables)


def weights_kernel(
    out_hbm, modes_hbm, own_hbm, scales_hbm, sums_hbm,
    output, d_spec, d_local, d_bias,
    modes_g, own_modes, scales, sums_ref, sems,
):
    small = [
        (modes_hbm, modes_g), (own_hbm, own_modes), (scales_hbm, scales), (sums_hbm, sums_ref)
    ]
    copies = [
        pltpu.make_async_copy(source, target, sems.at[8 + at])
        for at, (source, target) in enumerate(small)
    ]
    for copy in copies:
        copy.start()
    moves = [
        pltpu.make_async_copy(
            out_hbm.at[pl.ds(8 * part, 8)], output.at[pl.ds(8 * part, 8)], sems.at[part]
        )
        for part in range(8)
    ]
    for move in moves:
        move.start()
    for copy in copies:
        copy.wait()
    own = own_modes[...]
    shifted = jnp.concatenate([own * scales[s, 0:1, :] for s in range(N_GRP)], 0)
    columns = shifted.T
    rows = modes_g[...].astype(F32).reshape(64, 128)
    other = turned(rows, 1.0, -1.0)
    for k in range(16):
        total = jnp.zeros((64, 128), F32)
        for s in range(N_GRP):
            at = s * 16 + k
            total = total + columns[0:64, at : at + 1] * rows[at : at + 1]
            total = total + columns[64:128, at : at + 1] * other[at : at + 1]
        d_spec[k] = total
    sums = sums_ref[...].reshape(64, 128)
    d_local[...] = sums[:, 0:64]
    d_bias[...] = sums[0:1, 64:128]
    for move in moves:
        move.wait()


def weights_call(out, modes_g, own_modes, scales, sums):
    vmem = pl.BlockSpec(memory_space=pltpu.VMEM)
    hbm = pl.BlockSpec(memory_space=pl.ANY)
    return pl.pallas_call(
        weights_kernel,
        out_shape=(
            jax.ShapeDtypeStruct(out.shape, BF16),
            jax.ShapeDtypeStruct((16, 64, 128), F32),
            jax.ShapeDtypeStruct((64, 64), F32),
            jax.ShapeDtypeStruct((1, 64), F32),
        ),
        in_specs=[hbm] * 5,
        out_specs=(hbm,) + (vmem,) * 3,
        scratch_shapes=[
            pltpu.VMEM((4, 16, 128), BF16),
            pltpu.VMEM((16, 128), F32),
            pltpu.VMEM((4, 8, 128), F32),
            pltpu.VMEM((8, 8, 128), F32),
            pltpu.SemaphoreType.DMA((12,)),
        ],
        compiler_params=pltpu.CompilerParams(vmem_limit_bytes=58 * MIB),
    )(out, modes_g, own_modes, scales, sums)


def shards(base_field, cotangent, w_spec, w_local, bias, direction, shift):
    number = lax.axis_index("grp") + 1
    gray_code = jnp.bitwise_xor(number, number >> 1)
    picked = [
        jnp.where(gray_code >> bit_pos & 1 == 1, direction[:, bit_pos], 0)
        for bit_pos in range(N_GRP.bit_length())
    ]
    mixed_bits = reduce(jnp.bitwise_xor, picked)
    sobol_point = jnp.bitwise_xor(mixed_bits, shift[0]).astype(F32) * 2.0 ** (-30)
    scale = 0.5 + sobol_point
    scale_rows = jnp.broadcast_to(jnp.concatenate([scale, scale])[None, :], (8, 128))
    out, modes_g, own_modes, scales, sums = layer_call(
        base_field, cotangent[0], w_spec.reshape(16, 64, 128), w_local, scale_rows, bias
    )
    output, d_spec, d_local, d_bias = weights_call(out, modes_g, own_modes, scales, sums)
    return (output[None], d_spec.reshape(4, 4, 64, 128), d_local, d_bias.reshape(64))


def solution(mesh):
    return jax.shard_map(
        shards,
        mesh=mesh,
        in_specs=(
            P(None, "slab", None, None),
            P("grp", None, "slab", None, None),
            P("grp", "slab", None, None),
            P(),
            P(),
            P(),
            P("grp", None),
        ),
        out_specs=(P("grp", None, "slab", None, None), P("grp", "slab", None, None), P(), P()),
        check_vma=False,
    )
```

```python
from functools import reduce
import math

import jax
import jax.numpy as jnp
import ml_dtypes
import numpy as np
from jax import lax
from jax.experimental import pallas as pl
from jax.experimental.pallas import tpu as pltpu
from jax.sharding import PartitionSpec as P

CH = 64
NX = 128
NY = 128
NZ = 128
MODES = 16
BITS = 30
N_GRP = 4
N_SLAB = 64
N_LOW = 8
N_Z = 8
MESH = pl.DeviceIdType.MESH
F32 = jnp.float32
BF16 = jnp.bfloat16
MIB = 1024 * 1024


def waves(length, half):
    ids = np.arange(MODES)
    if not half:
        ids = np.where(ids < MODES // 2, ids, length - MODES + ids)
    angles = 2.0 * math.pi / length * (ids[:, None] * np.arange(length)[None, :] % length)
    return np.cos(angles), np.sin(angles)


def as_bf16(table):
    return np.asarray(table, np.float32).astype(ml_dtypes.bfloat16)


def table_ty():
    cos_y, sin_y = waves(NY, False)
    out = np.zeros((2, 2, MODES, 2, NY))
    for c2 in range(2):
        out[0, c2, :, c2] = cos_y
        out[1, c2, :, c2] = sin_y
    return as_bf16(out.reshape(64, 256))


def weights_z(backward):
    return np.where(np.arange(MODES) == 0, 1.0, 2.0 if backward else 1.0)[:, None]


def table_zt(backward):
    cos_z, sin_z = waves(NZ, True)
    weight = weights_z(backward)
    cos_z = (weight * cos_z).reshape(4, 4, NZ)
    sin_z = (weight * sin_z).reshape(4, 4, NZ)
    out = np.zeros((2, 4, 2, 4, 2, 2, NZ))
    for x in range(2):
        out[0, :, x, :, 0, x] = cos_z
        out[0, :, x, :, 1, x] = -sin_z
        out[1, :, x, :, 0, x] = -sin_z
        out[1, :, x, :, 1, x] = -cos_z
    return as_bf16(out.reshape(64, 512))


def table_tx():
    cos_x, sin_x = waves(NX, False)
    out = np.zeros((2, MODES, 4, NX, 4))
    for m in range(4):
        out[0, :, m, :, m] = cos_x
        out[1, :, m, :, m] = sin_x
    return as_bf16(out.reshape(128, 512))


def table_ey():
    cos_y, sin_y = waves(NY, False)
    out = np.zeros((2, NY, 2, 2, MODES))
    for c2 in range(2):
        out[c2, :, c2, 0] = cos_y.T
        out[c2, :, c2, 1] = -sin_y.T
    return as_bf16(out.reshape(256, 64))


def table_ez():
    cos_z, sin_z = waves(NZ, True)
    weight = weights_z(True) / math.sqrt(MODES**3)
    cos_z = (weight * cos_z).reshape(4, 4, NZ)
    sin_z = (weight * sin_z).reshape(4, 4, NZ)
    out = np.zeros((2, 4, 2, 4, 2, 2, NZ))
    for x in range(2):
        out[0, :, x, :, 0, x] = cos_z
        out[1, :, x, :, 0, x] = -sin_z
        out[0, :, x, :, 1, x] = sin_z
        out[1, :, x, :, 1, x] = cos_z
    return as_bf16(out.reshape(64, 512))


def lane_sign(rows, first, second):
    lane = lax.broadcasted_iota(jnp.int32, (rows, 128), 1)
    return jnp.where(lane < 64, first, second).astype(F32)


def turned(rows, first, second):
    return pltpu.roll(rows, 64, 1) * lane_sign(rows.shape[0], first, second)


def nt_dot(left, right, precision=None):
    return lax.dot_general(
        left, right, (((1,), (1,)), ((), ())), preferred_element_type=F32, precision=precision
    )


def fetch_field(field, held, sems):
    for part in range(8):
        rows = pl.ds(8 * part, 8)
        pltpu.make_async_copy(field.at[rows], held.at[rows], sems.at[part]).start()


def wait_field(field, held, sems, part):
    rows = pl.ds(8 * part, 8)
    pltpu.make_async_copy(field.at[rows], held.at[rows], sems.at[part]).wait()


def store_along_y(along_y, got, first):
    for cs in range(2):
        for c2 in range(2):
            at = cs * 32 + c2 * 16
            for x in range(2):
                start = (2 * cs + x) * 1024 + first + c2
                along_y[pl.ds(start, 16, stride=64), :] = got[
                    at : at + 16, x * 128 : x * 128 + 128
                ]


def along_z_modes(along_y, zt_ref, slab_modes):
    for quarter in range(4):
        rows = jnp.concatenate(
            [
                along_y[part * 1024 + quarter * 256 : part * 1024 + quarter * 256 + 256, :]
                for part in range(4)
            ],
            1,
        ).astype(BF16)
        got = nt_dot(zt_ref[...], rows)
        for jy in range(4):
            real = got[0:32, jy * 64 : jy * 64 + 64]
            imag = got[32:64, jy * 64 : jy * 64 + 64]
            owner = (quarter * 4 + jy) * 4
            slab_modes[owner : owner + 4] = (
                jnp.concatenate([real, imag], 1).reshape(4, 8, 128).astype(BF16)
            )


def greet(barrier, me, grp):
    def tell(step, carry):
        pl.semaphore_signal(
            barrier, inc=1, device_id={"slab": lax.rem(me + step, N_SLAB)}, device_id_type=MESH
        )
        return carry

    lax.fori_loop(1, N_SLAB, tell, 0)
    for step in range(1, N_GRP):
        pl.semaphore_signal(
            barrier, inc=1, device_id={"grp": lax.rem(grp + step, N_GRP)}, device_id_type=MESH
        )


def send_all(source, target, send_sem, recv_sem, me):
    low = lax.rem(me, N_LOW)
    z = me // N_LOW
    for dz in (4, 3, 5, 2, 6, 1, 7, 0):

        def go(step, carry):
            other = lax.rem(z + dz, N_Z) * N_LOW + lax.rem(low + step, N_LOW)
            pltpu.make_async_remote_copy(
                src_ref=source.at[other],
                dst_ref=target.at[me],
                send_sem=send_sem,
                recv_sem=recv_sem,
                device_id={"slab": other},
                device_id_type=MESH,
            ).start()
            return carry

        lax.fori_loop(1 if dz == 0 else 0, N_LOW, go, 0)
    target[pl.ds(me, 1)] = source[pl.ds(me, 1)]


def wait_blocks(source, target, send_sem, recv_sem, count, me):
    pltpu.make_async_remote_copy(
        src_ref=source.at[pl.ds(0, count)],
        dst_ref=target.at[pl.ds(0, count)],
        send_sem=send_sem,
        recv_sem=recv_sem,
        device_id={"slab": me},
        device_id_type=MESH,
    ).wait()


def send_grp(source, target, send_sem, recv_sem, grp, by_target):
    for step in range(1, N_GRP):
        other = lax.rem(grp + step, N_GRP)
        pltpu.make_async_remote_copy(
            src_ref=source.at[other] if by_target else source.at[grp],
            dst_ref=target.at[grp],
            send_sem=send_sem,
            recv_sem=recv_sem,
            device_id={"grp": other},
            device_id_type=MESH,
        ).start()


def x_modes(pencil, tx_ref):
    rows = pencil[...].astype(F32).reshape(512, 128).astype(BF16)
    both = jnp.dot(tx_ref[...], rows, preferred_element_type=F32)
    return both[:64] + turned(both[64:], 1.0, -1.0)


GELU_K = math.sqrt(2.0 / math.pi)
GELU_A = GELU_K * 0.044715
GRAD_SCALE = 1.0 / math.sqrt(N_GRP * NX * NY * NZ)


def local_step(part, held, kron, field_rows, local):
    y_at = pl.multiple_of(16 * part, 16)
    halves = [held[:, x, pl.ds(y_at, 16), :].astype(F32) for x in range(2)]
    for half in range(2):
        rows = jnp.concatenate(
            [block[:, 8 * half : 8 * half + 8].reshape(512, 128) for block in halves], 1
        ).astype(BF16)
        field_rows[part, :, half * 256 : half * 256 + 256] = rows
        got = jnp.dot(kron[...], rows, preferred_element_type=F32)
        local[:, pl.ds(pl.multiple_of(y_at + 8 * half, 8), 8), :] = got.reshape(64, 8, 256)


def fill_kron(wl_ref, scale_row, kron):
    local = (wl_ref[...].astype(F32) * scale_row[0:1, 0:64]).astype(BF16)
    pick = (
        lax.broadcasted_iota(jnp.int32, (64, 512), 0)
        == lax.broadcasted_iota(jnp.int32, (64, 512), 1) // 8
    )
    wide = jnp.dot(local, pick.astype(F32).astype(BF16), preferred_element_type=F32).astype(BF16)
    same = (
        lax.broadcasted_iota(jnp.int32, (64, 512), 0) % 8
        == lax.broadcasted_iota(jnp.int32, (64, 512), 1) % 8
    )
    row_ids = lax.broadcasted_iota(jnp.int32, (64, 64), 0) // 8
    col_ids = lax.broadcasted_iota(jnp.int32, (64, 64), 1)
    for octet in range(8):
        rows_of = (row_ids + 8 * octet == col_ids).astype(F32).astype(BF16)
        tall = jnp.dot(rows_of, wide, preferred_element_type=F32)
        kron[octet * 64 : octet * 64 + 64, :] = jnp.where(same, tall, 0.0).astype(BF16)


def fill_along_z(landed, ez_ref, along_z):
    for quarter in range(4):
        rows = landed[quarter * 16 : quarter * 16 + 16].astype(F32).reshape(128, 128)
        turn = rows.T
        per_c = jnp.concatenate(
            [
                jnp.concatenate(
                    [turn[0:64, jy * 32 : jy * 32 + 32], turn[64:128, jy * 32 : jy * 32 + 32]], 1
                )
                for jy in range(4)
            ],
            0,
        ).astype(BF16)
        got = jnp.dot(per_c, ez_ref[...], preferred_element_type=F32)
        for jy in range(4):
            for cs in range(2):
                for x in range(2):
                    start = x * 2048 + cs * 16 + quarter * 4 + jy
                    lane = cs * 256 + x * 128
                    along_z[pl.ds(start, 64, stride=32), :] = got[
                        jy * 64 : jy * 64 + 64, lane : lane + 128
                    ]


def cells_step(
    index, along_z, local, bias_ref, cotan_in, ey_ref, ty_ref, out_held, cotan_rows, bias_sum, along_y
):
    rows = jnp.concatenate(
        [along_z[pl.ds(pl.multiple_of(x * 2048 + 64 * index, 64), 64), :] for x in range(2)], 1
    ).astype(BF16)
    got = jnp.dot(ey_ref[...], rows, preferred_element_type=F32)
    cells = []
    for c2 in range(2):
        channel = 2 * index + c2
        both = []
        for x in range(2):
            lanes = slice(x * 128, x * 128 + 128)
            pre = got[c2 * 128 : c2 * 128 + 128, lanes] + (
                local[channel, :, lanes] + bias_ref[channel]
            )
            square = pre * pre
            half_tanh = 0.5 + 0.5 * jnp.tanh(pre * (GELU_K + GELU_A * square))
            out_held[channel, x] = (pre * half_tanh).astype(BF16)
            slope = half_tanh + half_tanh * (1.0 - half_tanh) * (
                pre * (2.0 * GELU_K + 6.0 * GELU_A * square)
            )
            both.append(slope * (cotan_in[channel, x].astype(F32) * GRAD_SCALE))
        total = both[0] + both[1]
        bias_sum[channel] = jnp.sum(total.reshape(16, 8, 128), axis=0)
        cells.append(both)
    for y8 in range(16):
        for x in range(2):
            block = jnp.concatenate(
                [cells[c2][x][8 * y8 : 8 * y8 + 8] for c2 in range(2)], 0
            ).astype(BF16)
            lane = (y8 % 2) * 256 + x * 128
            cotan_rows[
                y8 // 2, pl.ds(pl.multiple_of(16 * index, 16), 16), lane : lane + 128
            ] = block
    wide = jnp.concatenate([jnp.concatenate(both, 1) for both in cells], 0).astype(BF16)
    store_along_y(
        along_y, jnp.dot(ty_ref[...], wide, preferred_element_type=F32), 2 * index
    )


def sums_of(grad, bias_sum, scale_row):
    same = (
        lax.broadcasted_iota(jnp.int32, (512, 512), 0) % 8
        == lax.broadcasted_iota(jnp.int32, (512, 512), 1) % 8
    )
    per_c = jnp.sum(jnp.where(same, grad, 0.0).reshape(64, 8, 512), axis=1)
    pick = (
        lax.broadcasted_iota(jnp.int32, (512, 64), 0) // 8
        == lax.broadcasted_iota(jnp.int32, (512, 64), 1)
    ).astype(F32)
    d_local = jnp.dot(per_c, pick, preferred_element_type=F32, precision=lax.Precision.HIGHEST)
    d_local = d_local * scale_row[0:1, 0:64]
    lanes = jnp.sum(bias_sum[...], axis=1)
    d_bias = nt_dot(jnp.ones((8, 128), F32), lanes, lax.Precision.HIGHEST)
    side = jnp.concatenate([d_bias, jnp.zeros((56, 64), F32)], 0)
    return jnp.concatenate([d_local, side], 1).reshape(8, 8, 128)


def layer_kernel(
    field, cotan, w_hbm, wl_hbm, scale_hbm, bias_ref,
    ty_hbm, ztf_hbm, ztb_hbm, tx_hbm, txb_hbm, ey_hbm, ez_hbm,
    out_hbm, modes_out, own_modes, scales, sums_out,
    ty_ref, ztf_ref, ztb_ref, tx_ref, txb_ref, ey_ref, ez_ref, w_ref, wl_ref, scale_ref,
    held, cotan_in, out_held, field_rows, cotan_rows, local, along_y, along_z, kron, w_two,
    slab_modes, pencil, mixed, gathered, back, landed, slab_g, pencil_g, mixed_g, gathered_g,
    all_modes, scale_own, scale_all, bias_sum, own_sums, first, second, second_own, third,
    field_sems, cotan_sems, table_sems, out_sems, send_sems, recv_sems,
):
    me = lax.axis_index("slab")
    grp = lax.axis_index("grp")
    low = lax.rem(me, N_LOW)
    z = me // N_LOW
    barrier = pltpu.get_barrier_semaphore()
    small = [
        (ty_hbm, ty_ref), (ztf_hbm, ztf_ref), (scale_hbm, scale_ref), (wl_hbm, wl_ref),
        (w_hbm, w_ref), (tx_hbm, tx_ref), (txb_hbm, txb_ref), (ey_hbm, ey_ref),
        (ez_hbm, ez_ref), (ztb_hbm, ztb_ref),
    ]
    copies = [
        pltpu.make_async_copy(source, target, table_sems.at[at])
        for at, (source, target) in enumerate(small)
    ]
    for copy in copies[:2]:
        copy.start()
    fetch_field(field, held, field_sems)
    for copy in copies[2:]:
        copy.start()
    fetch_field(cotan, cotan_in, cotan_sems)
    greet(barrier, me, grp)
    for g_step in range(1, N_GRP):

        def tell(step, carry):
            pl.semaphore_signal(
                barrier,
                inc=1,
                device_id={
                    "grp": lax.rem(grp + g_step, N_GRP),
                    "slab": lax.rem(z + step, N_Z) * N_LOW + low,
                },
                device_id_type=MESH,
            )
            return carry

        lax.fori_loop(1, N_Z, tell, 0)

    copies[0].wait()

    def channels(part, carry):
        wait_field(field, held, field_sems, part)
        for pair in range(4):
            first_c = 8 * part + 2 * pair
            rows = jnp.concatenate(
                [
                    jnp.concatenate([held[first_c + c2, 0], held[first_c + c2, 1]], 1)
                    for c2 in range(2)
                ],
                0,
            )
            store_along_y(
                along_y, jnp.dot(ty_ref[...], rows, preferred_element_type=F32), first_c
            )
        return carry

    lax.fori_loop(0, 8, channels, 0)
    copies[1].wait()
    along_z_modes(along_y, ztf_ref, slab_modes)
    copies[2].wait()
    scale_own[grp] = scale_ref[...]
    scale_all[grp] = scale_ref[...]
    pl.semaphore_wait(barrier, N_SLAB - 1 + N_GRP - 1 + (N_GRP - 1) * (N_Z - 1))
    send_all(slab_modes, pencil, send_sems.at[0], recv_sems.at[0], me)
    send_grp(scale_own, scale_all, send_sems.at[1], recv_sems.at[1], grp, False)

    copies[3].wait()
    copies[4].wait()
    for k in range(16):
        block = w_ref[k].astype(F32)
        w_two[k * 128 : k * 128 + 64, :] = w_ref[k]
        w_two[k * 128 + 64 : k * 128 + 128, :] = turned(block, -1.0, 1.0).astype(BF16)
    fill_kron(wl_ref, scale_ref[...], kron)

    def local_some(part, carry):
        local_step(part, held, kron, field_rows, local)
        return carry

    lax.fori_loop(0, 3, local_some, 0)
    pltpu.make_async_remote_copy(
        src_ref=scale_own.at[pl.ds(0, N_GRP - 1)],
        dst_ref=scale_all.at[pl.ds(0, N_GRP - 1)],
        send_sem=send_sems.at[1],
        recv_sem=recv_sems.at[1],
        device_id={"slab": me},
        device_id_type=MESH,
    ).wait()
    scales[...] = scale_all[...]
    copies[5].wait()
    copies[6].wait()
    wait_blocks(slab_modes, pencil, send_sems.at[0], recv_sems.at[0], N_SLAB - 1, me)

    all_modes[...] = x_modes(pencil, tx_ref) * (1.0 / math.sqrt(NX * NY * NZ))
    own = all_modes[pl.ds(pl.multiple_of(16 * grp, 16), 16), :]
    own_modes[...] = own
    shifted = jnp.concatenate([own * scale_all[s, 0:1, :] for s in range(N_GRP)], 0)
    row_mode = lax.broadcasted_iota(jnp.int32, (64, 128), 0) % 16
    spread = jnp.concatenate(
        [jnp.where(row_mode == k, shifted, 0.0).astype(BF16) for k in range(16)], 1
    )
    mixed[...] = (
        jnp.dot(spread, w_two[...], preferred_element_type=F32).astype(BF16).reshape(4, 16, 128)
    )
    send_grp(mixed, gathered, send_sems.at[2], recv_sems.at[2], grp, True)
    gathered[pl.ds(grp, 1)] = mixed[pl.ds(grp, 1)]
    lax.fori_loop(3, 5, local_some, 0)
    wait_blocks(mixed, gathered, send_sems.at[2], recv_sems.at[2], N_GRP - 1, me)
    full = gathered[...].reshape(64, 128)
    both = jnp.concatenate([full, turned(full.astype(F32), -1.0, 1.0).astype(BF16)], 0)
    back[...] = (
        jnp.dot(txb_ref[...], both, preferred_element_type=F32).reshape(64, 8, 128).astype(BF16)
    )
    send_all(back, landed, send_sems.at[3], recv_sems.at[3], me)
    lax.fori_loop(5, 8, local_some, 0)
    for copy in copies[7:]:
        copy.wait()
    for part in range(8):
        wait_field(cotan, cotan_in, cotan_sems, part)
    wait_blocks(back, landed, send_sems.at[3], recv_sems.at[3], N_SLAB - 1, me)

    fill_along_z(landed, ez_ref, along_z)

    def some_cells(part, carry):
        for pair in range(2):
            cells_step(
                2 * part + pair, along_z, local, bias_ref, cotan_in, ey_ref, ty_ref, out_held,
                cotan_rows, bias_sum, along_y,
            )
        return carry

    def cells_part(part, carry):
        lax.fori_loop(2 * part, 2 * part + 2, some_cells, 0)
        rows = pl.ds(8 * part, 8)
        pltpu.make_async_copy(out_held.at[rows], out_hbm.at[rows], out_sems.at[part]).start()
        return carry

    lax.fori_loop(0, 8, cells_part, 0)

    grad = jnp.zeros((512, 512), F32)
    for part in range(8):
        grad = grad + nt_dot(cotan_rows[part], field_rows[part])
    own_sums[...] = sums_of(grad, bias_sum, scale_ref[...])

    def scatter(step, carry):
        other = lax.rem(low + step, N_LOW)
        pltpu.make_async_remote_copy(
            src_ref=own_sums.at[other],
            dst_ref=first.at[low],
            send_sem=send_sems.at[4],
            recv_sem=recv_sems.at[4],
            device_id={"slab": z * N_LOW + other},
            device_id_type=MESH,
        ).start()
        return carry

    lax.fori_loop(1, N_LOW, scatter, 0)
    first[pl.ds(low, 1)] = own_sums[pl.ds(low, 1)]
    along_z_modes(along_y, ztb_ref, slab_g)
    send_all(slab_g, pencil_g, send_sems.at[5], recv_sems.at[5], me)
    wait_blocks(own_sums, first, send_sems.at[4], recv_sems.at[4], N_LOW - 1, me)
    part_sum = jnp.sum(first[...], axis=0, keepdims=True)
    mine = grp * N_Z + z
    second[pl.ds(mine, 1)] = part_sum
    second_own[...] = part_sum
    for g_step in (2, 1, 3, 0):

        def spread_sum(step, carry):
            pltpu.make_async_remote_copy(
                src_ref=second_own.at[0],
                dst_ref=second.at[mine],
                send_sem=send_sems.at[6],
                recv_sem=recv_sems.at[6],
                device_id={
                    "grp": lax.rem(grp + g_step, N_GRP),
                    "slab": lax.rem(z + step, N_Z) * N_LOW + low,
                },
                device_id_type=MESH,
            ).start()
            return carry

        lax.fori_loop(1 if g_step == 0 else 0, N_Z, spread_sum, 0)
    wait_blocks(slab_g, pencil_g, send_sems.at[5], recv_sems.at[5], N_SLAB - 1, me)
    mixed_g[...] = x_modes(pencil_g, tx_ref).astype(BF16).reshape(4, 16, 128)
    send_grp(mixed_g, gathered_g, send_sems.at[7], recv_sems.at[7], grp, True)
    gathered_g[pl.ds(grp, 1)] = mixed_g[pl.ds(grp, 1)]
    wait_blocks(second, second, send_sems.at[6], recv_sems.at[6], N_GRP * N_Z - 1, me)
    third[pl.ds(low, 1)] = jnp.sum(second[...], axis=0, keepdims=True)

    def collect(step, carry):
        pltpu.make_async_remote_copy(
            src_ref=third.at[low],
            dst_ref=third.at[low],
            send_sem=send_sems.at[8],
            recv_sem=recv_sems.at[8],
            device_id={"slab": z * N_LOW + lax.rem(low + step, N_LOW)},
            device_id_type=MESH,
        ).start()
        return carry

    lax.fori_loop(1, N_LOW, collect, 0)
    wait_blocks(mixed_g, gathered_g, send_sems.at[7], recv_sems.at[7], N_GRP - 1, me)
    modes_out[...] = gathered_g[...]
    for part in range(8):
        rows = pl.ds(8 * part, 8)
        pltpu.make_async_copy(out_held.at[rows], out_hbm.at[rows], out_sems.at[part]).wait()
    wait_blocks(third, third, send_sems.at[8], recv_sems.at[8], N_LOW - 1, me)
    sums_out[...] = third[...]


def layer_call(field, cotangent, w_spec, w_local, scale_rows, bias):
    vmem = pl.BlockSpec(memory_space=pltpu.VMEM)
    hbm = pl.BlockSpec(memory_space=pl.ANY)
    tables = (
        table_ty(), table_zt(False), table_zt(True), table_tx(),
        np.ascontiguousarray(table_tx().T), table_ey(), table_ez(),
    )
    cells = (64, 2, 128, 128)
    blocks = pltpu.VMEM((64, 8, 128), BF16)
    quads = pltpu.VMEM((4, 16, 128), BF16)
    return pl.pallas_call(
        layer_kernel,
        out_shape=(
            jax.ShapeDtypeStruct(cells, BF16),
            jax.ShapeDtypeStruct((4, 16, 128), BF16),
            jax.ShapeDtypeStruct((16, 128), F32),
            jax.ShapeDtypeStruct((4, 8, 128), F32),
            jax.ShapeDtypeStruct((8, 8, 128), F32),
        ),
        in_specs=[hbm] * 5 + [pl.BlockSpec(memory_space=pltpu.SMEM)] + [hbm] * 7,
        out_specs=(hbm,) + (vmem,) * 4,
        scratch_shapes=[pltpu.VMEM(table.shape, BF16) for table in tables]
        + [
            pltpu.VMEM((16, 64, 128), BF16),
            pltpu.VMEM((64, 64), BF16),
            pltpu.VMEM((8, 128), F32),
            pltpu.VMEM(cells, BF16),
            pltpu.VMEM(cells, BF16),
            pltpu.VMEM(cells, BF16),
            pltpu.VMEM((8, 512, 512), BF16),
            pltpu.VMEM((8, 512, 512), BF16),
            pltpu.VMEM((64, 128, 256), F32),
            pltpu.VMEM((4096, 128), F32),
            pltpu.VMEM((4096, 128), F32),
            pltpu.VMEM((512, 512), BF16),
            pltpu.VMEM((2048, 128), BF16),
            blocks, blocks, quads, quads, blocks, blocks, blocks, blocks, quads, quads,
            pltpu.VMEM((64, 128), F32),
            pltpu.VMEM((4, 8, 128), F32),
            pltpu.VMEM((4, 8, 128), F32),
            pltpu.VMEM((64, 8, 128), F32),
            pltpu.VMEM((8, 8, 128), F32),
            pltpu.VMEM((8, 8, 128), F32),
            pltpu.VMEM((32, 8, 128), F32),
            pltpu.VMEM((1, 8, 128), F32),
            pltpu.VMEM((8, 8, 128), F32),
            pltpu.SemaphoreType.DMA((8,)),
            pltpu.SemaphoreType.DMA((8,)),
            pltpu.SemaphoreType.DMA((10,)),
            pltpu.SemaphoreType.DMA((8,)),
            pltpu.SemaphoreType.DMA((9,)),
            pltpu.SemaphoreType.DMA((9,)),
        ],
        compiler_params=pltpu.CompilerParams(
            collective_id=0, has_side_effects=True, vmem_limit_bytes=58 * MIB
        ),
    )(field, cotangent, w_spec, w_local, scale_rows, bias, *tables)


def weights_kernel(
    out_hbm, modes_hbm, own_hbm, scales_hbm, sums_hbm,
    output, d_spec, d_local, d_bias,
    held, modes_g, own_modes, scales, sums_ref, sems, in_sems, out_sems,
):
    small = [
        (modes_hbm, modes_g), (own_hbm, own_modes), (scales_hbm, scales), (sums_hbm, sums_ref)
    ]
    copies = [
        pltpu.make_async_copy(source, target, sems.at[at])
        for at, (source, target) in enumerate(small)
    ]
    for copy in copies:
        copy.start()
    ins = []
    outs = []
    for part in range(8):
        rows = pl.ds(8 * part, 8)
        ins.append(pltpu.make_async_copy(out_hbm.at[rows], held.at[rows], in_sems.at[part]))
        outs.append(pltpu.make_async_copy(held.at[rows], output.at[rows], out_sems.at[part]))
    for copy in ins:
        copy.start()
    for copy in copies:
        copy.wait()
    own = own_modes[...]
    shifted = jnp.concatenate([own * scales[s, 0:1, :] for s in range(N_GRP)], 0)
    columns = shifted.T
    rows = modes_g[...].astype(F32).reshape(64, 128)
    other = turned(rows, 1.0, -1.0)
    for k in range(16):
        total = jnp.zeros((64, 128), F32)
        for s in range(N_GRP):
            at = s * 16 + k
            total = total + columns[0:64, at : at + 1] * rows[at : at + 1]
            total = total + columns[64:128, at : at + 1] * other[at : at + 1]
        d_spec[k] = total
        if k % 2:
            ins[k // 2].wait()
            outs[k // 2].start()
    sums = sums_ref[...].reshape(64, 128)
    d_local[...] = sums[:, 0:64]
    d_bias[...] = sums[0:1, 64:128]
    for copy in outs:
        copy.wait()


def weights_call(out, modes_g, own_modes, scales, sums):
    vmem = pl.BlockSpec(memory_space=pltpu.VMEM)
    hbm = pl.BlockSpec(memory_space=pl.ANY)
    return pl.pallas_call(
        weights_kernel,
        out_shape=(
            jax.ShapeDtypeStruct(out.shape, BF16),
            jax.ShapeDtypeStruct((16, 64, 128), F32),
            jax.ShapeDtypeStruct((64, 64), F32),
            jax.ShapeDtypeStruct((1, 64), F32),
        ),
        in_specs=[hbm] * 5,
        out_specs=(hbm,) + (vmem,) * 3,
        scratch_shapes=[
            pltpu.VMEM(out.shape, BF16),
            pltpu.VMEM((4, 16, 128), BF16),
            pltpu.VMEM((16, 128), F32),
            pltpu.VMEM((4, 8, 128), F32),
            pltpu.VMEM((8, 8, 128), F32),
            pltpu.SemaphoreType.DMA((4,)),
            pltpu.SemaphoreType.DMA((8,)),
            pltpu.SemaphoreType.DMA((8,)),
        ],
        compiler_params=pltpu.CompilerParams(vmem_limit_bytes=58 * MIB),
    )(out, modes_g, own_modes, scales, sums)


def shards(base_field, cotangent, w_spec, w_local, bias, direction, shift):
    number = lax.axis_index("grp") + 1
    gray_code = jnp.bitwise_xor(number, number >> 1)
    picked = [
        jnp.where(gray_code >> bit_pos & 1 == 1, direction[:, bit_pos], 0)
        for bit_pos in range(N_GRP.bit_length())
    ]
    mixed_bits = reduce(jnp.bitwise_xor, picked)
    sobol_point = jnp.bitwise_xor(mixed_bits, shift[0]).astype(F32) * 2.0 ** (-30)
    scale = 0.5 + sobol_point
    scale_rows = jnp.broadcast_to(jnp.concatenate([scale, scale])[None, :], (8, 128))
    out, modes_g, own_modes, scales, sums = layer_call(
        base_field, cotangent[0], w_spec.reshape(16, 64, 128), w_local, scale_rows, bias
    )
    output, d_spec, d_local, d_bias = weights_call(out, modes_g, own_modes, scales, sums)
    return (output[None], d_spec.reshape(4, 4, 64, 128), d_local, d_bias.reshape(64))


def solution(mesh):
    return jax.shard_map(
        shards,
        mesh=mesh,
        in_specs=(
            P(None, "slab", None, None),
            P("grp", None, "slab", None, None),
            P("grp", "slab", None, None),
            P(),
            P(),
            P(),
            P("grp", None),
        ),
        out_specs=(P("grp", None, "slab", None, None), P("grp", "slab", None, None), P(), P()),
        check_vma=False,
    )
```

```python
import math

import jax
import jax.numpy as jnp
import ml_dtypes
import numpy as np
from jax import lax
from jax.experimental import pallas as pl
from jax.experimental.pallas import tpu as pltpu
from jax.sharding import PartitionSpec as P

CH = 64
NX = 128
NY = 128
NZ = 128
MODES = 16
BITS = 30
N_GRP = 4
N_SLAB = 64
N_LOW = 8
N_Z = 8
MESH = pl.DeviceIdType.MESH
F32 = jnp.float32
BF16 = jnp.bfloat16
MIB = 1024 * 1024
GELU_K = math.sqrt(2.0 / math.pi)
GELU_A = 0.044715
GRAD_SCALE = 1.0 / math.sqrt(N_GRP * NX * NY * NZ)


def waves(length, half):
    ids = np.arange(MODES)
    if not half:
        ids = np.where(ids < MODES // 2, ids, length - MODES + ids)
    angles = 2.0 * math.pi / length * (ids[:, None] * np.arange(length)[None, :] % length)
    return np.cos(angles), np.sin(angles)


def as_bf16(table):
    return np.asarray(table, np.float32).astype(ml_dtypes.bfloat16)


def table_ty():
    cos_y, sin_y = waves(NY, False)
    out = np.zeros((2, 2, MODES, 2, NY))
    for c2 in range(2):
        out[0, c2, :, c2] = cos_y
        out[1, c2, :, c2] = sin_y
    return as_bf16(out.reshape(64, 256))


def weights_z(backward):
    return np.where(np.arange(MODES) == 0, 1.0, 2.0 if backward else 1.0)[:, None]


def table_zt(backward):
    cos_z, sin_z = waves(NZ, True)
    weight = weights_z(backward)
    if backward:
        weight = weight * GRAD_SCALE
    cos_z = (weight * cos_z).reshape(4, 4, NZ)
    sin_z = (weight * sin_z).reshape(4, 4, NZ)
    out = np.zeros((2, 4, 2, 4, 2, 2, NZ))
    for x in range(2):
        out[0, :, x, :, 0, x] = cos_z
        out[0, :, x, :, 1, x] = -sin_z
        out[1, :, x, :, 0, x] = -sin_z
        out[1, :, x, :, 1, x] = -cos_z
    return as_bf16(out.reshape(64, 512))


def table_tx():
    cos_x, sin_x = waves(NX, False)
    out = np.zeros((2, MODES, 4, NX, 4))
    for m in range(4):
        out[0, :, m, :, m] = cos_x
        out[1, :, m, :, m] = sin_x
    return as_bf16(out.reshape(128, 512))


def table_ey():
    cos_y, sin_y = waves(NY, False)
    out = np.zeros((2, NY, 2, 2, MODES))
    for c2 in range(2):
        out[c2, :, c2, 0] = cos_y.T
        out[c2, :, c2, 1] = -sin_y.T
    return as_bf16(out.reshape(256, 64))


def table_ez():
    cos_z, sin_z = waves(NZ, True)
    weight = weights_z(True) / math.sqrt(MODES**3)
    cos_z = (weight * cos_z).reshape(4, 4, NZ)
    sin_z = (weight * sin_z).reshape(4, 4, NZ)
    out = np.zeros((2, 4, 2, 4, 2, 2, NZ))
    for x in range(2):
        out[0, :, x, :, 0, x] = cos_z
        out[1, :, x, :, 0, x] = -sin_z
        out[0, :, x, :, 1, x] = sin_z
        out[1, :, x, :, 1, x] = cos_z
    return as_bf16(out.reshape(64, 512))


def lane_sign(rows, first, second):
    lane = lax.broadcasted_iota(jnp.int32, (rows, 128), 1)
    return jnp.where(lane < 64, first, second).astype(F32)


def turned(rows, first, second):
    return pltpu.roll(rows, 64, 1) * lane_sign(rows.shape[0], first, second)


def nt_dot(left, right, precision=None):
    return lax.dot_general(
        left, right, (((1,), (1,)), ((), ())), preferred_element_type=F32, precision=precision
    )


def fetch_field(field, held, sems):
    for part in range(8):
        rows = pl.ds(8 * part, 8)
        pltpu.make_async_copy(field.at[rows], held.at[rows], sems.at[part]).start()


def wait_field(field, held, sems, part):
    rows = pl.ds(8 * part, 8)
    pltpu.make_async_copy(field.at[rows], held.at[rows], sems.at[part]).wait()


def store_along_y(along_y, got, first):
    for cs in range(2):
        for c2 in range(2):
            at = cs * 32 + c2 * 16
            for x in range(2):
                start = (2 * cs + x) * 1024 + first + c2
                along_y[pl.ds(start, 16, stride=64), :] = got[
                    at : at + 16, x * 128 : x * 128 + 128
                ]


def along_z_modes(along_y, zt_ref, slab_modes):
    for quarter in range(4):
        rows = jnp.concatenate(
            [
                along_y[part * 1024 + quarter * 256 : part * 1024 + quarter * 256 + 256, :]
                for part in range(4)
            ],
            1,
        ).astype(BF16)
        got = nt_dot(zt_ref[...], rows)
        for jy in range(4):
            real = got[0:32, jy * 64 : jy * 64 + 64]
            imag = got[32:64, jy * 64 : jy * 64 + 64]
            owner = (quarter * 4 + jy) * 4
            slab_modes[owner : owner + 4] = (
                jnp.concatenate([real, imag], 1).reshape(4, 8, 128).astype(BF16)
            )


def greet(barrier, me, grp):
    def tell(step, carry):
        pl.semaphore_signal(
            barrier, inc=1, device_id={"slab": lax.rem(me + step, N_SLAB)}, device_id_type=MESH
        )
        return carry

    lax.fori_loop(1, N_SLAB, tell, 0)
    for step in range(1, N_GRP):
        pl.semaphore_signal(
            barrier, inc=1, device_id={"grp": lax.rem(grp + step, N_GRP)}, device_id_type=MESH
        )


def send_all(source, target, send_sem, recv_sem, me):
    low = lax.rem(me, N_LOW)
    z = me // N_LOW
    for dz in (4, 3, 5, 2, 6, 1, 7, 0):

        def go(step, carry):
            other = lax.rem(z + dz, N_Z) * N_LOW + lax.rem(low + step, N_LOW)
            pltpu.make_async_remote_copy(
                src_ref=source.at[other],
                dst_ref=target.at[me],
                send_sem=send_sem,
                recv_sem=recv_sem,
                device_id={"slab": other},
                device_id_type=MESH,
            ).start()
            return carry

        lax.fori_loop(1 if dz == 0 else 0, N_LOW, go, 0)
    target[pl.ds(me, 1)] = source[pl.ds(me, 1)]


def wait_blocks(source, target, send_sem, recv_sem, count, me):
    pltpu.make_async_remote_copy(
        src_ref=source.at[pl.ds(0, count)],
        dst_ref=target.at[pl.ds(0, count)],
        send_sem=send_sem,
        recv_sem=recv_sem,
        device_id={"slab": me},
        device_id_type=MESH,
    ).wait()


def send_grp(source, target, send_sem, recv_sem, grp, by_target):
    for step in range(1, N_GRP):
        other = lax.rem(grp + step, N_GRP)
        pltpu.make_async_remote_copy(
            src_ref=source.at[other] if by_target else source.at[grp],
            dst_ref=target.at[grp],
            send_sem=send_sem,
            recv_sem=recv_sem,
            device_id={"grp": other},
            device_id_type=MESH,
        ).start()


def x_modes(pencil, tx_ref):
    rows = pencil[...].astype(F32).reshape(512, 128).astype(BF16)
    both = jnp.dot(tx_ref[...], rows, preferred_element_type=F32)
    return both[:64] + turned(both[64:], 1.0, -1.0)


def local_step(part, held, kron, bias_rows, field_rows, local):
    y_at = pl.multiple_of(16 * part, 16)
    halves = [held[:, x, pl.ds(y_at, 16), :].astype(F32) for x in range(2)]
    for half in range(2):
        rows = jnp.concatenate(
            [block[:, 8 * half : 8 * half + 8].reshape(512, 128) for block in halves], 1
        ).astype(BF16)
        field_rows[part, :, half * 256 : half * 256 + 256] = rows
        got = jnp.dot(kron[...], rows, preferred_element_type=F32)
        added = bias_rows[...]
        local[:, pl.ds(pl.multiple_of(y_at + 8 * half, 8), 8), :] = got.reshape(
            64, 8, 256
        ) + jnp.concatenate([added, added], 2)


def scale_rows(grp, direction_ref, shift_ref):
    number = grp + 1
    gray_code = number ^ (number >> 1)
    bits = jnp.zeros((64, 1), jnp.int32)
    for bit_pos in range(N_GRP.bit_length()):
        bits = bits ^ (direction_ref[:, bit_pos : bit_pos + 1] * ((gray_code >> bit_pos) & 1))
    diagonal = lax.broadcasted_iota(jnp.int32, (64, 64), 0) == lax.broadcasted_iota(
        jnp.int32, (64, 64), 1
    )
    row = jnp.sum(jnp.where(diagonal, jnp.broadcast_to(bits, (64, 64)), 0), axis=0, keepdims=True)
    scale = 0.5 + (row ^ shift_ref[...]).astype(F32) * 2.0 ** (-BITS)
    return jnp.broadcast_to(jnp.concatenate([scale, scale], 1), (8, 128))


def fill_kron(wl_ref, scale_row, kron):
    local = (wl_ref[...].astype(F32) * scale_row[0:1, 0:64]).astype(BF16)
    pick = (
        lax.broadcasted_iota(jnp.int32, (64, 512), 0)
        == lax.broadcasted_iota(jnp.int32, (64, 512), 1) // 8
    )
    wide = jnp.dot(local, pick.astype(F32).astype(BF16), preferred_element_type=F32).astype(BF16)
    same = (
        lax.broadcasted_iota(jnp.int32, (64, 512), 0) % 8
        == lax.broadcasted_iota(jnp.int32, (64, 512), 1) % 8
    )
    row_ids = lax.broadcasted_iota(jnp.int32, (64, 64), 0) // 8
    col_ids = lax.broadcasted_iota(jnp.int32, (64, 64), 1)
    for octet in range(8):
        rows_of = (row_ids + 8 * octet == col_ids).astype(F32).astype(BF16)
        tall = jnp.dot(rows_of, wide, preferred_element_type=F32)
        kron[octet * 64 : octet * 64 + 64, :] = jnp.where(same, tall, 0.0).astype(BF16)


def fill_along_z(landed, ez_ref, along_z):
    for quarter in range(4):
        rows = landed[quarter * 16 : quarter * 16 + 16].astype(F32).reshape(128, 128)
        turn = rows.T
        per_c = jnp.concatenate(
            [
                jnp.concatenate(
                    [turn[0:64, jy * 32 : jy * 32 + 32], turn[64:128, jy * 32 : jy * 32 + 32]], 1
                )
                for jy in range(4)
            ],
            0,
        ).astype(BF16)
        got = jnp.dot(per_c, ez_ref[...], preferred_element_type=F32)
        for jy in range(4):
            for cs in range(2):
                for x in range(2):
                    start = x * 2048 + cs * 16 + quarter * 4 + jy
                    lane = cs * 256 + x * 128
                    along_z[pl.ds(start, 64, stride=32), :] = got[
                        jy * 64 : jy * 64 + 64, lane : lane + 128
                    ]


def synthesis(group, along_z, local, ey_ref, pre_act):
    rows = jnp.concatenate(
        [
            along_z[pl.ds(x * 2048 + 256 * group + 64 * pair, 64), :].astype(BF16)
            for pair in range(4)
            for x in range(2)
        ],
        1,
    )
    got = jnp.dot(ey_ref[...], rows, preferred_element_type=F32)
    for pair in range(4):
        for c2 in range(2):
            at = slice(c2 * 128, c2 * 128 + 128)
            lanes = slice(pair * 256, pair * 256 + 256)
            pre_act[at, lanes] = (
                got[at, lanes] + local[8 * group + 2 * pair + c2]
            ).astype(BF16)


def activation(group, pre_act, cotan_in, out_held, cotan_pre):
    for pair in range(4):
        for c2 in range(2):
            for x in range(2):
                channel = 8 * group + 2 * pair + c2
                at = slice(c2 * 128, c2 * 128 + 128)
                lanes = slice(pair * 256 + x * 128, pair * 256 + x * 128 + 128)
                pre = pre_act[at, lanes]
                square = pre * pre
                inner = pre * (1.0 + GELU_A * square)
                tanh = jnp.tanh(inner.astype(F32) * GELU_K)
                half = 0.5 + 0.5 * tanh
                bell = (half * (GELU_K - GELU_K * tanh)).astype(BF16)
                half = half.astype(BF16)
                out_held[channel, x] = pre * half
                slope = half + bell * (pre * (1.0 + (3.0 * GELU_A) * square))
                cotan_pre[at, lanes] = slope * cotan_in[channel, x]


def gradient_modes(group, cotan_pre, ty_ref, cotan_rows, bias_sum, along_y):
    got = jnp.dot(ty_ref[...], cotan_pre[...], preferred_element_type=F32)
    for pair in range(4):
        store_along_y(along_y, got[:, pair * 256 : pair * 256 + 256], 8 * group + 2 * pair)
    for pair in range(4):
        for x in range(2):
            lanes = slice(pair * 256 + x * 128, pair * 256 + x * 128 + 128)
            wide = cotan_pre[:, lanes].astype(F32)
            sums = jnp.sum(wide.reshape(2, 16, 8, 128), axis=1)
            for c2 in range(2):
                bias_sum[8 * group + 2 * pair + c2, x * 8 : x * 8 + 8] = sums[c2]
            for y8 in range(16):
                block = jnp.concatenate(
                    [wide[c2 * 128 + 8 * y8 : c2 * 128 + 8 * y8 + 8] for c2 in range(2)], 0
                )
                lane = (y8 % 2) * 256 + x * 128
                cotan_rows[
                    y8 // 2, pl.ds(64 * group + 16 * pair, 16), lane : lane + 128
                ] = block.astype(BF16)


def sums_of(grad, bias_sum, scale_row):
    same = (
        lax.broadcasted_iota(jnp.int32, (512, 512), 0) % 8
        == lax.broadcasted_iota(jnp.int32, (512, 512), 1) % 8
    )
    per_c = jnp.sum(jnp.where(same, grad, 0.0).reshape(64, 8, 512), axis=1)
    pick = (
        lax.broadcasted_iota(jnp.int32, (512, 64), 0) // 8
        == lax.broadcasted_iota(jnp.int32, (512, 64), 1)
    ).astype(F32)
    d_local = jnp.dot(per_c, pick, preferred_element_type=F32, precision=lax.Precision.HIGHEST)
    d_local = d_local * (scale_row[0:1, 0:64] * GRAD_SCALE)
    lanes = jnp.sum(bias_sum[...], axis=1)
    d_bias = nt_dot(jnp.full((8, 128), GRAD_SCALE, F32), lanes, lax.Precision.HIGHEST)
    side = jnp.concatenate([d_bias, jnp.zeros((56, 64), F32)], 0)
    return jnp.concatenate([d_local, side], 1).reshape(8, 8, 128)


def weight_terms(gathered_g, shifted_modes, d_spec):
    columns = shifted_modes[...].T
    rows = gathered_g[...].astype(F32).reshape(64, 128)
    other = turned(rows, 1.0, -1.0)
    for k in range(16):
        total = jnp.zeros((64, 128), F32)
        for s in range(N_GRP):
            at = s * 16 + k
            total = total + columns[0:64, at : at + 1] * rows[at : at + 1]
            total = total + columns[64:128, at : at + 1] * other[at : at + 1]
        d_spec[k] = total


def layer_kernel(
    field, cotan, w_hbm, wl_hbm, direction_hbm, shift_hbm, bias_ref,
    ty_hbm, ztf_hbm, ztb_hbm, tx_hbm, txb_hbm, ey_hbm, ez_hbm,
    out_hbm, spec_hbm, sums_out,
    ty_ref, ztf_ref, ztb_ref, tx_ref, txb_ref, ey_ref, ez_ref, w_ref, wl_ref, direction_ref, shift_ref, scale_ref,
    held, cotan_in, out_held, field_rows, cotan_rows, local, along_y, along_z, kron, w_two,
    d_spec, pre_even, pre_odd, cotan_even, cotan_odd, bias_rows,
    slab_modes, pencil, mixed, gathered, back, landed, slab_g, pencil_g, mixed_g, gathered_g,
    all_modes, shifted_modes, scale_own, scale_all, bias_sum, own_sums, first, second, second_own, third,
    field_sems, cotan_sems, table_sems, out_sems, send_sems, recv_sems,
):
    me = lax.axis_index("slab")
    grp = lax.axis_index("grp")
    low = lax.rem(me, N_LOW)
    z = me // N_LOW
    barrier = pltpu.get_barrier_semaphore()
    small = [
        (ty_hbm, ty_ref), (ztf_hbm, ztf_ref), (direction_hbm, direction_ref), (wl_hbm, wl_ref),
        (w_hbm, w_ref), (tx_hbm, tx_ref), (txb_hbm, txb_ref), (ey_hbm, ey_ref),
        (ez_hbm, ez_ref), (ztb_hbm, ztb_ref), (shift_hbm, shift_ref),
    ]
    copies = [
        pltpu.make_async_copy(source, target, table_sems.at[at])
        for at, (source, target) in enumerate(small)
    ]
    for copy in copies[:2]:
        copy.start()
    fetch_field(field, held, field_sems)
    for copy in copies[2:]:
        copy.start()
    fetch_field(cotan, cotan_in, cotan_sems)
    greet(barrier, me, grp)
    for g_step in range(1, N_GRP):

        def tell(step, carry):
            pl.semaphore_signal(
                barrier,
                inc=1,
                device_id={
                    "grp": lax.rem(grp + g_step, N_GRP),
                    "slab": lax.rem(z + step, N_Z) * N_LOW + low,
                },
                device_id_type=MESH,
            )
            return carry

        lax.fori_loop(1, N_Z, tell, 0)

    copies[0].wait()

    for part in range(8):
        wait_field(field, held, field_sems, part)
        rows = jnp.concatenate(
            [
                jnp.concatenate([held[8 * part + 2 * pair + c2, x] for c2 in range(2)], 0)
                for pair in range(4)
                for x in range(2)
            ],
            1,
        )
        got = jnp.dot(ty_ref[...], rows, preferred_element_type=F32)
        for pair in range(4):
            store_along_y(along_y, got[:, pair * 256 : pair * 256 + 256], 8 * part + 2 * pair)
    copies[1].wait()
    along_z_modes(along_y, ztf_ref, slab_modes)
    copies[2].wait()
    copies[10].wait()
    scale_ref[...] = scale_rows(grp, direction_ref, shift_ref)
    scale_own[grp] = scale_ref[...]
    scale_all[grp] = scale_ref[...]
    pl.semaphore_wait(barrier, N_SLAB - 1 + N_GRP - 1 + (N_GRP - 1) * (N_Z - 1))
    send_all(slab_modes, pencil, send_sems.at[0], recv_sems.at[0], me)
    send_grp(scale_own, scale_all, send_sems.at[1], recv_sems.at[1], grp, False)

    copies[3].wait()
    copies[4].wait()
    for k in range(16):
        block = w_ref[k].astype(F32)
        w_two[k * 128 : k * 128 + 64, :] = w_ref[k]
        w_two[k * 128 + 64 : k * 128 + 128, :] = turned(block, -1.0, 1.0).astype(BF16)
    fill_kron(wl_ref, scale_ref[...], kron)
    for channel in range(CH):
        bias_rows[channel] = jnp.full((8, 128), bias_ref[channel], F32)

    def local_some(part, carry):
        local_step(part, held, kron, bias_rows, field_rows, local)
        return carry

    lax.fori_loop(0, 3, local_some, 0)
    pltpu.make_async_remote_copy(
        src_ref=scale_own.at[pl.ds(0, N_GRP - 1)],
        dst_ref=scale_all.at[pl.ds(0, N_GRP - 1)],
        send_sem=send_sems.at[1],
        recv_sem=recv_sems.at[1],
        device_id={"slab": me},
        device_id_type=MESH,
    ).wait()
    copies[5].wait()
    copies[6].wait()
    wait_blocks(slab_modes, pencil, send_sems.at[0], recv_sems.at[0], N_SLAB - 1, me)

    all_modes[...] = x_modes(pencil, tx_ref) * (1.0 / math.sqrt(NX * NY * NZ))
    own = all_modes[pl.ds(pl.multiple_of(16 * grp, 16), 16), :]
    shifted = jnp.concatenate([own * scale_all[s, 0:1, :] for s in range(N_GRP)], 0)
    shifted_modes[...] = shifted
    row_mode = lax.broadcasted_iota(jnp.int32, (64, 128), 0) % 16
    spread = jnp.concatenate(
        [jnp.where(row_mode == k, shifted, 0.0).astype(BF16) for k in range(16)], 1
    )
    mixed[...] = (
        jnp.dot(spread, w_two[...], preferred_element_type=F32).astype(BF16).reshape(4, 16, 128)
    )
    send_grp(mixed, gathered, send_sems.at[2], recv_sems.at[2], grp, True)
    gathered[pl.ds(grp, 1)] = mixed[pl.ds(grp, 1)]
    lax.fori_loop(3, 5, local_some, 0)
    wait_blocks(mixed, gathered, send_sems.at[2], recv_sems.at[2], N_GRP - 1, me)
    full = gathered[...].reshape(64, 128)
    both = jnp.concatenate([full, turned(full.astype(F32), -1.0, 1.0).astype(BF16)], 0)
    back[...] = (
        jnp.dot(txb_ref[...], both, preferred_element_type=F32).reshape(64, 8, 128).astype(BF16)
    )
    send_all(back, landed, send_sems.at[3], recv_sems.at[3], me)
    lax.fori_loop(5, 8, local_some, 0)
    for copy in copies[7:10]:
        copy.wait()
    for part in range(8):
        wait_field(cotan, cotan_in, cotan_sems, part)
    wait_blocks(back, landed, send_sems.at[3], recv_sems.at[3], N_SLAB - 1, me)

    fill_along_z(landed, ez_ref, along_z)

    slots = ((pre_even, cotan_even), (pre_odd, cotan_odd))
    for step in range(10):
        if step < 8:
            synthesis(step, along_z, local, ey_ref, slots[step % 2][0])
        if 0 < step < 9:
            pre_act, cotan_pre = slots[(step - 1) % 2]
            activation(step - 1, pre_act, cotan_in, out_held, cotan_pre)
            rows = pl.ds(8 * (step - 1), 8)
            pltpu.make_async_copy(
                out_held.at[rows], out_hbm.at[rows], out_sems.at[step - 1]
            ).start()
        if step > 1:
            gradient_modes(
                step - 2, slots[step % 2][1], ty_ref, cotan_rows, bias_sum, along_y
            )

    grad = jnp.zeros((512, 512), F32)
    for part in range(8):
        grad = grad + nt_dot(cotan_rows[part], field_rows[part])
    own_sums[...] = sums_of(grad, bias_sum, scale_ref[...])

    def scatter(step, carry):
        other = lax.rem(low + step, N_LOW)
        pltpu.make_async_remote_copy(
            src_ref=own_sums.at[other],
            dst_ref=first.at[low],
            send_sem=send_sems.at[4],
            recv_sem=recv_sems.at[4],
            device_id={"slab": z * N_LOW + other},
            device_id_type=MESH,
        ).start()
        return carry

    lax.fori_loop(1, N_LOW, scatter, 0)
    first[pl.ds(low, 1)] = own_sums[pl.ds(low, 1)]
    along_z_modes(along_y, ztb_ref, slab_g)
    send_all(slab_g, pencil_g, send_sems.at[5], recv_sems.at[5], me)
    wait_blocks(own_sums, first, send_sems.at[4], recv_sems.at[4], N_LOW - 1, me)
    part_sum = jnp.sum(first[...], axis=0, keepdims=True)
    mine = grp * N_Z + z
    second[pl.ds(mine, 1)] = part_sum
    second_own[...] = part_sum
    for g_step in (2, 1, 3, 0):

        def spread_sum(step, carry):
            pltpu.make_async_remote_copy(
                src_ref=second_own.at[0],
                dst_ref=second.at[mine],
                send_sem=send_sems.at[6],
                recv_sem=recv_sems.at[6],
                device_id={
                    "grp": lax.rem(grp + g_step, N_GRP),
                    "slab": lax.rem(z + step, N_Z) * N_LOW + low,
                },
                device_id_type=MESH,
            ).start()
            return carry

        lax.fori_loop(1 if g_step == 0 else 0, N_Z, spread_sum, 0)
    wait_blocks(slab_g, pencil_g, send_sems.at[5], recv_sems.at[5], N_SLAB - 1, me)
    mixed_g[...] = x_modes(pencil_g, tx_ref).astype(BF16).reshape(4, 16, 128)
    send_grp(mixed_g, gathered_g, send_sems.at[7], recv_sems.at[7], grp, True)
    gathered_g[pl.ds(grp, 1)] = mixed_g[pl.ds(grp, 1)]
    wait_blocks(second, second, send_sems.at[6], recv_sems.at[6], N_GRP * N_Z - 1, me)
    third[pl.ds(low, 1)] = jnp.sum(second[...], axis=0, keepdims=True)

    def collect(step, carry):
        pltpu.make_async_remote_copy(
            src_ref=third.at[low],
            dst_ref=third.at[low],
            send_sem=send_sems.at[8],
            recv_sem=recv_sems.at[8],
            device_id={"slab": z * N_LOW + lax.rem(low + step, N_LOW)},
            device_id_type=MESH,
        ).start()
        return carry

    lax.fori_loop(1, N_LOW, collect, 0)
    wait_blocks(mixed_g, gathered_g, send_sems.at[7], recv_sems.at[7], N_GRP - 1, me)
    weight_terms(gathered_g, shifted_modes, d_spec)
    spec_copy = pltpu.make_async_copy(d_spec, spec_hbm, out_sems.at[8])
    spec_copy.start()
    for part in range(8):
        rows = pl.ds(8 * part, 8)
        pltpu.make_async_copy(out_held.at[rows], out_hbm.at[rows], out_sems.at[part]).wait()
    wait_blocks(third, third, send_sems.at[8], recv_sems.at[8], N_LOW - 1, me)
    sums_out[...] = third[...]
    spec_copy.wait()


def layer_call(field, cotangent, w_spec, w_local, direction, shift, bias):
    vmem = pl.BlockSpec(memory_space=pltpu.VMEM)
    hbm = pl.BlockSpec(memory_space=pl.ANY)
    tables = (
        table_ty(), table_zt(False), table_zt(True), table_tx(),
        np.ascontiguousarray(table_tx().T), table_ey(), table_ez(),
    )
    cells = (64, 2, 128, 128)
    blocks = pltpu.VMEM((64, 8, 128), BF16)
    quads = pltpu.VMEM((4, 16, 128), BF16)
    return pl.pallas_call(
        layer_kernel,
        out_shape=(
            jax.ShapeDtypeStruct(cells, BF16),
            jax.ShapeDtypeStruct((16, 64, 128), F32),
            jax.ShapeDtypeStruct((8, 8, 128), F32),
        ),
        in_specs=[hbm] * 6 + [pl.BlockSpec(memory_space=pltpu.SMEM)] + [hbm] * 7,
        out_specs=(hbm, hbm, vmem),
        scratch_shapes=[pltpu.VMEM(table.shape, BF16) for table in tables]
        + [
            pltpu.VMEM((16, 64, 128), BF16),
            pltpu.VMEM((64, 64), BF16),
            pltpu.VMEM((64, BITS), jnp.int32),
            pltpu.VMEM((1, 64), jnp.int32),
            pltpu.VMEM((8, 128), F32),
            pltpu.VMEM(cells, BF16),
            pltpu.VMEM(cells, BF16),
            pltpu.VMEM(cells, BF16),
            pltpu.VMEM((8, 512, 512), BF16),
            pltpu.VMEM((8, 512, 512), BF16),
            pltpu.VMEM((64, 128, 256), F32),
            pltpu.VMEM((4096, 128), F32),
            pltpu.VMEM((4096, 128), F32),
            pltpu.VMEM((512, 512), BF16),
            pltpu.VMEM((2048, 128), BF16),
            pltpu.VMEM((16, 64, 128), F32),
            pltpu.VMEM((256, 1024), BF16),
            pltpu.VMEM((256, 1024), BF16),
            pltpu.VMEM((256, 1024), BF16),
            pltpu.VMEM((256, 1024), BF16),
            pltpu.VMEM((64, 8, 128), F32),
            blocks, blocks, quads, quads, blocks, blocks, blocks, blocks, quads, quads,
            pltpu.VMEM((64, 128), F32),
            pltpu.VMEM((64, 128), F32),
            pltpu.VMEM((4, 8, 128), F32),
            pltpu.VMEM((4, 8, 128), F32),
            pltpu.VMEM((64, 16, 128), F32),
            pltpu.VMEM((8, 8, 128), F32),
            pltpu.VMEM((8, 8, 128), F32),
            pltpu.VMEM((32, 8, 128), F32),
            pltpu.VMEM((1, 8, 128), F32),
            pltpu.VMEM((8, 8, 128), F32),
            pltpu.SemaphoreType.DMA((8,)),
            pltpu.SemaphoreType.DMA((8,)),
            pltpu.SemaphoreType.DMA((11,)),
            pltpu.SemaphoreType.DMA((9,)),
            pltpu.SemaphoreType.DMA((9,)),
            pltpu.SemaphoreType.DMA((9,)),
        ],
        compiler_params=pltpu.CompilerParams(
            collective_id=0, has_side_effects=True, vmem_limit_bytes=58 * MIB
        ),
    )(field, cotangent, w_spec, w_local, direction, shift, bias, *tables)


def results_kernel(
    out_hbm, spec_hbm, sums_hbm,
    output, spec_out, d_local, d_bias,
    held, spec_held, sums_ref, in_sems, out_sems,
):
    moves = []
    for part in range(8):
        rows = pl.ds(8 * part, 8)
        moves.append((out_hbm.at[rows], held.at[rows], output.at[rows]))
    for part in range(2):
        rows = pl.ds(8 * part, 8)
        moves.append((spec_hbm.at[rows], spec_held.at[rows], spec_out.at[rows]))
    ins = [
        pltpu.make_async_copy(source, middle, in_sems.at[at])
        for at, (source, middle, _) in enumerate(moves)
    ]
    outs = [
        pltpu.make_async_copy(middle, target, out_sems.at[at])
        for at, (_, middle, target) in enumerate(moves)
    ]
    sums_copy = pltpu.make_async_copy(sums_hbm, sums_ref, in_sems.at[10])
    for copy in ins:
        copy.start()
    sums_copy.start()
    for before, after in zip(ins, outs):
        before.wait()
        after.start()
    sums_copy.wait()
    sums = sums_ref[...].reshape(64, 128)
    d_local[...] = sums[:, 0:64]
    d_bias[...] = sums[0:1, 64:128]
    for copy in outs:
        copy.wait()


def results_call(out, d_spec, sums):
    vmem = pl.BlockSpec(memory_space=pltpu.VMEM)
    hbm = pl.BlockSpec(memory_space=pl.ANY)
    return pl.pallas_call(
        results_kernel,
        out_shape=(
            jax.ShapeDtypeStruct(out.shape, BF16),
            jax.ShapeDtypeStruct(d_spec.shape, F32),
            jax.ShapeDtypeStruct((64, 64), F32),
            jax.ShapeDtypeStruct((1, 64), F32),
        ),
        in_specs=[hbm] * 3,
        out_specs=(hbm, hbm, vmem, vmem),
        scratch_shapes=[
            pltpu.VMEM(out.shape, BF16),
            pltpu.VMEM(d_spec.shape, F32),
            pltpu.VMEM((8, 8, 128), F32),
            pltpu.SemaphoreType.DMA((11,)),
            pltpu.SemaphoreType.DMA((10,)),
        ],
        compiler_params=pltpu.CompilerParams(vmem_limit_bytes=58 * MIB),
    )(out, d_spec, sums)


def shards(base_field, cotangent, w_spec, w_local, bias, direction, shift):
    out, d_spec, sums = layer_call(
        base_field, cotangent[0], w_spec.reshape(16, 64, 128), w_local, direction, shift, bias
    )
    output, d_spec, d_local, d_bias = results_call(out, d_spec, sums)
    return (output[None], d_spec.reshape(4, 4, 64, 128), d_local, d_bias.reshape(64))


def solution(mesh):
    return jax.shard_map(
        shards,
        mesh=mesh,
        in_specs=(
            P(None, "slab", None, None),
            P("grp", None, "slab", None, None),
            P("grp", "slab", None, None),
            P(),
            P(),
            P(),
            P("grp", None),
        ),
        out_specs=(P("grp", None, "slab", None, None), P("grp", "slab", None, None), P(), P()),
        check_vma=False,
    )
```

```python
import math

import jax
import jax.numpy as jnp
import ml_dtypes
import numpy as np
from jax import lax
from jax.experimental import pallas as pl
from jax.experimental.pallas import tpu as pltpu
from jax.sharding import PartitionSpec as P

CH = 64
NX = 128
NY = 128
NZ = 128
MODES = 16
BITS = 30
N_GRP = 4
N_SLAB = 64
N_LOW = 8
N_Z = 8
MESH = pl.DeviceIdType.MESH
F32 = jnp.float32
BF16 = jnp.bfloat16
MIB = 1024 * 1024
GELU_K = math.sqrt(2.0 / math.pi)
GELU_A = 0.044715
GRAD_SCALE = 1.0 / math.sqrt(N_GRP * NX * NY * NZ)


def waves(length, half):
    ids = np.arange(MODES)
    if not half:
        ids = np.where(ids < MODES // 2, ids, length - MODES + ids)
    angles = 2.0 * math.pi / length * (ids[:, None] * np.arange(length)[None, :] % length)
    return np.cos(angles), np.sin(angles)


def as_bf16(table):
    return np.asarray(table, np.float32).astype(ml_dtypes.bfloat16)


def table_ty():
    cos_y, sin_y = waves(NY, False)
    out = np.zeros((2, 2, MODES, 2, NY))
    for c2 in range(2):
        out[0, c2, :, c2] = cos_y
        out[1, c2, :, c2] = sin_y
    return as_bf16(out.reshape(64, 256))


def weights_z(backward):
    return np.where(np.arange(MODES) == 0, 1.0, 2.0 if backward else 1.0)[:, None]


def table_zt(backward):
    cos_z, sin_z = waves(NZ, True)
    weight = weights_z(backward)
    if backward:
        weight = weight * GRAD_SCALE
    cos_z = (weight * cos_z).reshape(4, 4, NZ)
    sin_z = (weight * sin_z).reshape(4, 4, NZ)
    out = np.zeros((2, 4, 2, 4, 2, 2, NZ))
    for x in range(2):
        out[0, :, x, :, 0, x] = cos_z
        out[0, :, x, :, 1, x] = -sin_z
        out[1, :, x, :, 0, x] = -sin_z
        out[1, :, x, :, 1, x] = -cos_z
    return as_bf16(out.reshape(64, 512))


def table_tx():
    cos_x, sin_x = waves(NX, False)
    out = np.zeros((2, MODES, 4, NX, 4))
    for m in range(4):
        out[0, :, m, :, m] = cos_x
        out[1, :, m, :, m] = sin_x
    return as_bf16(out.reshape(128, 512))


def table_ey():
    cos_y, sin_y = waves(NY, False)
    out = np.zeros((2, NY, 2, 2, MODES))
    for c2 in range(2):
        out[c2, :, c2, 0] = cos_y.T
        out[c2, :, c2, 1] = -sin_y.T
    return as_bf16(out.reshape(256, 64))


def table_ez():
    cos_z, sin_z = waves(NZ, True)
    weight = weights_z(True) / math.sqrt(MODES**3)
    cos_z = (weight * cos_z).reshape(4, 4, NZ)
    sin_z = (weight * sin_z).reshape(4, 4, NZ)
    out = np.zeros((2, 4, 2, 4, 2, 2, NZ))
    for x in range(2):
        out[0, :, x, :, 0, x] = cos_z
        out[1, :, x, :, 0, x] = -sin_z
        out[0, :, x, :, 1, x] = sin_z
        out[1, :, x, :, 1, x] = cos_z
    return as_bf16(out.reshape(64, 512))


def lane_sign(rows, first, second):
    lane = lax.broadcasted_iota(jnp.int32, (rows, 128), 1)
    return jnp.where(lane < 64, first, second).astype(F32)


def turned(rows, first, second):
    return pltpu.roll(rows, 64, 1) * lane_sign(rows.shape[0], first, second)


def nt_dot(left, right, precision=None):
    return lax.dot_general(
        left, right, (((1,), (1,)), ((), ())), preferred_element_type=F32, precision=precision
    )


def fetch_field(field, held, sems):
    for part in range(8):
        rows = pl.ds(8 * part, 8)
        pltpu.make_async_copy(field.at[rows], held.at[rows], sems.at[part]).start()


def wait_field(field, held, sems, part):
    rows = pl.ds(8 * part, 8)
    pltpu.make_async_copy(field.at[rows], held.at[rows], sems.at[part]).wait()


def store_along_y(along_y, got, first):
    for cs in range(2):
        for c2 in range(2):
            at = cs * 32 + c2 * 16
            for x in range(2):
                start = (2 * cs + x) * 1024 + first + c2
                along_y[pl.ds(start, 16, stride=64), :] = got[
                    at : at + 16, x * 128 : x * 128 + 128
                ]


def along_z_half(half, along_y, zt_ref, modes_z):
    for part in range(2):
        rows = jnp.concatenate(
            [
                jnp.concatenate(
                    [
                        along_y[
                            cs_x * 1024 + jy * 64 + half * 32 : cs_x * 1024 + jy * 64 + half * 32 + 32,
                            :,
                        ]
                        for jy in range(part * 8, part * 8 + 8)
                    ],
                    0,
                ).astype(BF16)
                for cs_x in range(4)
            ],
            1,
        )
        modes_z[half, part] = nt_dot(zt_ref[...], rows)


def join_halves(modes_z, slab_modes):
    for jy in range(16):
        lanes = slice((jy % 8) * 32, (jy % 8) * 32 + 32)
        block = jnp.concatenate(
            [
                modes_z[half, jy // 8, re * 32 : re * 32 + 32, lanes]
                for re in range(2)
                for half in range(2)
            ],
            1,
        )
        slab_modes[jy * 4 : jy * 4 + 4] = block.reshape(4, 8, 128).astype(BF16)


def greet(barrier, me, grp):
    def tell(step, carry):
        pl.semaphore_signal(
            barrier, inc=1, device_id={"slab": lax.rem(me + step, N_SLAB)}, device_id_type=MESH
        )
        return carry

    lax.fori_loop(1, N_SLAB, tell, 0)
    for step in range(1, N_GRP):
        pl.semaphore_signal(
            barrier, inc=1, device_id={"grp": lax.rem(grp + step, N_GRP)}, device_id_type=MESH
        )


def send_all(source, target, send_sem, recv_sem, me):
    low = lax.rem(me, N_LOW)
    z = me // N_LOW
    for dz in (4, 3, 5, 2, 6, 1, 7, 0):

        def go(step, carry):
            other = lax.rem(z + dz, N_Z) * N_LOW + lax.rem(low + step, N_LOW)
            pltpu.make_async_remote_copy(
                src_ref=source.at[other],
                dst_ref=target.at[me],
                send_sem=send_sem,
                recv_sem=recv_sem,
                device_id={"slab": other},
                device_id_type=MESH,
            ).start()
            return carry

        lax.fori_loop(1 if dz == 0 else 0, N_LOW, go, 0)
    target[pl.ds(me, 1)] = source[pl.ds(me, 1)]


def wait_blocks(source, target, send_sem, recv_sem, count, me):
    pltpu.make_async_remote_copy(
        src_ref=source.at[pl.ds(0, count)],
        dst_ref=target.at[pl.ds(0, count)],
        send_sem=send_sem,
        recv_sem=recv_sem,
        device_id={"slab": me},
        device_id_type=MESH,
    ).wait()


def send_grp(source, target, send_sem, recv_sem, grp, by_target):
    for step in range(1, N_GRP):
        other = lax.rem(grp + step, N_GRP)
        pltpu.make_async_remote_copy(
            src_ref=source.at[other] if by_target else source.at[grp],
            dst_ref=target.at[grp],
            send_sem=send_sem,
            recv_sem=recv_sem,
            device_id={"grp": other},
            device_id_type=MESH,
        ).start()


def x_modes(pencil, tx_ref):
    rows = pencil[...].astype(F32).reshape(512, 128).astype(BF16)
    both = jnp.dot(tx_ref[...], rows, preferred_element_type=F32)
    return both[:64] + turned(both[64:], 1.0, -1.0)


def local_step(part, held, kron, bias_rows, field_rows, local):
    y_at = pl.multiple_of(16 * part, 16)
    halves = [held[:, x, pl.ds(y_at, 16), :].astype(F32) for x in range(2)]
    for half in range(2):
        rows = jnp.concatenate(
            [block[:, 8 * half : 8 * half + 8].reshape(512, 128) for block in halves], 1
        ).astype(BF16)
        field_rows[part, :, half * 256 : half * 256 + 256] = rows
        got = jnp.dot(kron[...], rows, preferred_element_type=F32)
        added = bias_rows[...]
        local[:, pl.ds(pl.multiple_of(y_at + 8 * half, 8), 8), :] = got.reshape(
            64, 8, 256
        ) + jnp.concatenate([added, added], 2)


def scale_rows(grp, direction_ref, shift_ref):
    number = grp + 1
    gray_code = number ^ (number >> 1)
    bits = shift_ref[...]
    for bit_pos in range(N_GRP.bit_length()):
        bits = bits ^ (direction_ref[bit_pos : bit_pos + 1, :] * ((gray_code >> bit_pos) & 1))
    scale = 0.5 + bits.astype(F32) * 2.0 ** (-BITS)
    return jnp.broadcast_to(jnp.concatenate([scale, scale], 1), (8, 128))


def fill_kron(wl_ref, scale_row, kron):
    local = (wl_ref[...].astype(F32) * scale_row[0:1, 0:64]).astype(BF16)
    pick = (
        lax.broadcasted_iota(jnp.int32, (64, 512), 0)
        == lax.broadcasted_iota(jnp.int32, (64, 512), 1) // 8
    )
    wide = jnp.dot(local, pick.astype(F32).astype(BF16), preferred_element_type=F32).astype(BF16)
    same = (
        lax.broadcasted_iota(jnp.int32, (64, 512), 0) % 8
        == lax.broadcasted_iota(jnp.int32, (64, 512), 1) % 8
    )
    row_ids = lax.broadcasted_iota(jnp.int32, (64, 64), 0) // 8
    col_ids = lax.broadcasted_iota(jnp.int32, (64, 64), 1)
    for octet in range(8):
        rows_of = (row_ids + 8 * octet == col_ids).astype(F32).astype(BF16)
        tall = jnp.dot(rows_of, wide, preferred_element_type=F32)
        kron[octet * 64 : octet * 64 + 64, :] = jnp.where(same, tall, 0.0).astype(BF16)


def fill_along_z(landed, ez_ref, along_z):
    for quarter in range(4):
        rows = landed[quarter * 16 : quarter * 16 + 16].astype(F32).reshape(128, 128)
        turn = rows.T
        per_c = jnp.concatenate(
            [
                jnp.concatenate(
                    [turn[0:64, jy * 32 : jy * 32 + 32], turn[64:128, jy * 32 : jy * 32 + 32]], 1
                )
                for jy in range(4)
            ],
            0,
        ).astype(BF16)
        got = jnp.dot(per_c, ez_ref[...], preferred_element_type=F32)
        for jy in range(4):
            for cs in range(2):
                for x in range(2):
                    start = x * 2048 + cs * 16 + quarter * 4 + jy
                    lane = cs * 256 + x * 128
                    along_z[pl.ds(start, 64, stride=32), :] = got[
                        jy * 64 : jy * 64 + 64, lane : lane + 128
                    ]


def synthesis(group, along_z, local, ey_ref, pre_act):
    rows = jnp.concatenate(
        [
            along_z[pl.ds(x * 2048 + 256 * group + 64 * pair, 64), :].astype(BF16)
            for pair in range(4)
            for x in range(2)
        ],
        1,
    )
    got = jnp.dot(ey_ref[...], rows, preferred_element_type=F32)
    for pair in range(4):
        for c2 in range(2):
            at = slice(c2 * 128, c2 * 128 + 128)
            lanes = slice(pair * 256, pair * 256 + 256)
            pre_act[at, lanes] = (
                got[at, lanes] + local[8 * group + 2 * pair + c2]
            ).astype(BF16)


def activation(group, pre_act, cotan_in, out_held, cotan_pre):
    for pair in range(4):
        for c2 in range(2):
            for x in range(2):
                channel = 8 * group + 2 * pair + c2
                at = slice(c2 * 128, c2 * 128 + 128)
                lanes = slice(pair * 256 + x * 128, pair * 256 + x * 128 + 128)
                pre = pre_act[at, lanes]
                square = pre * pre
                inner = pre * (1.0 + GELU_A * square)
                tanh = jnp.tanh(inner.astype(F32) * GELU_K)
                half = 0.5 + 0.5 * tanh
                bell = (half * (GELU_K - GELU_K * tanh)).astype(BF16)
                half = half.astype(BF16)
                out_held[channel, x] = pre * half
                slope = half + bell * (pre * (1.0 + (3.0 * GELU_A) * square))
                cotan_pre[at, lanes] = slope * cotan_in[channel, x]


def gradient_modes(group, cotan_pre, ty_ref, cotan_rows, bias_sum, along_y):
    got = jnp.dot(ty_ref[...], cotan_pre[...], preferred_element_type=F32)
    for pair in range(4):
        store_along_y(along_y, got[:, pair * 256 : pair * 256 + 256], 8 * group + 2 * pair)
    for pair in range(4):
        for x in range(2):
            lanes = slice(pair * 256 + x * 128, pair * 256 + x * 128 + 128)
            wide = cotan_pre[:, lanes].astype(F32)
            sums = jnp.sum(wide.reshape(2, 16, 8, 128), axis=1)
            for c2 in range(2):
                bias_sum[8 * group + 2 * pair + c2, x * 8 : x * 8 + 8] = sums[c2]
            for y8 in range(16):
                block = jnp.concatenate(
                    [wide[c2 * 128 + 8 * y8 : c2 * 128 + 8 * y8 + 8] for c2 in range(2)], 0
                )
                lane = (y8 % 2) * 256 + x * 128
                cotan_rows[
                    y8 // 2, pl.ds(64 * group + 16 * pair, 16), lane : lane + 128
                ] = block.astype(BF16)


def local_grad(grad):
    same = (
        lax.broadcasted_iota(jnp.int32, (256, 512), 0) % 8
        == lax.broadcasted_iota(jnp.int32, (256, 512), 1) % 8
    )
    kept = jnp.where(same, grad, 0.0)
    high = kept.astype(BF16)
    low = (kept - high.astype(F32)).astype(BF16)
    pick = (
        lax.broadcasted_iota(jnp.int32, (512, 64), 0) // 8
        == lax.broadcasted_iota(jnp.int32, (512, 64), 1)
    )
    pick = pick.astype(F32).astype(BF16)
    got = jnp.dot(high, pick, preferred_element_type=F32) + jnp.dot(
        low, pick, preferred_element_type=F32
    )
    return jnp.sum(got.reshape(32, 8, 64), axis=1)


def weight_terms(gathered_g, shifted_modes, d_spec):
    columns = shifted_modes[...].T
    rows = gathered_g[...].astype(F32).reshape(64, 128)
    other = turned(rows, 1.0, -1.0)
    for k in range(16):
        total = jnp.zeros((64, 128), F32)
        for s in range(N_GRP):
            at = s * 16 + k
            total = total + columns[0:64, at : at + 1] * rows[at : at + 1]
            total = total + columns[64:128, at : at + 1] * other[at : at + 1]
        d_spec[k] = total


def layer_kernel(
    field, cotan, w_hbm, wl_hbm, direction_hbm, shift_hbm, bias_ref,
    ty_hbm, ztf_hbm, ztb_hbm, tx_hbm, txb_hbm, ey_hbm, ez_hbm,
    out_hbm, spec_hbm, sums_out,
    ty_ref, ztf_ref, ztb_ref, tx_ref, txb_ref, ey_ref, ez_ref, w_ref, wl_ref, direction_ref, shift_ref, scale_ref,
    held, cotan_in, out_held, field_rows, cotan_rows, local, along_y, along_z, kron, w_two,
    d_spec, modes_z, grad, pre_even, pre_odd, cotan_even, cotan_odd, bias_rows,
    slab_modes, pencil, mixed, gathered, back, landed, slab_g, pencil_g, mixed_g, gathered_g,
    all_modes, shifted_modes, scale_own, scale_all, bias_sum, own_sums, first, second, second_own, third,
    field_sems, cotan_sems, table_sems, out_sems, send_sems, recv_sems,
):
    me = lax.axis_index("slab")
    grp = lax.axis_index("grp")
    low = lax.rem(me, N_LOW)
    z = me // N_LOW
    barrier = pltpu.get_barrier_semaphore()
    small = [
        (ty_hbm, ty_ref), (ztf_hbm, ztf_ref), (direction_hbm, direction_ref), (wl_hbm, wl_ref),
        (w_hbm, w_ref), (tx_hbm, tx_ref), (txb_hbm, txb_ref), (ey_hbm, ey_ref),
        (ez_hbm, ez_ref), (ztb_hbm, ztb_ref), (shift_hbm, shift_ref),
    ]
    copies = [
        pltpu.make_async_copy(source, target, table_sems.at[at])
        for at, (source, target) in enumerate(small)
    ]
    for copy in copies[:2]:
        copy.start()
    fetch_field(field, held, field_sems)
    for copy in copies[2:]:
        copy.start()
    fetch_field(cotan, cotan_in, cotan_sems)
    greet(barrier, me, grp)
    for g_step in range(1, N_GRP):

        def tell(step, carry):
            pl.semaphore_signal(
                barrier,
                inc=1,
                device_id={
                    "grp": lax.rem(grp + g_step, N_GRP),
                    "slab": lax.rem(z + step, N_Z) * N_LOW + low,
                },
                device_id_type=MESH,
            )
            return carry

        lax.fori_loop(1, N_Z, tell, 0)

    copies[0].wait()

    for part in range(8):
        wait_field(field, held, field_sems, part)
        rows = jnp.concatenate(
            [
                jnp.concatenate([held[8 * part + 2 * pair + c2, x] for c2 in range(2)], 0)
                for pair in range(4)
                for x in range(2)
            ],
            1,
        )
        got = jnp.dot(ty_ref[...], rows, preferred_element_type=F32)
        for pair in range(4):
            store_along_y(along_y, got[:, pair * 256 : pair * 256 + 256], 8 * part + 2 * pair)
        if part == 3:
            copies[1].wait()
            along_z_half(0, along_y, ztf_ref, modes_z)
    along_z_half(1, along_y, ztf_ref, modes_z)
    join_halves(modes_z, slab_modes)
    copies[2].wait()
    copies[10].wait()
    scale_ref[...] = scale_rows(grp, direction_ref, shift_ref)
    scale_own[grp] = scale_ref[...]
    scale_all[grp] = scale_ref[...]
    pl.semaphore_wait(barrier, N_SLAB - 1 + N_GRP - 1 + (N_GRP - 1) * (N_Z - 1))
    send_all(slab_modes, pencil, send_sems.at[0], recv_sems.at[0], me)
    send_grp(scale_own, scale_all, send_sems.at[1], recv_sems.at[1], grp, False)

    copies[3].wait()
    copies[4].wait()
    for k in range(16):
        block = w_ref[k].astype(F32)
        w_two[k * 128 : k * 128 + 64, :] = w_ref[k]
        w_two[k * 128 + 64 : k * 128 + 128, :] = turned(block, -1.0, 1.0).astype(BF16)
    fill_kron(wl_ref, scale_ref[...], kron)
    for channel in range(CH):
        bias_rows[channel] = jnp.full((8, 128), bias_ref[channel], F32)

    def local_some(part, carry):
        local_step(part, held, kron, bias_rows, field_rows, local)
        return carry

    lax.fori_loop(0, 3, local_some, 0)
    pltpu.make_async_remote_copy(
        src_ref=scale_own.at[pl.ds(0, N_GRP - 1)],
        dst_ref=scale_all.at[pl.ds(0, N_GRP - 1)],
        send_sem=send_sems.at[1],
        recv_sem=recv_sems.at[1],
        device_id={"slab": me},
        device_id_type=MESH,
    ).wait()
    copies[5].wait()
    copies[6].wait()
    wait_blocks(slab_modes, pencil, send_sems.at[0], recv_sems.at[0], N_SLAB - 1, me)

    all_modes[...] = x_modes(pencil, tx_ref) * (1.0 / math.sqrt(NX * NY * NZ))
    own = all_modes[pl.ds(pl.multiple_of(16 * grp, 16), 16), :]
    shifted = jnp.concatenate([own * scale_all[s, 0:1, :] for s in range(N_GRP)], 0)
    shifted_modes[...] = shifted
    row_mode = lax.broadcasted_iota(jnp.int32, (64, 128), 0) % 16
    spread = jnp.concatenate(
        [jnp.where(row_mode == k, shifted, 0.0).astype(BF16) for k in range(16)], 1
    )
    mixed[...] = (
        jnp.dot(spread, w_two[...], preferred_element_type=F32).astype(BF16).reshape(4, 16, 128)
    )
    send_grp(mixed, gathered, send_sems.at[2], recv_sems.at[2], grp, True)
    gathered[pl.ds(grp, 1)] = mixed[pl.ds(grp, 1)]
    lax.fori_loop(3, 5, local_some, 0)
    wait_blocks(mixed, gathered, send_sems.at[2], recv_sems.at[2], N_GRP - 1, me)
    full = gathered[...].reshape(64, 128)
    both = jnp.concatenate([full, turned(full.astype(F32), -1.0, 1.0).astype(BF16)], 0)
    back[...] = (
        jnp.dot(txb_ref[...], both, preferred_element_type=F32).reshape(64, 8, 128).astype(BF16)
    )
    send_all(back, landed, send_sems.at[3], recv_sems.at[3], me)
    lax.fori_loop(5, 8, local_some, 0)
    for copy in copies[7:10]:
        copy.wait()
    for part in range(8):
        wait_field(cotan, cotan_in, cotan_sems, part)
    wait_blocks(back, landed, send_sems.at[3], recv_sems.at[3], N_SLAB - 1, me)

    fill_along_z(landed, ez_ref, along_z)

    slots = ((pre_even, cotan_even), (pre_odd, cotan_odd))
    for step in range(10):
        if step < 8:
            synthesis(step, along_z, local, ey_ref, slots[step % 2][0])
        if 0 < step < 9:
            pre_act, cotan_pre = slots[(step - 1) % 2]
            activation(step - 1, pre_act, cotan_in, out_held, cotan_pre)
            rows = pl.ds(8 * (step - 1), 8)
            pltpu.make_async_copy(
                out_held.at[rows], out_hbm.at[rows], out_sems.at[step - 1]
            ).start()
        if step > 1:
            gradient_modes(
                step - 2, slots[step % 2][1], ty_ref, cotan_rows, bias_sum, along_y
            )
        if step == 5:
            along_z_half(0, along_y, ztb_ref, modes_z)
            grad[...] = jnp.zeros_like(grad)
        if step > 5:
            for part in (2 * step - 12, 2 * step - 11):
                grad[...] += nt_dot(cotan_rows[part, 0:256, :], field_rows[part])

    d_top = local_grad(grad[...])
    bottom = jnp.zeros((256, 512), F32)
    for part in range(8):
        bottom = bottom + nt_dot(cotan_rows[part, 256:512, :], field_rows[part])
    d_local = jnp.concatenate([d_top, local_grad(bottom)], 0)
    d_local = d_local * (scale_ref[0:1, 0:64] * GRAD_SCALE)
    lanes = jnp.sum(bias_sum[...], axis=1)
    d_bias = nt_dot(jnp.full((8, 128), GRAD_SCALE, F32), lanes, lax.Precision.HIGHEST)
    side = jnp.concatenate([d_bias, jnp.zeros((56, 64), F32)], 0)
    own_sums[...] = jnp.concatenate([d_local, side], 1).reshape(8, 8, 128)

    def scatter(step, carry):
        other = lax.rem(low + step, N_LOW)
        pltpu.make_async_remote_copy(
            src_ref=own_sums.at[other],
            dst_ref=first.at[low],
            send_sem=send_sems.at[4],
            recv_sem=recv_sems.at[4],
            device_id={"slab": z * N_LOW + other},
            device_id_type=MESH,
        ).start()
        return carry

    lax.fori_loop(1, N_LOW, scatter, 0)
    first[pl.ds(low, 1)] = own_sums[pl.ds(low, 1)]
    along_z_half(1, along_y, ztb_ref, modes_z)
    join_halves(modes_z, slab_g)
    send_all(slab_g, pencil_g, send_sems.at[5], recv_sems.at[5], me)
    wait_blocks(own_sums, first, send_sems.at[4], recv_sems.at[4], N_LOW - 1, me)
    part_sum = jnp.sum(first[...], axis=0, keepdims=True)
    mine = grp * N_Z + z
    second[pl.ds(mine, 1)] = part_sum
    second_own[...] = part_sum
    for g_step in (2, 1, 3, 0):

        def spread_sum(step, carry):
            pltpu.make_async_remote_copy(
                src_ref=second_own.at[0],
                dst_ref=second.at[mine],
                send_sem=send_sems.at[6],
                recv_sem=recv_sems.at[6],
                device_id={
                    "grp": lax.rem(grp + g_step, N_GRP),
                    "slab": lax.rem(z + step, N_Z) * N_LOW + low,
                },
                device_id_type=MESH,
            ).start()
            return carry

        lax.fori_loop(1 if g_step == 0 else 0, N_Z, spread_sum, 0)
    wait_blocks(slab_g, pencil_g, send_sems.at[5], recv_sems.at[5], N_SLAB - 1, me)
    mixed_g[...] = x_modes(pencil_g, tx_ref).astype(BF16).reshape(4, 16, 128)
    send_grp(mixed_g, gathered_g, send_sems.at[7], recv_sems.at[7], grp, True)
    gathered_g[pl.ds(grp, 1)] = mixed_g[pl.ds(grp, 1)]
    wait_blocks(second, second, send_sems.at[6], recv_sems.at[6], N_GRP * N_Z - 1, me)
    third[pl.ds(low, 1)] = jnp.sum(second[...], axis=0, keepdims=True)

    def collect(step, carry):
        pltpu.make_async_remote_copy(
            src_ref=third.at[low],
            dst_ref=third.at[low],
            send_sem=send_sems.at[8],
            recv_sem=recv_sems.at[8],
            device_id={"slab": z * N_LOW + lax.rem(low + step, N_LOW)},
            device_id_type=MESH,
        ).start()
        return carry

    lax.fori_loop(1, N_LOW, collect, 0)
    wait_blocks(mixed_g, gathered_g, send_sems.at[7], recv_sems.at[7], N_GRP - 1, me)
    weight_terms(gathered_g, shifted_modes, d_spec)
    spec_copy = pltpu.make_async_copy(d_spec, spec_hbm, out_sems.at[8])
    spec_copy.start()
    for part in range(8):
        rows = pl.ds(8 * part, 8)
        pltpu.make_async_copy(out_held.at[rows], out_hbm.at[rows], out_sems.at[part]).wait()
    wait_blocks(third, third, send_sems.at[8], recv_sems.at[8], N_LOW - 1, me)
    sums_out[...] = third[...]
    spec_copy.wait()


def layer_call(field, cotangent, w_spec, w_local, direction, shift, bias):
    vmem = pl.BlockSpec(memory_space=pltpu.VMEM)
    hbm = pl.BlockSpec(memory_space=pl.ANY)
    tables = (
        table_ty(), table_zt(False), table_zt(True), table_tx(),
        np.ascontiguousarray(table_tx().T), table_ey(), table_ez(),
    )
    cells = (64, 2, 128, 128)
    blocks = pltpu.VMEM((64, 8, 128), BF16)
    quads = pltpu.VMEM((4, 16, 128), BF16)
    return pl.pallas_call(
        layer_kernel,
        out_shape=(
            jax.ShapeDtypeStruct(cells, BF16),
            jax.ShapeDtypeStruct((16, 64, 128), F32),
            jax.ShapeDtypeStruct((8, 8, 128), F32),
        ),
        in_specs=[hbm] * 6 + [pl.BlockSpec(memory_space=pltpu.SMEM)] + [hbm] * 7,
        out_specs=(hbm, hbm, vmem),
        scratch_shapes=[pltpu.VMEM(table.shape, BF16) for table in tables]
        + [
            pltpu.VMEM((16, 64, 128), BF16),
            pltpu.VMEM((64, 64), BF16),
            pltpu.VMEM((BITS, 64), jnp.int32),
            pltpu.VMEM((1, 64), jnp.int32),
            pltpu.VMEM((8, 128), F32),
            pltpu.VMEM(cells, BF16),
            pltpu.VMEM(cells, BF16),
            pltpu.VMEM(cells, BF16),
            pltpu.VMEM((8, 512, 512), BF16),
            pltpu.VMEM((8, 512, 512), BF16),
            pltpu.VMEM((64, 128, 256), F32),
            pltpu.VMEM((4096, 128), F32),
            pltpu.VMEM((4096, 128), F32),
            pltpu.VMEM((512, 512), BF16),
            pltpu.VMEM((2048, 128), BF16),
            pltpu.VMEM((16, 64, 128), F32),
            pltpu.VMEM((2, 2, 64, 256), F32),
            pltpu.VMEM((256, 512), F32),
            pltpu.VMEM((256, 1024), BF16),
            pltpu.VMEM((256, 1024), BF16),
            pltpu.VMEM((256, 1024), BF16),
            pltpu.VMEM((256, 1024), BF16),
            pltpu.VMEM((64, 8, 128), F32),
            blocks, blocks, quads, quads, blocks, blocks, blocks, blocks, quads, quads,
            pltpu.VMEM((64, 128), F32),
            pltpu.VMEM((64, 128), F32),
            pltpu.VMEM((4, 8, 128), F32),
            pltpu.VMEM((4, 8, 128), F32),
            pltpu.VMEM((64, 16, 128), F32),
            pltpu.VMEM((8, 8, 128), F32),
            pltpu.VMEM((8, 8, 128), F32),
            pltpu.VMEM((32, 8, 128), F32),
            pltpu.VMEM((1, 8, 128), F32),
            pltpu.VMEM((8, 8, 128), F32),
            pltpu.SemaphoreType.DMA((8,)),
            pltpu.SemaphoreType.DMA((8,)),
            pltpu.SemaphoreType.DMA((11,)),
            pltpu.SemaphoreType.DMA((9,)),
            pltpu.SemaphoreType.DMA((9,)),
            pltpu.SemaphoreType.DMA((9,)),
        ],
        compiler_params=pltpu.CompilerParams(
            collective_id=0, has_side_effects=True, vmem_limit_bytes=58 * MIB
        ),
    )(field, cotangent, w_spec, w_local, direction, shift, bias, *tables)


def results_kernel(
    out_hbm, spec_hbm, sums_hbm,
    output, spec_out, d_local, d_bias,
    held, spec_held, sums_ref, in_sems, out_sems,
):
    moves = []
    for part in range(8):
        rows = pl.ds(8 * part, 8)
        moves.append((out_hbm.at[rows], held.at[rows], output.at[rows]))
    for part in range(2):
        rows = pl.ds(8 * part, 8)
        moves.append((spec_hbm.at[rows], spec_held.at[rows], spec_out.at[rows]))
    ins = [
        pltpu.make_async_copy(source, middle, in_sems.at[at])
        for at, (source, middle, _) in enumerate(moves)
    ]
    outs = [
        pltpu.make_async_copy(middle, target, out_sems.at[at])
        for at, (_, middle, target) in enumerate(moves)
    ]
    sums_copy = pltpu.make_async_copy(sums_hbm, sums_ref, in_sems.at[10])
    for copy in ins:
        copy.start()
    sums_copy.start()
    for before, after in zip(ins, outs):
        before.wait()
        after.start()
    sums_copy.wait()
    sums = sums_ref[...].reshape(64, 128)
    d_local[...] = sums[:, 0:64]
    d_bias[...] = sums[0:1, 64:128]
    for copy in outs:
        copy.wait()


def results_call(out, d_spec, sums):
    vmem = pl.BlockSpec(memory_space=pltpu.VMEM)
    hbm = pl.BlockSpec(memory_space=pl.ANY)
    return pl.pallas_call(
        results_kernel,
        out_shape=(
            jax.ShapeDtypeStruct(out.shape, BF16),
            jax.ShapeDtypeStruct(d_spec.shape, F32),
            jax.ShapeDtypeStruct((64, 64), F32),
            jax.ShapeDtypeStruct((1, 64), F32),
        ),
        in_specs=[hbm] * 3,
        out_specs=(hbm, hbm, vmem, vmem),
        scratch_shapes=[
            pltpu.VMEM(out.shape, BF16),
            pltpu.VMEM(d_spec.shape, F32),
            pltpu.VMEM((8, 8, 128), F32),
            pltpu.SemaphoreType.DMA((11,)),
            pltpu.SemaphoreType.DMA((10,)),
        ],
        compiler_params=pltpu.CompilerParams(vmem_limit_bytes=58 * MIB),
    )(out, d_spec, sums)


def shards(base_field, cotangent, w_spec, w_local, bias, direction, shift):
    out, d_spec, sums = layer_call(
        base_field, cotangent[0], w_spec.reshape(16, 64, 128), w_local, direction.T, shift, bias
    )
    output, d_spec, d_local, d_bias = results_call(out, d_spec, sums)
    return (output[None], d_spec.reshape(4, 4, 64, 128), d_local, d_bias.reshape(64))


def solution(mesh):
    return jax.shard_map(
        shards,
        mesh=mesh,
        in_specs=(
            P(None, "slab", None, None),
            P("grp", None, "slab", None, None),
            P("grp", "slab", None, None),
            P(),
            P(),
            P(),
            P("grp", None),
        ),
        out_specs=(P("grp", None, "slab", None, None), P("grp", "slab", None, None), P(), P()),
        check_vma=False,
    )
```

```python
import functools
import math

import jax
import jax.numpy as jnp
import ml_dtypes
import numpy as np
from jax import lax
from jax.experimental import pallas as pl
from jax.experimental.pallas import tpu as pltpu
from jax.sharding import PartitionSpec as P

CH = 64
NX = 128
NY = 128
NZ = 128
MODES = 16
BITS = 30
N_GRP = 4
N_SLAB = 64
N_LOW = 8
N_Z = 8
MESH = pl.DeviceIdType.MESH
F32 = jnp.float32
BF16 = jnp.bfloat16
MIB = 1024 * 1024
GELU_K = math.sqrt(2.0 / math.pi)
GELU_A = 0.044715
GRAD_SCALE = 1.0 / math.sqrt(N_GRP * NX * NY * NZ)


def waves(length, half):
    ids = np.arange(MODES)
    if not half:
        ids = np.where(ids < MODES // 2, ids, length - MODES + ids)
    angles = 2.0 * math.pi / length * (ids[:, None] * np.arange(length)[None, :] % length)
    return np.cos(angles), np.sin(angles)


def as_bf16(table):
    return np.asarray(table, np.float32).astype(ml_dtypes.bfloat16)


def table_ty():
    cos_y, sin_y = waves(NY, False)
    out = np.zeros((2, 2, MODES, 2, NY))
    for c2 in range(2):
        out[0, c2, :, c2] = cos_y
        out[1, c2, :, c2] = sin_y
    return as_bf16(out.reshape(64, 256))


def weights_z(backward):
    return np.where(np.arange(MODES) == 0, 1.0, 2.0 if backward else 1.0)[:, None]


def table_zt(backward):
    cos_z, sin_z = waves(NZ, True)
    weight = weights_z(backward)
    if backward:
        weight = weight * GRAD_SCALE
    cos_z = (weight * cos_z).reshape(4, 4, NZ)
    sin_z = (weight * sin_z).reshape(4, 4, NZ)
    out = np.zeros((2, 4, 2, 4, 2, 2, NZ))
    for x in range(2):
        out[0, :, x, :, 0, x] = cos_z
        out[0, :, x, :, 1, x] = -sin_z
        out[1, :, x, :, 0, x] = -sin_z
        out[1, :, x, :, 1, x] = -cos_z
    return as_bf16(out.reshape(64, 512))


def table_tx():
    cos_x, sin_x = waves(NX, False)
    out = np.zeros((2, MODES, 4, NX, 4))
    for m in range(4):
        out[0, :, m, :, m] = cos_x
        out[1, :, m, :, m] = sin_x
    return as_bf16(out.reshape(128, 512))


def table_ey():
    cos_y, sin_y = waves(NY, False)
    out = np.zeros((2, NY, 2, 2, MODES))
    for c2 in range(2):
        out[c2, :, c2, 0] = cos_y.T
        out[c2, :, c2, 1] = -sin_y.T
    return as_bf16(out.reshape(256, 64))


def table_ez():
    cos_z, sin_z = waves(NZ, True)
    weight = weights_z(True) / math.sqrt(MODES**3)
    cos_z = (weight * cos_z).reshape(4, 4, NZ)
    sin_z = (weight * sin_z).reshape(4, 4, NZ)
    out = np.zeros((2, 4, 2, 4, 2, 2, NZ))
    for x in range(2):
        out[0, :, x, :, 0, x] = cos_z
        out[1, :, x, :, 0, x] = -sin_z
        out[0, :, x, :, 1, x] = sin_z
        out[1, :, x, :, 1, x] = cos_z
    return as_bf16(out.reshape(64, 512))


def lane_sign(rows, first, second):
    lane = lax.broadcasted_iota(jnp.int32, (rows, 128), 1)
    return jnp.where(lane < 64, first, second).astype(F32)


def turned(rows, first, second):
    return pltpu.roll(rows, 64, 1) * lane_sign(rows.shape[0], first, second)


def nt_dot(left, right, precision=None):
    return lax.dot_general(
        left, right, (((1,), (1,)), ((), ())), preferred_element_type=F32, precision=precision
    )


def fetch_field(field, held, sems):
    for part in range(8):
        rows = pl.ds(8 * part, 8)
        pltpu.make_async_copy(field.at[rows], held.at[rows], sems.at[part]).start()


def wait_field(field, held, sems, part):
    rows = pl.ds(8 * part, 8)
    pltpu.make_async_copy(field.at[rows], held.at[rows], sems.at[part]).wait()


def store_along_y(along_y, got, first):
    for cs in range(2):
        for c2 in range(2):
            at = cs * 32 + c2 * 16
            for x in range(2):
                start = (2 * cs + x) * 1024 + first + c2
                along_y[pl.ds(start, 16, stride=64), :] = got[
                    at : at + 16, x * 128 : x * 128 + 128
                ]


def along_z_half(half, along_y, zt_ref, modes_z):
    for part in range(2):
        rows = jnp.concatenate(
            [
                jnp.concatenate(
                    [
                        along_y[
                            cs_x * 1024 + jy * 64 + half * 32 : cs_x * 1024 + jy * 64 + half * 32 + 32,
                            :,
                        ]
                        for jy in range(part * 8, part * 8 + 8)
                    ],
                    0,
                ).astype(BF16)
                for cs_x in range(4)
            ],
            1,
        )
        modes_z[half, part] = nt_dot(zt_ref[...], rows)


def join_halves(modes_z, slab_modes):
    for jy in range(16):
        lanes = slice((jy % 8) * 32, (jy % 8) * 32 + 32)
        block = jnp.concatenate(
            [
                modes_z[half, jy // 8, re * 32 : re * 32 + 32, lanes]
                for re in range(2)
                for half in range(2)
            ],
            1,
        )
        slab_modes[jy * 4 : jy * 4 + 4] = block.reshape(4, 8, 128).astype(BF16)


def greetings(barrier, me, grp, low, z):
    def tell(device):
        pl.semaphore_signal(barrier, inc=1, device_id=device, device_id_type=MESH)

    calls = []
    for dz in (4, 3, 5, 2, 6, 1, 7, 0):
        other_z = lax.rem(z + dz, N_Z) * N_LOW
        for g_step in (2, 1, 3):
            calls.append(
                functools.partial(
                    tell, {"grp": lax.rem(grp + g_step, N_GRP), "slab": other_z + low}
                )
            )
        for step in (4, 5, 2, 3, 6, 7, 1, 0):
            if dz or step:
                calls.append(
                    functools.partial(tell, {"slab": other_z + lax.rem(low + step, N_LOW)})
                )
    return calls


def send_all(source, target, send_sem, recv_sem, me):
    low = lax.rem(me, N_LOW)
    z = me // N_LOW
    for dz in (4, 3, 5, 2, 6, 1, 7, 0):

        def go(step, carry):
            other = lax.rem(z + dz, N_Z) * N_LOW + lax.rem(low + step, N_LOW)
            pltpu.make_async_remote_copy(
                src_ref=source.at[other],
                dst_ref=target.at[me],
                send_sem=send_sem,
                recv_sem=recv_sem,
                device_id={"slab": other},
                device_id_type=MESH,
            ).start()
            return carry

        lax.fori_loop(1 if dz == 0 else 0, N_LOW, go, 0)
    target[pl.ds(me, 1)] = source[pl.ds(me, 1)]


def wait_blocks(source, target, send_sem, recv_sem, count, me):
    pltpu.make_async_remote_copy(
        src_ref=source.at[pl.ds(0, count)],
        dst_ref=target.at[pl.ds(0, count)],
        send_sem=send_sem,
        recv_sem=recv_sem,
        device_id={"slab": me},
        device_id_type=MESH,
    ).wait()


def send_grp(source, target, send_sem, recv_sem, grp, by_target):
    for step in range(1, N_GRP):
        other = lax.rem(grp + step, N_GRP)
        pltpu.make_async_remote_copy(
            src_ref=source.at[other] if by_target else source.at[grp],
            dst_ref=target.at[grp],
            send_sem=send_sem,
            recv_sem=recv_sem,
            device_id={"grp": other},
            device_id_type=MESH,
        ).start()


def x_modes(pencil, tx_ref):
    rows = pencil[...].astype(F32).reshape(512, 128).astype(BF16)
    both = jnp.dot(tx_ref[...], rows, preferred_element_type=F32)
    return both[:64] + turned(both[64:], 1.0, -1.0)


def local_step(part, held, kron, bias_rows, field_rows, local):
    y_at = pl.multiple_of(16 * part, 16)
    halves = [held[:, x, pl.ds(y_at, 16), :].astype(F32) for x in range(2)]
    for half in range(2):
        rows = jnp.concatenate(
            [block[:, 8 * half : 8 * half + 8].reshape(512, 128) for block in halves], 1
        ).astype(BF16)
        field_rows[part, :, half * 256 : half * 256 + 256] = rows
        got = jnp.dot(kron[...], rows, preferred_element_type=F32)
        added = bias_rows[...]
        local[:, pl.ds(pl.multiple_of(y_at + 8 * half, 8), 8), :] = got.reshape(
            64, 8, 256
        ) + jnp.concatenate([added, added], 2)


def scale_rows(grp, direction_ref, shift_ref):
    number = grp + 1
    gray_code = number ^ (number >> 1)
    bits = shift_ref[...]
    for bit_pos in range(N_GRP.bit_length()):
        bits = bits ^ (direction_ref[bit_pos : bit_pos + 1, :] * ((gray_code >> bit_pos) & 1))
    scale = 0.5 + bits.astype(F32) * 2.0 ** (-BITS)
    return jnp.broadcast_to(jnp.concatenate([scale, scale], 1), (8, 128))


def fill_kron(wl_ref, scale_row, kron):
    local = (wl_ref[...].astype(F32) * scale_row[0:1, 0:64]).astype(BF16)
    pick = (
        lax.broadcasted_iota(jnp.int32, (64, 512), 0)
        == lax.broadcasted_iota(jnp.int32, (64, 512), 1) // 8
    )
    wide = jnp.dot(local, pick.astype(F32).astype(BF16), preferred_element_type=F32).astype(BF16)
    same = (
        lax.broadcasted_iota(jnp.int32, (64, 512), 0) % 8
        == lax.broadcasted_iota(jnp.int32, (64, 512), 1) % 8
    )
    row_ids = lax.broadcasted_iota(jnp.int32, (64, 64), 0) // 8
    col_ids = lax.broadcasted_iota(jnp.int32, (64, 64), 1)
    for octet in range(8):
        rows_of = (row_ids + 8 * octet == col_ids).astype(F32).astype(BF16)
        tall = jnp.dot(rows_of, wide, preferred_element_type=F32)
        kron[octet * 64 : octet * 64 + 64, :] = jnp.where(same, tall, 0.0).astype(BF16)


def fill_along_z(landed, ez_ref, along_z):
    for quarter in range(4):
        rows = landed[quarter * 16 : quarter * 16 + 16].astype(F32).reshape(128, 128)
        turn = rows.T
        per_c = jnp.concatenate(
            [
                jnp.concatenate(
                    [turn[0:64, jy * 32 : jy * 32 + 32], turn[64:128, jy * 32 : jy * 32 + 32]], 1
                )
                for jy in range(4)
            ],
            0,
        ).astype(BF16)
        got = jnp.dot(per_c, ez_ref[...], preferred_element_type=F32)
        for jy in range(4):
            for cs in range(2):
                for x in range(2):
                    start = x * 2048 + cs * 16 + quarter * 4 + jy
                    lane = cs * 256 + x * 128
                    along_z[pl.ds(start, 64, stride=32), :] = got[
                        jy * 64 : jy * 64 + 64, lane : lane + 128
                    ]


def synthesis(group, along_z, local, ey_ref, pre_act):
    rows = jnp.concatenate(
        [
            along_z[pl.ds(x * 2048 + 256 * group + 64 * pair, 64), :].astype(BF16)
            for pair in range(4)
            for x in range(2)
        ],
        1,
    )
    got = jnp.dot(ey_ref[...], rows, preferred_element_type=F32)
    for pair in range(4):
        for c2 in range(2):
            at = slice(c2 * 128, c2 * 128 + 128)
            lanes = slice(pair * 256, pair * 256 + 256)
            pre_act[at, lanes] = (
                got[at, lanes] + local[8 * group + 2 * pair + c2]
            ).astype(BF16)


def activation(group, pre_act, cotan_in, out_held, cotan_pre):
    for pair in range(4):
        for c2 in range(2):
            for x in range(2):
                channel = 8 * group + 2 * pair + c2
                at = slice(c2 * 128, c2 * 128 + 128)
                lanes = slice(pair * 256 + x * 128, pair * 256 + x * 128 + 128)
                pre = pre_act[at, lanes]
                square = pre * pre
                inner = pre * (1.0 + GELU_A * square)
                tanh = jnp.tanh(inner.astype(F32) * GELU_K)
                half = 0.5 + 0.5 * tanh
                bell = (half * (GELU_K - GELU_K * tanh)).astype(BF16)
                half = half.astype(BF16)
                out_held[channel, x] = pre * half
                slope = half + bell * (pre * (1.0 + (3.0 * GELU_A) * square))
                cotan_pre[at, lanes] = slope * cotan_in[channel, x]


def gradient_modes(group, cotan_pre, ty_ref, cotan_rows, bias_sum, along_y):
    got = jnp.dot(ty_ref[...], cotan_pre[...], preferred_element_type=F32)
    for pair in range(4):
        store_along_y(along_y, got[:, pair * 256 : pair * 256 + 256], 8 * group + 2 * pair)
    for pair in range(4):
        for x in range(2):
            lanes = slice(pair * 256 + x * 128, pair * 256 + x * 128 + 128)
            wide = cotan_pre[:, lanes].astype(F32)
            sums = jnp.sum(wide.reshape(2, 16, 8, 128), axis=1)
            for c2 in range(2):
                bias_sum[8 * group + 2 * pair + c2, x * 8 : x * 8 + 8] = sums[c2]
            for y8 in range(16):
                block = jnp.concatenate(
                    [wide[c2 * 128 + 8 * y8 : c2 * 128 + 8 * y8 + 8] for c2 in range(2)], 0
                )
                lane = (y8 % 2) * 256 + x * 128
                cotan_rows[
                    y8 // 2, pl.ds(64 * group + 16 * pair, 16), lane : lane + 128
                ] = block.astype(BF16)


def local_grad(grad):
    same = (
        lax.broadcasted_iota(jnp.int32, (256, 512), 0) % 8
        == lax.broadcasted_iota(jnp.int32, (256, 512), 1) % 8
    )
    kept = jnp.where(same, grad, 0.0)
    high = kept.astype(BF16)
    low = (kept - high.astype(F32)).astype(BF16)
    pick = (
        lax.broadcasted_iota(jnp.int32, (512, 64), 0) // 8
        == lax.broadcasted_iota(jnp.int32, (512, 64), 1)
    )
    pick = pick.astype(F32).astype(BF16)
    got = jnp.dot(high, pick, preferred_element_type=F32) + jnp.dot(
        low, pick, preferred_element_type=F32
    )
    return jnp.sum(got.reshape(32, 8, 64), axis=1)


def fill_terms(shifted_modes, terms):
    turn = shifted_modes[...].T
    columns = jnp.concatenate([turn[0:64], turn[64:128]], 1)
    mode = lax.broadcasted_iota(jnp.int32, (64, 128), 1) % 16
    for k in range(16):
        terms[k * 64 : k * 64 + 64, :] = jnp.where(mode == k, columns, 0.0).astype(BF16)


def weight_terms(gathered_g, terms, d_spec):
    rows = gathered_g[...].reshape(64, 128)
    both = jnp.concatenate([rows, turned(rows.astype(F32), 1.0, -1.0).astype(BF16)], 0)
    got = jnp.dot(terms[...], both, preferred_element_type=F32)
    d_spec[...] = got.reshape(16, 64, 128)


def layer_kernel(
    field, cotan, w_hbm, wl_hbm, direction_hbm, shift_hbm, bias_ref,
    ty_hbm, ztf_hbm, ztb_hbm, tx_hbm, txb_hbm, ey_hbm, ez_hbm,
    out_hbm, spec_hbm, sums_out,
    ty_ref, ztf_ref, ztb_ref, tx_ref, txb_ref, ey_ref, ez_ref, w_ref, wl_ref, direction_ref, shift_ref, scale_ref,
    held, cotan_in, out_held, field_rows, cotan_rows, local, along_y, along_z, kron, w_two,
    d_spec, terms, modes_z, grad, pre_even, pre_odd, cotan_even, cotan_odd, bias_rows,
    slab_modes, pencil, mixed, gathered, back, landed, slab_g, pencil_g, mixed_g, gathered_g,
    all_modes, shifted_modes, scale_own, scale_all, bias_sum, own_sums, first, second, second_own, third,
    field_sems, cotan_sems, table_sems, out_sems, send_sems, recv_sems,
):
    me = lax.axis_index("slab")
    grp = lax.axis_index("grp")
    low = lax.rem(me, N_LOW)
    z = me // N_LOW
    barrier = pltpu.get_barrier_semaphore()
    small = [
        (ty_hbm, ty_ref), (ztf_hbm, ztf_ref), (direction_hbm, direction_ref), (wl_hbm, wl_ref),
        (w_hbm, w_ref), (tx_hbm, tx_ref), (txb_hbm, txb_ref), (ey_hbm, ey_ref),
        (ez_hbm, ez_ref), (ztb_hbm, ztb_ref), (shift_hbm, shift_ref),
    ]
    copies = [
        pltpu.make_async_copy(source, target, table_sems.at[at])
        for at, (source, target) in enumerate(small)
    ]
    for copy in copies[:2]:
        copy.start()
    fetch_field(field, held, field_sems)
    for copy in copies[2:]:
        copy.start()
    fetch_field(cotan, cotan_in, cotan_sems)
    calls = greetings(barrier, me, grp, low, z)

    for call in calls[:15]:
        call()
    copies[0].wait()

    for part in range(8):
        for call in calls[15 * part + 15 : 15 * part + 30]:
            call()
        wait_field(field, held, field_sems, part)
        rows = jnp.concatenate(
            [
                jnp.concatenate([held[8 * part + 2 * pair + c2, x] for c2 in range(2)], 0)
                for pair in range(4)
                for x in range(2)
            ],
            1,
        )
        got = jnp.dot(ty_ref[...], rows, preferred_element_type=F32)
        for pair in range(4):
            store_along_y(along_y, got[:, pair * 256 : pair * 256 + 256], 8 * part + 2 * pair)
        if part == 3:
            copies[1].wait()
            along_z_half(0, along_y, ztf_ref, modes_z)
    along_z_half(1, along_y, ztf_ref, modes_z)
    join_halves(modes_z, slab_modes)
    copies[2].wait()
    copies[10].wait()
    scale_ref[...] = scale_rows(grp, direction_ref, shift_ref)
    scale_own[grp] = scale_ref[...]
    scale_all[grp] = scale_ref[...]
    pl.semaphore_wait(barrier, N_SLAB - 1 + N_GRP - 1 + (N_GRP - 1) * (N_Z - 1))
    send_all(slab_modes, pencil, send_sems.at[0], recv_sems.at[0], me)
    send_grp(scale_own, scale_all, send_sems.at[1], recv_sems.at[1], grp, False)

    copies[3].wait()
    copies[4].wait()
    for k in range(16):
        block = w_ref[k].astype(F32)
        w_two[k * 128 : k * 128 + 64, :] = w_ref[k]
        w_two[k * 128 + 64 : k * 128 + 128, :] = turned(block, -1.0, 1.0).astype(BF16)
    fill_kron(wl_ref, scale_ref[...], kron)
    for channel in range(CH):
        bias_rows[channel] = jnp.full((8, 128), bias_ref[channel], F32)

    def local_some(part, carry):
        local_step(part, held, kron, bias_rows, field_rows, local)
        return carry

    lax.fori_loop(0, 3, local_some, 0)
    pltpu.make_async_remote_copy(
        src_ref=scale_own.at[pl.ds(0, N_GRP - 1)],
        dst_ref=scale_all.at[pl.ds(0, N_GRP - 1)],
        send_sem=send_sems.at[1],
        recv_sem=recv_sems.at[1],
        device_id={"slab": me},
        device_id_type=MESH,
    ).wait()
    copies[5].wait()
    copies[6].wait()
    wait_blocks(slab_modes, pencil, send_sems.at[0], recv_sems.at[0], N_SLAB - 1, me)

    all_modes[...] = x_modes(pencil, tx_ref) * (1.0 / math.sqrt(NX * NY * NZ))
    own = all_modes[pl.ds(pl.multiple_of(16 * grp, 16), 16), :]
    shifted = jnp.concatenate([own * scale_all[s, 0:1, :] for s in range(N_GRP)], 0)
    shifted_modes[...] = shifted
    row_mode = lax.broadcasted_iota(jnp.int32, (64, 128), 0) % 16
    spread = jnp.concatenate(
        [jnp.where(row_mode == k, shifted, 0.0).astype(BF16) for k in range(16)], 1
    )
    mixed[...] = (
        jnp.dot(spread, w_two[...], preferred_element_type=F32).astype(BF16).reshape(4, 16, 128)
    )
    send_grp(mixed, gathered, send_sems.at[2], recv_sems.at[2], grp, True)
    gathered[pl.ds(grp, 1)] = mixed[pl.ds(grp, 1)]
    lax.fori_loop(3, 5, local_some, 0)
    wait_blocks(mixed, gathered, send_sems.at[2], recv_sems.at[2], N_GRP - 1, me)
    full = gathered[...].reshape(64, 128)
    both = jnp.concatenate([full, turned(full.astype(F32), -1.0, 1.0).astype(BF16)], 0)
    back[...] = (
        jnp.dot(txb_ref[...], both, preferred_element_type=F32).reshape(64, 8, 128).astype(BF16)
    )
    send_all(back, landed, send_sems.at[3], recv_sems.at[3], me)
    lax.fori_loop(5, 8, local_some, 0)
    fill_terms(shifted_modes, terms)
    for copy in copies[7:10]:
        copy.wait()
    for part in range(8):
        wait_field(cotan, cotan_in, cotan_sems, part)
    wait_blocks(back, landed, send_sems.at[3], recv_sems.at[3], N_SLAB - 1, me)

    fill_along_z(landed, ez_ref, along_z)

    slots = ((pre_even, cotan_even), (pre_odd, cotan_odd))
    for step in range(10):
        if step < 8:
            synthesis(step, along_z, local, ey_ref, slots[step % 2][0])
        if 0 < step < 9:
            pre_act, cotan_pre = slots[(step - 1) % 2]
            activation(step - 1, pre_act, cotan_in, out_held, cotan_pre)
            rows = pl.ds(8 * (step - 1), 8)
            pltpu.make_async_copy(
                out_held.at[rows], out_hbm.at[rows], out_sems.at[step - 1]
            ).start()
        if step > 1:
            gradient_modes(
                step - 2, slots[step % 2][1], ty_ref, cotan_rows, bias_sum, along_y
            )
        if step == 5:
            along_z_half(0, along_y, ztb_ref, modes_z)
            grad[...] = jnp.zeros_like(grad)
        if step > 5:
            for part in (2 * step - 12, 2 * step - 11):
                grad[...] += nt_dot(cotan_rows[part, 0:256, :], field_rows[part])

    d_top = local_grad(grad[...])
    bottom = jnp.zeros((256, 512), F32)
    for part in range(8):
        bottom = bottom + nt_dot(cotan_rows[part, 256:512, :], field_rows[part])
    d_local = jnp.concatenate([d_top, local_grad(bottom)], 0)
    d_local = d_local * (scale_ref[0:1, 0:64] * GRAD_SCALE)
    lanes = jnp.sum(bias_sum[...], axis=1)
    d_bias = nt_dot(jnp.full((8, 128), GRAD_SCALE, F32), lanes, lax.Precision.HIGHEST)
    side = jnp.concatenate([d_bias, jnp.zeros((56, 64), F32)], 0)
    own_sums[...] = jnp.concatenate([d_local, side], 1).reshape(8, 8, 128)

    def scatter(step, carry):
        other = lax.rem(low + step, N_LOW)
        pltpu.make_async_remote_copy(
            src_ref=own_sums.at[other],
            dst_ref=first.at[low],
            send_sem=send_sems.at[4],
            recv_sem=recv_sems.at[4],
            device_id={"slab": z * N_LOW + other},
            device_id_type=MESH,
        ).start()
        return carry

    lax.fori_loop(1, N_LOW, scatter, 0)
    first[pl.ds(low, 1)] = own_sums[pl.ds(low, 1)]
    along_z_half(1, along_y, ztb_ref, modes_z)
    join_halves(modes_z, slab_g)
    send_all(slab_g, pencil_g, send_sems.at[5], recv_sems.at[5], me)
    wait_blocks(own_sums, first, send_sems.at[4], recv_sems.at[4], N_LOW - 1, me)
    part_sum = jnp.sum(first[...], axis=0, keepdims=True)
    mine = grp * N_Z + z
    second[pl.ds(mine, 1)] = part_sum
    second_own[...] = part_sum
    for g_step in (2, 1, 3, 0):

        def spread_sum(step, carry):
            pltpu.make_async_remote_copy(
                src_ref=second_own.at[0],
                dst_ref=second.at[mine],
                send_sem=send_sems.at[6],
                recv_sem=recv_sems.at[6],
                device_id={
                    "grp": lax.rem(grp + g_step, N_GRP),
                    "slab": lax.rem(z + step, N_Z) * N_LOW + low,
                },
                device_id_type=MESH,
            ).start()
            return carry

        lax.fori_loop(1 if g_step == 0 else 0, N_Z, spread_sum, 0)
    wait_blocks(slab_g, pencil_g, send_sems.at[5], recv_sems.at[5], N_SLAB - 1, me)
    mixed_g[...] = x_modes(pencil_g, tx_ref).astype(BF16).reshape(4, 16, 128)
    send_grp(mixed_g, gathered_g, send_sems.at[7], recv_sems.at[7], grp, True)
    gathered_g[pl.ds(grp, 1)] = mixed_g[pl.ds(grp, 1)]
    wait_blocks(second, second, send_sems.at[6], recv_sems.at[6], N_GRP * N_Z - 1, me)
    third[pl.ds(low, 1)] = jnp.sum(second[...], axis=0, keepdims=True)

    def collect(step, carry):
        pltpu.make_async_remote_copy(
            src_ref=third.at[low],
            dst_ref=third.at[low],
            send_sem=send_sems.at[8],
            recv_sem=recv_sems.at[8],
            device_id={"slab": z * N_LOW + lax.rem(low + step, N_LOW)},
            device_id_type=MESH,
        ).start()
        return carry

    lax.fori_loop(1, N_LOW, collect, 0)
    wait_blocks(mixed_g, gathered_g, send_sems.at[7], recv_sems.at[7], N_GRP - 1, me)
    weight_terms(gathered_g, terms, d_spec)
    spec_copy = pltpu.make_async_copy(d_spec, spec_hbm, out_sems.at[8])
    spec_copy.start()
    for part in range(8):
        rows = pl.ds(8 * part, 8)
        pltpu.make_async_copy(out_held.at[rows], out_hbm.at[rows], out_sems.at[part]).wait()
    wait_blocks(third, third, send_sems.at[8], recv_sems.at[8], N_LOW - 1, me)
    sums_out[...] = third[...]
    spec_copy.wait()


def layer_call(field, cotangent, w_spec, w_local, direction, shift, bias):
    vmem = pl.BlockSpec(memory_space=pltpu.VMEM)
    hbm = pl.BlockSpec(memory_space=pl.ANY)
    tables = (
        table_ty(), table_zt(False), table_zt(True), table_tx(),
        np.ascontiguousarray(table_tx().T), table_ey(), table_ez(),
    )
    cells = (64, 2, 128, 128)
    blocks = pltpu.VMEM((64, 8, 128), BF16)
    quads = pltpu.VMEM((4, 16, 128), BF16)
    return pl.pallas_call(
        layer_kernel,
        out_shape=(
            jax.ShapeDtypeStruct(cells, BF16),
            jax.ShapeDtypeStruct((16, 64, 128), F32),
            jax.ShapeDtypeStruct((8, 8, 128), F32),
        ),
        in_specs=[hbm] * 6 + [pl.BlockSpec(memory_space=pltpu.SMEM)] + [hbm] * 7,
        out_specs=(hbm, hbm, vmem),
        scratch_shapes=[pltpu.VMEM(table.shape, BF16) for table in tables]
        + [
            pltpu.VMEM((16, 64, 128), BF16),
            pltpu.VMEM((64, 64), BF16),
            pltpu.VMEM((BITS, 64), jnp.int32),
            pltpu.VMEM((1, 64), jnp.int32),
            pltpu.VMEM((8, 128), F32),
            pltpu.VMEM(cells, BF16),
            pltpu.VMEM(cells, BF16),
            pltpu.VMEM(cells, BF16),
            pltpu.VMEM((8, 512, 512), BF16),
            pltpu.VMEM((8, 512, 512), BF16),
            pltpu.VMEM((64, 128, 256), F32),
            pltpu.VMEM((4096, 128), F32),
            pltpu.VMEM((4096, 128), F32),
            pltpu.VMEM((512, 512), BF16),
            pltpu.VMEM((2048, 128), BF16),
            pltpu.VMEM((16, 64, 128), F32),
            pltpu.VMEM((1024, 128), BF16),
            pltpu.VMEM((2, 2, 64, 256), F32),
            pltpu.VMEM((256, 512), F32),
            pltpu.VMEM((256, 1024), BF16),
            pltpu.VMEM((256, 1024), BF16),
            pltpu.VMEM((256, 1024), BF16),
            pltpu.VMEM((256, 1024), BF16),
            pltpu.VMEM((64, 8, 128), F32),
            blocks, blocks, quads, quads, blocks, blocks, blocks, blocks, quads, quads,
            pltpu.VMEM((64, 128), F32),
            pltpu.VMEM((64, 128), F32),
            pltpu.VMEM((4, 8, 128), F32),
            pltpu.VMEM((4, 8, 128), F32),
            pltpu.VMEM((64, 16, 128), F32),
            pltpu.VMEM((8, 8, 128), F32),
            pltpu.VMEM((8, 8, 128), F32),
            pltpu.VMEM((32, 8, 128), F32),
            pltpu.VMEM((1, 8, 128), F32),
            pltpu.VMEM((8, 8, 128), F32),
            pltpu.SemaphoreType.DMA((8,)),
            pltpu.SemaphoreType.DMA((8,)),
            pltpu.SemaphoreType.DMA((11,)),
            pltpu.SemaphoreType.DMA((9,)),
            pltpu.SemaphoreType.DMA((9,)),
            pltpu.SemaphoreType.DMA((9,)),
        ],
        compiler_params=pltpu.CompilerParams(
            collective_id=0, has_side_effects=True, vmem_limit_bytes=58 * MIB
        ),
    )(field, cotangent, w_spec, w_local, direction, shift, bias, *tables)


def results_kernel(
    out_hbm, spec_hbm, sums_hbm,
    output, spec_out, d_local, d_bias,
    held, spec_held, sums_ref, in_sems, out_sems,
):
    moves = []
    for part in range(8):
        rows = pl.ds(8 * part, 8)
        moves.append((out_hbm.at[rows], held.at[rows], output.at[rows]))
    for part in range(2):
        rows = pl.ds(8 * part, 8)
        moves.append((spec_hbm.at[rows], spec_held.at[rows], spec_out.at[rows]))
    ins = [
        pltpu.make_async_copy(source, middle, in_sems.at[at])
        for at, (source, middle, _) in enumerate(moves)
    ]
    outs = [
        pltpu.make_async_copy(middle, target, out_sems.at[at])
        for at, (_, middle, target) in enumerate(moves)
    ]
    sums_copy = pltpu.make_async_copy(sums_hbm, sums_ref, in_sems.at[10])
    for copy in ins:
        copy.start()
    sums_copy.start()
    for before, after in zip(ins, outs):
        before.wait()
        after.start()
    sums_copy.wait()
    sums = sums_ref[...].reshape(64, 128)
    d_local[...] = sums[:, 0:64]
    d_bias[...] = sums[0:1, 64:128]
    for copy in outs:
        copy.wait()


def results_call(out, d_spec, sums):
    vmem = pl.BlockSpec(memory_space=pltpu.VMEM)
    hbm = pl.BlockSpec(memory_space=pl.ANY)
    return pl.pallas_call(
        results_kernel,
        out_shape=(
            jax.ShapeDtypeStruct(out.shape, BF16),
            jax.ShapeDtypeStruct(d_spec.shape, F32),
            jax.ShapeDtypeStruct((64, 64), F32),
            jax.ShapeDtypeStruct((1, 64), F32),
        ),
        in_specs=[hbm] * 3,
        out_specs=(hbm, hbm, vmem, vmem),
        scratch_shapes=[
            pltpu.VMEM(out.shape, BF16),
            pltpu.VMEM(d_spec.shape, F32),
            pltpu.VMEM((8, 8, 128), F32),
            pltpu.SemaphoreType.DMA((11,)),
            pltpu.SemaphoreType.DMA((10,)),
        ],
        compiler_params=pltpu.CompilerParams(vmem_limit_bytes=58 * MIB),
    )(out, d_spec, sums)


def shards(base_field, cotangent, w_spec, w_local, bias, direction, shift):
    out, d_spec, sums = layer_call(
        base_field, cotangent[0], w_spec.reshape(16, 64, 128), w_local, direction.T, shift, bias
    )
    output, d_spec, d_local, d_bias = results_call(out, d_spec, sums)
    return (output[None], d_spec.reshape(4, 4, 64, 128), d_local, d_bias.reshape(64))


def solution(mesh):
    return jax.shard_map(
        shards,
        mesh=mesh,
        in_specs=(
            P(None, "slab", None, None),
            P("grp", None, "slab", None, None),
            P("grp", "slab", None, None),
            P(),
            P(),
            P(),
            P("grp", None),
        ),
        out_specs=(P("grp", None, "slab", None, None), P("grp", "slab", None, None), P(), P()),
        check_vma=False,
    )
```

```python
import functools
import math

import jax
import jax.numpy as jnp
import ml_dtypes
import numpy as np
from jax import lax
from jax.experimental import pallas as pl
from jax.experimental.pallas import tpu as pltpu
from jax.sharding import PartitionSpec as P

CH = 64
NX = 128
NY = 128
NZ = 128
MODES = 16
BITS = 30
N_GRP = 4
N_SLAB = 64
N_LOW = 8
N_Z = 8
MESH = pl.DeviceIdType.MESH
F32 = jnp.float32
BF16 = jnp.bfloat16
MIB = 1024 * 1024
GELU_K = math.sqrt(2.0 / math.pi)
GELU_A = 0.044715
GRAD_SCALE = 0.5 / math.sqrt(N_GRP * NX * NY * NZ)


def waves(length, half):
    ids = np.arange(MODES)
    if not half:
        ids = np.where(ids < MODES // 2, ids, length - MODES + ids)
    angles = 2.0 * math.pi / length * (ids[:, None] * np.arange(length)[None, :] % length)
    return np.cos(angles), np.sin(angles)


def as_bf16(table):
    return np.asarray(table, np.float32).astype(ml_dtypes.bfloat16)


def table_ty():
    cos_y, sin_y = waves(NY, False)
    out = np.zeros((2, 2, MODES, 2, NY))
    for c2 in range(2):
        out[0, c2, :, c2] = cos_y
        out[1, c2, :, c2] = sin_y
    return as_bf16(out.reshape(64, 256))


def weights_z(backward):
    return np.where(np.arange(MODES) == 0, 1.0, 2.0 if backward else 1.0)[:, None]


def table_zt(backward):
    cos_z, sin_z = waves(NZ, True)
    weight = weights_z(backward)
    if backward:
        weight = weight * GRAD_SCALE
    cos_z = (weight * cos_z).reshape(4, 4, NZ)
    sin_z = (weight * sin_z).reshape(4, 4, NZ)
    out = np.zeros((2, 4, 2, 4, 2, 2, NZ))
    for x in range(2):
        out[0, :, x, :, 0, x] = cos_z
        out[0, :, x, :, 1, x] = -sin_z
        out[1, :, x, :, 0, x] = -sin_z
        out[1, :, x, :, 1, x] = -cos_z
    return as_bf16(out.reshape(64, 512))


def table_tx():
    cos_x, sin_x = waves(NX, False)
    out = np.zeros((2, MODES, 4, NX, 4))
    for m in range(4):
        out[0, :, m, :, m] = cos_x
        out[1, :, m, :, m] = sin_x
    return as_bf16(out.reshape(128, 512))


def table_ey():
    cos_y, sin_y = waves(NY, False)
    out = np.zeros((2, NY, 2, 2, MODES))
    for c2 in range(2):
        out[c2, :, c2, 0] = cos_y.T
        out[c2, :, c2, 1] = -sin_y.T
    return as_bf16(out.reshape(256, 64))


def table_ez():
    cos_z, sin_z = waves(NZ, True)
    weight = weights_z(True) / math.sqrt(MODES**3)
    cos_z = (weight * cos_z).reshape(4, 4, NZ)
    sin_z = (weight * sin_z).reshape(4, 4, NZ)
    out = np.zeros((2, 4, 2, 4, 2, 2, NZ))
    for x in range(2):
        out[0, :, x, :, 0, x] = cos_z
        out[1, :, x, :, 0, x] = -sin_z
        out[0, :, x, :, 1, x] = sin_z
        out[1, :, x, :, 1, x] = cos_z
    return as_bf16(out.reshape(64, 512))


def lane_sign(rows, first, second):
    lane = lax.broadcasted_iota(jnp.int32, (rows, 128), 1)
    return jnp.where(lane < 64, first, second).astype(F32)


def turned(rows, first, second):
    return pltpu.roll(rows, 64, 1) * lane_sign(rows.shape[0], first, second)


def nt_dot(left, right, precision=None):
    return lax.dot_general(
        left, right, (((1,), (1,)), ((), ())), preferred_element_type=F32, precision=precision
    )


def fetch_field(field, held, sems):
    for part in range(8):
        rows = pl.ds(8 * part, 8)
        pltpu.make_async_copy(field.at[rows], held.at[rows], sems.at[part]).start()


def wait_field(field, held, sems, part):
    rows = pl.ds(8 * part, 8)
    pltpu.make_async_copy(field.at[rows], held.at[rows], sems.at[part]).wait()


def store_along_y(along_y, got, first):
    for cs in range(2):
        for c2 in range(2):
            at = cs * 32 + c2 * 16
            for x in range(2):
                start = (2 * cs + x) * 1024 + first + c2
                along_y[pl.ds(start, 16, stride=64), :] = got[
                    at : at + 16, x * 128 : x * 128 + 128
                ]


def along_z_half(half, along_y, zt_ref, modes_z):
    for part in range(2):
        rows = jnp.concatenate(
            [
                jnp.concatenate(
                    [
                        along_y[
                            cs_x * 1024 + jy * 64 + half * 32 : cs_x * 1024 + jy * 64 + half * 32 + 32,
                            :,
                        ]
                        for jy in range(part * 8, part * 8 + 8)
                    ],
                    0,
                ).astype(BF16)
                for cs_x in range(4)
            ],
            1,
        )
        modes_z[half, part] = nt_dot(zt_ref[...], rows)


def join_halves(modes_z, slab_modes):
    for jy in range(16):
        lanes = slice((jy % 8) * 32, (jy % 8) * 32 + 32)
        block = jnp.concatenate(
            [
                modes_z[half, jy // 8, re * 32 : re * 32 + 32, lanes]
                for re in range(2)
                for half in range(2)
            ],
            1,
        )
        slab_modes[jy * 4 : jy * 4 + 4] = block.reshape(4, 8, 128).astype(BF16)


def greetings(barrier, me, grp, low, z):
    def tell(device):
        pl.semaphore_signal(barrier, inc=1, device_id=device, device_id_type=MESH)

    calls = []
    for dz in (4, 3, 5, 2, 6, 1, 7, 0):
        other_z = lax.rem(z + dz, N_Z) * N_LOW
        for g_step in (2, 1, 3):
            calls.append(
                functools.partial(
                    tell, {"grp": lax.rem(grp + g_step, N_GRP), "slab": other_z + low}
                )
            )
        for step in (4, 5, 2, 3, 6, 7, 1, 0):
            if dz or step:
                calls.append(
                    functools.partial(tell, {"slab": other_z + lax.rem(low + step, N_LOW)})
                )
    return calls


def send_all(source, target, send_sem, recv_sem, me):
    low = lax.rem(me, N_LOW)
    z = me // N_LOW
    for dz in (4, 3, 5, 2, 6, 1, 7, 0):

        def go(step, carry):
            other = lax.rem(z + dz, N_Z) * N_LOW + lax.rem(low + step, N_LOW)
            pltpu.make_async_remote_copy(
                src_ref=source.at[other],
                dst_ref=target.at[me],
                send_sem=send_sem,
                recv_sem=recv_sem,
                device_id={"slab": other},
                device_id_type=MESH,
            ).start()
            return carry

        lax.fori_loop(1 if dz == 0 else 0, N_LOW, go, 0)
    target[pl.ds(me, 1)] = source[pl.ds(me, 1)]


def wait_blocks(source, target, send_sem, recv_sem, count, me):
    pltpu.make_async_remote_copy(
        src_ref=source.at[pl.ds(0, count)],
        dst_ref=target.at[pl.ds(0, count)],
        send_sem=send_sem,
        recv_sem=recv_sem,
        device_id={"slab": me},
        device_id_type=MESH,
    ).wait()


def send_grp(source, target, send_sem, recv_sem, grp, by_target):
    for step in range(1, N_GRP):
        other = lax.rem(grp + step, N_GRP)
        pltpu.make_async_remote_copy(
            src_ref=source.at[other] if by_target else source.at[grp],
            dst_ref=target.at[grp],
            send_sem=send_sem,
            recv_sem=recv_sem,
            device_id={"grp": other},
            device_id_type=MESH,
        ).start()


def x_modes(pencil, tx_ref):
    rows = pencil[...].astype(F32).reshape(512, 128).astype(BF16)
    both = jnp.dot(tx_ref[...], rows, preferred_element_type=F32)
    return both[:64] + turned(both[64:], 1.0, -1.0)


def local_step(part, held, kron, bias_rows, field_rows, local):
    y_at = pl.multiple_of(16 * part, 16)
    halves = [held[:, x, pl.ds(y_at, 16), :].astype(F32) for x in range(2)]
    for half in range(2):
        rows = jnp.concatenate(
            [block[:, 8 * half : 8 * half + 8].reshape(512, 128) for block in halves], 1
        ).astype(BF16)
        field_rows[part, :, half * 256 : half * 256 + 256] = rows
        got = jnp.dot(kron[...], rows, preferred_element_type=F32)
        added = bias_rows[...]
        local[:, pl.ds(pl.multiple_of(y_at + 8 * half, 8), 8), :] = got.reshape(
            64, 8, 256
        ) + jnp.concatenate([added, added], 2)


def scale_rows(grp, direction_ref, shift_ref):
    number = grp + 1
    gray_code = number ^ (number >> 1)
    bits = shift_ref[...]
    for bit_pos in range(N_GRP.bit_length()):
        bits = bits ^ (direction_ref[bit_pos : bit_pos + 1, :] * ((gray_code >> bit_pos) & 1))
    scale = 0.5 + bits.astype(F32) * 2.0 ** (-BITS)
    return jnp.broadcast_to(jnp.concatenate([scale, scale], 1), (8, 128))


def fill_kron(wl_ref, scale_row, kron):
    local = (wl_ref[...].astype(F32) * scale_row[0:1, 0:64]).astype(BF16)
    pick = (
        lax.broadcasted_iota(jnp.int32, (64, 512), 0)
        == lax.broadcasted_iota(jnp.int32, (64, 512), 1) // 8
    )
    wide = jnp.dot(local, pick.astype(F32).astype(BF16), preferred_element_type=F32).astype(BF16)
    same = (
        lax.broadcasted_iota(jnp.int32, (64, 512), 0) % 8
        == lax.broadcasted_iota(jnp.int32, (64, 512), 1) % 8
    )
    row_ids = lax.broadcasted_iota(jnp.int32, (64, 64), 0) // 8
    col_ids = lax.broadcasted_iota(jnp.int32, (64, 64), 1)
    for octet in range(8):
        rows_of = (row_ids + 8 * octet == col_ids).astype(F32).astype(BF16)
        tall = jnp.dot(rows_of, wide, preferred_element_type=F32)
        kron[octet * 64 : octet * 64 + 64, :] = jnp.where(same, tall, 0.0).astype(BF16)


def fill_along_z(landed, ez_ref, along_z):
    for quarter in range(4):
        rows = landed[quarter * 16 : quarter * 16 + 16].astype(F32).reshape(128, 128)
        turn = rows.T
        per_c = jnp.concatenate(
            [
                jnp.concatenate(
                    [turn[0:64, jy * 32 : jy * 32 + 32], turn[64:128, jy * 32 : jy * 32 + 32]], 1
                )
                for jy in range(4)
            ],
            0,
        ).astype(BF16)
        got = jnp.dot(per_c, ez_ref[...], preferred_element_type=F32)
        for jy in range(4):
            for cs in range(2):
                for x in range(2):
                    start = x * 2048 + cs * 16 + quarter * 4 + jy
                    lane = cs * 256 + x * 128
                    along_z[pl.ds(start, 64, stride=32), :] = got[
                        jy * 64 : jy * 64 + 64, lane : lane + 128
                    ]


def synthesis(group, along_z, local, ey_ref, pre_act):
    rows = jnp.concatenate(
        [
            along_z[pl.ds(x * 2048 + 256 * group + 64 * pair, 64), :].astype(BF16)
            for pair in range(4)
            for x in range(2)
        ],
        1,
    )
    got = jnp.dot(ey_ref[...], rows, preferred_element_type=F32)
    for pair in range(4):
        for c2 in range(2):
            at = slice(c2 * 128, c2 * 128 + 128)
            lanes = slice(pair * 256, pair * 256 + 256)
            pre_act[at, lanes] = (
                got[at, lanes] + local[8 * group + 2 * pair + c2]
            ).astype(BF16)


def activation(group, pre_act, cotan_in, out_held, cotan_pre):
    for pair in range(4):
        for c2 in range(2):
            for x in range(2):
                channel = 8 * group + 2 * pair + c2
                at = slice(c2 * 128, c2 * 128 + 128)
                lanes = slice(pair * 256 + x * 128, pair * 256 + x * 128 + 128)
                pre = pre_act[at, lanes]
                square = pre * pre
                inner = pre * (1.0 + GELU_A * square)
                tanh = jnp.tanh(inner.astype(F32) * GELU_K)
                above = 1.0 + tanh
                bell = (above * (1.0 - tanh)).astype(BF16)
                above = above.astype(BF16)
                out_held[channel, x] = (0.5 * pre) * above
                slope = above + bell * (pre * (GELU_K + (3.0 * GELU_K * GELU_A) * square))
                cotan_pre[at, lanes] = slope * cotan_in[channel, x]


def gradient_modes(group, cotan_pre, ty_ref, cotan_rows, along_y):
    got = jnp.dot(ty_ref[...], cotan_pre[...], preferred_element_type=F32)
    for pair in range(4):
        store_along_y(along_y, got[:, pair * 256 : pair * 256 + 256], 8 * group + 2 * pair)
    for pair in range(4):
        for x in range(2):
            lanes = slice(pair * 256 + x * 128, pair * 256 + x * 128 + 128)
            wide = cotan_pre[:, lanes].astype(F32)
            for y8 in range(16):
                block = jnp.concatenate(
                    [wide[c2 * 128 + 8 * y8 : c2 * 128 + 8 * y8 + 8] for c2 in range(2)], 0
                )
                lane = (y8 % 2) * 256 + x * 128
                cotan_rows[
                    y8 // 2, pl.ds(64 * group + 16 * pair, 16), lane : lane + 128
                ] = block.astype(BF16)


def local_grad(grad):
    same = (
        lax.broadcasted_iota(jnp.int32, (256, 512), 0) % 8
        == lax.broadcasted_iota(jnp.int32, (256, 512), 1) % 8
    )
    kept = jnp.where(same, grad, 0.0)
    high = kept.astype(BF16)
    low = (kept - high.astype(F32)).astype(BF16)
    pick = (
        lax.broadcasted_iota(jnp.int32, (512, 64), 0) // 8
        == lax.broadcasted_iota(jnp.int32, (512, 64), 1)
    )
    pick = pick.astype(F32).astype(BF16)
    got = jnp.dot(high, pick, preferred_element_type=F32) + jnp.dot(
        low, pick, preferred_element_type=F32
    )
    return jnp.sum(got.reshape(32, 8, 64), axis=1)


def fill_terms(shifted_modes, terms):
    turn = shifted_modes[...].T
    columns = jnp.concatenate([turn[0:64], turn[64:128]], 1)
    mode = lax.broadcasted_iota(jnp.int32, (64, 128), 1) % 16
    for k in range(16):
        terms[k * 64 : k * 64 + 64, :] = jnp.where(mode == k, columns, 0.0).astype(BF16)


def weight_terms(gathered_g, terms, d_spec):
    rows = gathered_g[...].reshape(64, 128)
    both = jnp.concatenate([rows, turned(rows.astype(F32), 1.0, -1.0).astype(BF16)], 0)
    got = jnp.dot(terms[...], both, preferred_element_type=F32)
    d_spec[...] = got.reshape(16, 64, 128)


def layer_kernel(
    field, cotan, w_hbm, wl_hbm, direction_hbm, shift_hbm, bias_ref,
    ty_hbm, ztf_hbm, ztb_hbm, tx_hbm, txb_hbm, ey_hbm, ez_hbm,
    out_hbm, spec_hbm, sums_out,
    ty_ref, ztf_ref, ztb_ref, tx_ref, txb_ref, ey_ref, ez_ref, w_ref, wl_ref, direction_ref, shift_ref, scale_ref,
    held, cotan_in, out_held, field_rows, cotan_rows, local, along_y, along_z, kron, w_two,
    d_spec, terms, modes_z, grad, pre_even, pre_odd, cotan_even, cotan_odd, bias_rows,
    slab_modes, pencil, mixed, gathered, back, landed, slab_g, pencil_g, mixed_g, gathered_g,
    all_modes, shifted_modes, scale_own, scale_all, own_sums, first, second, second_own, third,
    field_sems, cotan_sems, table_sems, out_sems, send_sems, recv_sems,
):
    me = lax.axis_index("slab")
    grp = lax.axis_index("grp")
    low = lax.rem(me, N_LOW)
    z = me // N_LOW
    barrier = pltpu.get_barrier_semaphore()
    small = [
        (ty_hbm, ty_ref), (ztf_hbm, ztf_ref), (direction_hbm, direction_ref), (wl_hbm, wl_ref),
        (w_hbm, w_ref), (tx_hbm, tx_ref), (txb_hbm, txb_ref), (ey_hbm, ey_ref),
        (ez_hbm, ez_ref), (ztb_hbm, ztb_ref), (shift_hbm, shift_ref),
    ]
    copies = [
        pltpu.make_async_copy(source, target, table_sems.at[at])
        for at, (source, target) in enumerate(small)
    ]
    for copy in copies[:2]:
        copy.start()
    fetch_field(field, held, field_sems)
    for copy in copies[2:]:
        copy.start()
    calls = greetings(barrier, me, grp, low, z)

    for call in calls[:15]:
        call()
    copies[0].wait()

    for part in range(8):
        for call in calls[15 * part + 15 : 15 * part + 30]:
            call()
        wait_field(field, held, field_sems, part)
        rows = jnp.concatenate(
            [
                jnp.concatenate([held[8 * part + 2 * pair + c2, x] for c2 in range(2)], 0)
                for pair in range(4)
                for x in range(2)
            ],
            1,
        )
        got = jnp.dot(ty_ref[...], rows, preferred_element_type=F32)
        for pair in range(4):
            store_along_y(along_y, got[:, pair * 256 : pair * 256 + 256], 8 * part + 2 * pair)
        if part == 3:
            copies[1].wait()
            along_z_half(0, along_y, ztf_ref, modes_z)
    along_z_half(1, along_y, ztf_ref, modes_z)
    join_halves(modes_z, slab_modes)
    copies[2].wait()
    copies[10].wait()
    scale_ref[...] = scale_rows(grp, direction_ref, shift_ref)
    scale_own[grp] = scale_ref[...]
    scale_all[grp] = scale_ref[...]
    pl.semaphore_wait(barrier, N_SLAB - 1 + N_GRP - 1 + (N_GRP - 1) * (N_Z - 1))
    send_all(slab_modes, pencil, send_sems.at[0], recv_sems.at[0], me)
    send_grp(scale_own, scale_all, send_sems.at[1], recv_sems.at[1], grp, False)
    fetch_field(cotan, cotan_in, cotan_sems)

    copies[3].wait()
    copies[4].wait()
    for k in range(16):
        block = w_ref[k].astype(F32)
        w_two[k * 128 : k * 128 + 64, :] = w_ref[k]
        w_two[k * 128 + 64 : k * 128 + 128, :] = turned(block, -1.0, 1.0).astype(BF16)
    fill_kron(wl_ref, scale_ref[...], kron)
    for channel in range(CH):
        bias_rows[channel] = jnp.full((8, 128), bias_ref[channel], F32)

    def local_some(part, carry):
        local_step(part, held, kron, bias_rows, field_rows, local)
        return carry

    lax.fori_loop(0, 3, local_some, 0)
    pltpu.make_async_remote_copy(
        src_ref=scale_own.at[pl.ds(0, N_GRP - 1)],
        dst_ref=scale_all.at[pl.ds(0, N_GRP - 1)],
        send_sem=send_sems.at[1],
        recv_sem=recv_sems.at[1],
        device_id={"slab": me},
        device_id_type=MESH,
    ).wait()
    copies[5].wait()
    copies[6].wait()
    wait_blocks(slab_modes, pencil, send_sems.at[0], recv_sems.at[0], N_SLAB - 1, me)

    all_modes[...] = x_modes(pencil, tx_ref) * (1.0 / math.sqrt(NX * NY * NZ))
    own = all_modes[pl.ds(pl.multiple_of(16 * grp, 16), 16), :]
    shifted = jnp.concatenate([own * scale_all[s, 0:1, :] for s in range(N_GRP)], 0)
    shifted_modes[...] = shifted
    row_mode = lax.broadcasted_iota(jnp.int32, (64, 128), 0) % 16
    spread = jnp.concatenate(
        [jnp.where(row_mode == k, shifted, 0.0).astype(BF16) for k in range(16)], 1
    )
    mixed[...] = (
        jnp.dot(spread, w_two[...], preferred_element_type=F32).astype(BF16).reshape(4, 16, 128)
    )
    send_grp(mixed, gathered, send_sems.at[2], recv_sems.at[2], grp, True)
    gathered[pl.ds(grp, 1)] = mixed[pl.ds(grp, 1)]
    lax.fori_loop(3, 5, local_some, 0)
    wait_blocks(mixed, gathered, send_sems.at[2], recv_sems.at[2], N_GRP - 1, me)
    full = gathered[...].reshape(64, 128)
    both = jnp.concatenate([full, turned(full.astype(F32), -1.0, 1.0).astype(BF16)], 0)
    back[...] = (
        jnp.dot(txb_ref[...], both, preferred_element_type=F32).reshape(64, 8, 128).astype(BF16)
    )
    send_all(back, landed, send_sems.at[3], recv_sems.at[3], me)
    lax.fori_loop(5, 8, local_some, 0)
    fill_terms(shifted_modes, terms)
    for copy in copies[7:10]:
        copy.wait()
    for part in range(8):
        wait_field(cotan, cotan_in, cotan_sems, part)
    wait_blocks(back, landed, send_sems.at[3], recv_sems.at[3], N_SLAB - 1, me)

    fill_along_z(landed, ez_ref, along_z)

    slots = ((pre_even, cotan_even), (pre_odd, cotan_odd))
    for step in range(10):
        if step < 8:
            synthesis(step, along_z, local, ey_ref, slots[step % 2][0])
        if 0 < step < 9:
            pre_act, cotan_pre = slots[(step - 1) % 2]
            activation(step - 1, pre_act, cotan_in, out_held, cotan_pre)
            rows = pl.ds(8 * (step - 1), 8)
            pltpu.make_async_copy(
                out_held.at[rows], out_hbm.at[rows], out_sems.at[step - 1]
            ).start()
        if step > 1:
            gradient_modes(
                step - 2, slots[step % 2][1], ty_ref, cotan_rows, along_y
            )
        if step == 5:
            along_z_half(0, along_y, ztb_ref, modes_z)
            grad[...] = jnp.zeros_like(grad)
        if step > 5:
            for part in (2 * step - 12, 2 * step - 11):
                grad[...] += nt_dot(cotan_rows[part, 0:256, :], field_rows[part])

    d_top = local_grad(grad[...])
    bottom = jnp.zeros((256, 512), F32)
    for part in range(8):
        bottom = bottom + nt_dot(cotan_rows[part, 256:512, :], field_rows[part])
    d_local = jnp.concatenate([d_top, local_grad(bottom)], 0)
    d_local = d_local * (scale_ref[0:1, 0:64] * GRAD_SCALE)
    lanes = along_y[0:64, :] + along_y[1024:1088, :]
    d_bias = nt_dot(jnp.full((8, 128), GRAD_SCALE, F32), lanes, lax.Precision.HIGHEST)
    side = jnp.concatenate([d_bias, jnp.zeros((56, 64), F32)], 0)
    own_sums[...] = jnp.concatenate([d_local, side], 1).reshape(8, 8, 128)

    def scatter(step, carry):
        other = lax.rem(low + step, N_LOW)
        pltpu.make_async_remote_copy(
            src_ref=own_sums.at[other],
            dst_ref=first.at[low],
            send_sem=send_sems.at[4],
            recv_sem=recv_sems.at[4],
            device_id={"slab": z * N_LOW + other},
            device_id_type=MESH,
        ).start()
        return carry

    lax.fori_loop(1, N_LOW, scatter, 0)
    first[pl.ds(low, 1)] = own_sums[pl.ds(low, 1)]
    along_z_half(1, along_y, ztb_ref, modes_z)
    join_halves(modes_z, slab_g)
    send_all(slab_g, pencil_g, send_sems.at[5], recv_sems.at[5], me)
    wait_blocks(own_sums, first, send_sems.at[4], recv_sems.at[4], N_LOW - 1, me)
    part_sum = jnp.sum(first[...], axis=0, keepdims=True)
    mine = grp * N_Z + z
    second[pl.ds(mine, 1)] = part_sum
    second_own[...] = part_sum
    for g_step in (2, 1, 3, 0):

        def spread_sum(step, carry):
            pltpu.make_async_remote_copy(
                src_ref=second_own.at[0],
                dst_ref=second.at[mine],
                send_sem=send_sems.at[6],
                recv_sem=recv_sems.at[6],
                device_id={
                    "grp": lax.rem(grp + g_step, N_GRP),
                    "slab": lax.rem(z + step, N_Z) * N_LOW + low,
                },
                device_id_type=MESH,
            ).start()
            return carry

        lax.fori_loop(1 if g_step == 0 else 0, N_Z, spread_sum, 0)
    wait_blocks(slab_g, pencil_g, send_sems.at[5], recv_sems.at[5], N_SLAB - 1, me)
    mixed_g[...] = x_modes(pencil_g, tx_ref).astype(BF16).reshape(4, 16, 128)
    send_grp(mixed_g, gathered_g, send_sems.at[7], recv_sems.at[7], grp, True)
    gathered_g[pl.ds(grp, 1)] = mixed_g[pl.ds(grp, 1)]
    wait_blocks(second, second, send_sems.at[6], recv_sems.at[6], N_GRP * N_Z - 1, me)
    third[pl.ds(low, 1)] = jnp.sum(second[...], axis=0, keepdims=True)

    def collect(step, carry):
        pltpu.make_async_remote_copy(
            src_ref=third.at[low],
            dst_ref=third.at[low],
            send_sem=send_sems.at[8],
            recv_sem=recv_sems.at[8],
            device_id={"slab": z * N_LOW + lax.rem(low + step, N_LOW)},
            device_id_type=MESH,
        ).start()
        return carry

    lax.fori_loop(1, N_LOW, collect, 0)
    wait_blocks(mixed_g, gathered_g, send_sems.at[7], recv_sems.at[7], N_GRP - 1, me)
    weight_terms(gathered_g, terms, d_spec)
    spec_copy = pltpu.make_async_copy(d_spec, spec_hbm, out_sems.at[8])
    spec_copy.start()
    for part in range(8):
        rows = pl.ds(8 * part, 8)
        pltpu.make_async_copy(out_held.at[rows], out_hbm.at[rows], out_sems.at[part]).wait()
    wait_blocks(third, third, send_sems.at[8], recv_sems.at[8], N_LOW - 1, me)
    sums_out[...] = third[...]
    spec_copy.wait()


def layer_call(field, cotangent, w_spec, w_local, direction, shift, bias):
    vmem = pl.BlockSpec(memory_space=pltpu.VMEM)
    hbm = pl.BlockSpec(memory_space=pl.ANY)
    tables = (
        table_ty(), table_zt(False), table_zt(True), table_tx(),
        np.ascontiguousarray(table_tx().T), table_ey(), table_ez(),
    )
    cells = (64, 2, 128, 128)
    blocks = pltpu.VMEM((64, 8, 128), BF16)
    quads = pltpu.VMEM((4, 16, 128), BF16)
    return pl.pallas_call(
        layer_kernel,
        out_shape=(
            jax.ShapeDtypeStruct(cells, BF16),
            jax.ShapeDtypeStruct((16, 64, 128), F32),
            jax.ShapeDtypeStruct((8, 8, 128), F32),
        ),
        in_specs=[hbm] * 6 + [pl.BlockSpec(memory_space=pltpu.SMEM)] + [hbm] * 7,
        out_specs=(hbm, hbm, vmem),
        scratch_shapes=[pltpu.VMEM(table.shape, BF16) for table in tables]
        + [
            pltpu.VMEM((16, 64, 128), BF16),
            pltpu.VMEM((64, 64), BF16),
            pltpu.VMEM((BITS, 64), jnp.int32),
            pltpu.VMEM((1, 64), jnp.int32),
            pltpu.VMEM((8, 128), F32),
            pltpu.VMEM(cells, BF16),
            pltpu.VMEM(cells, BF16),
            pltpu.VMEM(cells, BF16),
            pltpu.VMEM((8, 512, 512), BF16),
            pltpu.VMEM((8, 512, 512), BF16),
            pltpu.VMEM((64, 128, 256), F32),
            pltpu.VMEM((4096, 128), F32),
            pltpu.VMEM((4096, 128), F32),
            pltpu.VMEM((512, 512), BF16),
            pltpu.VMEM((2048, 128), BF16),
            pltpu.VMEM((16, 64, 128), F32),
            pltpu.VMEM((1024, 128), BF16),
            pltpu.VMEM((2, 2, 64, 256), F32),
            pltpu.VMEM((256, 512), F32),
            pltpu.VMEM((256, 1024), BF16),
            pltpu.VMEM((256, 1024), BF16),
            pltpu.VMEM((256, 1024), BF16),
            pltpu.VMEM((256, 1024), BF16),
            pltpu.VMEM((64, 8, 128), F32),
            blocks, blocks, quads, quads, blocks, blocks, blocks, blocks, quads, quads,
            pltpu.VMEM((64, 128), F32),
            pltpu.VMEM((64, 128), F32),
            pltpu.VMEM((4, 8, 128), F32),
            pltpu.VMEM((4, 8, 128), F32),
            pltpu.VMEM((8, 8, 128), F32),
            pltpu.VMEM((8, 8, 128), F32),
            pltpu.VMEM((32, 8, 128), F32),
            pltpu.VMEM((1, 8, 128), F32),
            pltpu.VMEM((8, 8, 128), F32),
            pltpu.SemaphoreType.DMA((8,)),
            pltpu.SemaphoreType.DMA((8,)),
            pltpu.SemaphoreType.DMA((11,)),
            pltpu.SemaphoreType.DMA((9,)),
            pltpu.SemaphoreType.DMA((9,)),
            pltpu.SemaphoreType.DMA((9,)),
        ],
        compiler_params=pltpu.CompilerParams(
            collective_id=0, has_side_effects=True, vmem_limit_bytes=58 * MIB
        ),
    )(field, cotangent, w_spec, w_local, direction, shift, bias, *tables)


def results_kernel(
    out_hbm, spec_hbm, sums_hbm,
    output, spec_out, d_local, d_bias,
    held, spec_held, sums_ref, in_sems, out_sems,
):
    moves = []
    for part in range(8):
        rows = pl.ds(8 * part, 8)
        moves.append((out_hbm.at[rows], held.at[rows], output.at[rows]))
    for part in range(2):
        rows = pl.ds(8 * part, 8)
        moves.append((spec_hbm.at[rows], spec_held.at[rows], spec_out.at[rows]))
    ins = [
        pltpu.make_async_copy(source, middle, in_sems.at[at])
        for at, (source, middle, _) in enumerate(moves)
    ]
    outs = [
        pltpu.make_async_copy(middle, target, out_sems.at[at])
        for at, (_, middle, target) in enumerate(moves)
    ]
    sums_copy = pltpu.make_async_copy(sums_hbm, sums_ref, in_sems.at[10])
    for copy in ins:
        copy.start()
    sums_copy.start()
    for before, after in zip(ins, outs):
        before.wait()
        after.start()
    sums_copy.wait()
    sums = sums_ref[...].reshape(64, 128)
    d_local[...] = sums[:, 0:64]
    d_bias[...] = sums[0:1, 64:128]
    for copy in outs:
        copy.wait()


def results_call(out, d_spec, sums):
    vmem = pl.BlockSpec(memory_space=pltpu.VMEM)
    hbm = pl.BlockSpec(memory_space=pl.ANY)
    return pl.pallas_call(
        results_kernel,
        out_shape=(
            jax.ShapeDtypeStruct(out.shape, BF16),
            jax.ShapeDtypeStruct(d_spec.shape, F32),
            jax.ShapeDtypeStruct((64, 64), F32),
            jax.ShapeDtypeStruct((1, 64), F32),
        ),
        in_specs=[hbm] * 3,
        out_specs=(hbm, hbm, vmem, vmem),
        scratch_shapes=[
            pltpu.VMEM(out.shape, BF16),
            pltpu.VMEM(d_spec.shape, F32),
            pltpu.VMEM((8, 8, 128), F32),
            pltpu.SemaphoreType.DMA((11,)),
            pltpu.SemaphoreType.DMA((10,)),
        ],
        compiler_params=pltpu.CompilerParams(vmem_limit_bytes=58 * MIB),
    )(out, d_spec, sums)


def shards(base_field, cotangent, w_spec, w_local, bias, direction, shift):
    out, d_spec, sums = layer_call(
        base_field, cotangent[0], w_spec.reshape(16, 64, 128), w_local, direction.T, shift, bias
    )
    output, d_spec, d_local, d_bias = results_call(out, d_spec, sums)
    return (output[None], d_spec.reshape(4, 4, 64, 128), d_local, d_bias.reshape(64))


def solution(mesh):
    return jax.shard_map(
        shards,
        mesh=mesh,
        in_specs=(
            P(None, "slab", None, None),
            P("grp", None, "slab", None, None),
            P("grp", "slab", None, None),
            P(),
            P(),
            P(),
            P("grp", None),
        ),
        out_specs=(P("grp", None, "slab", None, None), P("grp", "slab", None, None), P(), P()),
        check_vma=False,
    )
```

```python
import functools
import math

import jax
import jax.numpy as jnp
import ml_dtypes
import numpy as np
from jax import lax
from jax.experimental import pallas as pl
from jax.experimental.pallas import tpu as pltpu
from jax.sharding import PartitionSpec as P

CH = 64
NX = 128
NY = 128
NZ = 128
MODES = 16
BITS = 30
N_GRP = 4
N_SLAB = 64
N_LOW = 8
N_Z = 8
MESH = pl.DeviceIdType.MESH
F32 = jnp.float32
BF16 = jnp.bfloat16
MIB = 1024 * 1024
GELU_K = math.sqrt(2.0 / math.pi)
GELU_A = 0.044715
GRAD_SCALE = 0.5 / math.sqrt(N_GRP * NX * NY * NZ)


def waves(length, half):
    ids = np.arange(MODES)
    if not half:
        ids = np.where(ids < MODES // 2, ids, length - MODES + ids)
    angles = 2.0 * math.pi / length * (ids[:, None] * np.arange(length)[None, :] % length)
    return np.cos(angles), np.sin(angles)


def as_bf16(table):
    return np.asarray(table, np.float32).astype(ml_dtypes.bfloat16)


def table_ty():
    cos_y, sin_y = waves(NY, False)
    out = np.zeros((2, 2, MODES, 2, NY))
    for c2 in range(2):
        out[0, c2, :, c2] = cos_y
        out[1, c2, :, c2] = sin_y
    return as_bf16(out.reshape(64, 256))


def weights_z(backward):
    return np.where(np.arange(MODES) == 0, 1.0, 2.0 if backward else 1.0)[:, None]


def table_zt(backward):
    cos_z, sin_z = waves(NZ, True)
    weight = weights_z(backward)
    if backward:
        weight = weight * GRAD_SCALE
    cos_z = (weight * cos_z).reshape(4, 4, NZ)
    sin_z = (weight * sin_z).reshape(4, 4, NZ)
    out = np.zeros((2, 4, 2, 4, 2, 2, NZ))
    for x in range(2):
        out[0, :, x, :, 0, x] = cos_z
        out[0, :, x, :, 1, x] = -sin_z
        out[1, :, x, :, 0, x] = -sin_z
        out[1, :, x, :, 1, x] = -cos_z
    return as_bf16(out.reshape(64, 512))


def table_tx():
    cos_x, sin_x = waves(NX, False)
    out = np.zeros((2, MODES, 4, NX, 4))
    for m in range(4):
        out[0, :, m, :, m] = cos_x
        out[1, :, m, :, m] = sin_x
    return as_bf16(out.reshape(128, 512))


def table_ey():
    cos_y, sin_y = waves(NY, False)
    out = np.zeros((2, NY, 2, 2, MODES))
    for c2 in range(2):
        out[c2, :, c2, 0] = cos_y.T
        out[c2, :, c2, 1] = -sin_y.T
    return as_bf16(out.reshape(256, 64))


def table_ez():
    cos_z, sin_z = waves(NZ, True)
    weight = weights_z(True) / math.sqrt(MODES**3)
    cos_z = (weight * cos_z).reshape(4, 4, NZ)
    sin_z = (weight * sin_z).reshape(4, 4, NZ)
    out = np.zeros((2, 4, 2, 4, 2, 2, NZ))
    for x in range(2):
        out[0, :, x, :, 0, x] = cos_z
        out[1, :, x, :, 0, x] = -sin_z
        out[0, :, x, :, 1, x] = sin_z
        out[1, :, x, :, 1, x] = cos_z
    return as_bf16(out.reshape(64, 512))


def lane_sign(rows, first, second):
    lane = lax.broadcasted_iota(jnp.int32, (rows, 128), 1)
    return jnp.where(lane < 64, first, second).astype(F32)


def turned(rows, first, second):
    return pltpu.roll(rows, 64, 1) * lane_sign(rows.shape[0], first, second)


def nt_dot(left, right, precision=None):
    return lax.dot_general(
        left, right, (((1,), (1,)), ((), ())), preferred_element_type=F32, precision=precision
    )


def fetch_field(field, held, sems):
    for part in range(8):
        rows = pl.ds(8 * part, 8)
        pltpu.make_async_copy(field.at[rows], held.at[rows], sems.at[part]).start()


def wait_field(field, held, sems, part):
    rows = pl.ds(8 * part, 8)
    pltpu.make_async_copy(field.at[rows], held.at[rows], sems.at[part]).wait()


def store_along_y(along_y, got, first):
    for cs in range(2):
        for c2 in range(2):
            at = cs * 32 + c2 * 16
            for x in range(2):
                start = (2 * cs + x) * 1024 + first + c2
                along_y[pl.ds(start, 16, stride=64), :] = got[
                    at : at + 16, x * 128 : x * 128 + 128
                ]


def along_z_half(half, along_y, zt_ref, modes_z):
    for part in range(2):
        rows = jnp.concatenate(
            [
                jnp.concatenate(
                    [
                        along_y[
                            cs_x * 1024 + jy * 64 + half * 32 : cs_x * 1024 + jy * 64 + half * 32 + 32,
                            :,
                        ]
                        for jy in range(part * 8, part * 8 + 8)
                    ],
                    0,
                ).astype(BF16)
                for cs_x in range(4)
            ],
            1,
        )
        modes_z[half, part] = nt_dot(zt_ref[...], rows)


def join_halves(modes_z, slab_modes):
    for jy in range(16):
        lanes = slice((jy % 8) * 32, (jy % 8) * 32 + 32)
        block = jnp.concatenate(
            [
                modes_z[half, jy // 8, re * 32 : re * 32 + 32, lanes]
                for re in range(2)
                for half in range(2)
            ],
            1,
        )
        slab_modes[jy * 4 : jy * 4 + 4] = block.reshape(4, 8, 128).astype(BF16)


def greetings(barrier, me, grp, low, z):
    def tell(device):
        pl.semaphore_signal(barrier, inc=1, device_id=device, device_id_type=MESH)

    calls = []
    for dz in (4, 3, 5, 2, 6, 1, 7, 0):
        other_z = lax.rem(z + dz, N_Z) * N_LOW
        for g_step in (2, 1, 3):
            calls.append(
                functools.partial(
                    tell, {"grp": lax.rem(grp + g_step, N_GRP), "slab": other_z + low}
                )
            )
        for step in (4, 5, 2, 3, 6, 7, 1, 0):
            if dz or step:
                calls.append(
                    functools.partial(tell, {"slab": other_z + lax.rem(low + step, N_LOW)})
                )
    return calls


def send_all(source, target, send_sem, recv_sem, me):
    low = lax.rem(me, N_LOW)
    z = me // N_LOW
    for dz in (4, 3, 5, 2, 6, 1, 7, 0):

        def go(step, carry):
            other = lax.rem(z + dz, N_Z) * N_LOW + lax.rem(low + step, N_LOW)
            pltpu.make_async_remote_copy(
                src_ref=source.at[other],
                dst_ref=target.at[me],
                send_sem=send_sem,
                recv_sem=recv_sem,
                device_id={"slab": other},
                device_id_type=MESH,
            ).start()
            return carry

        lax.fori_loop(1 if dz == 0 else 0, N_LOW, go, 0)
    target[pl.ds(me, 1)] = source[pl.ds(me, 1)]


def wait_blocks(source, target, send_sem, recv_sem, count, me):
    pltpu.make_async_remote_copy(
        src_ref=source.at[pl.ds(0, count)],
        dst_ref=target.at[pl.ds(0, count)],
        send_sem=send_sem,
        recv_sem=recv_sem,
        device_id={"slab": me},
        device_id_type=MESH,
    ).wait()


def send_grp(source, target, send_sem, recv_sem, grp, by_target):
    for step in (2, 1, 3):
        other = lax.rem(grp + step, N_GRP)
        pltpu.make_async_remote_copy(
            src_ref=source.at[other] if by_target else source.at[grp],
            dst_ref=target.at[grp],
            send_sem=send_sem,
            recv_sem=recv_sem,
            device_id={"grp": other},
            device_id_type=MESH,
        ).start()


def x_modes(pencil, tx_ref):
    rows = pencil[...].astype(F32).reshape(512, 128).astype(BF16)
    both = jnp.dot(tx_ref[...], rows, preferred_element_type=F32)
    return both[:64] + turned(both[64:], 1.0, -1.0)


def local_step(part, held, kron, bias_rows, field_rows, local):
    y_at = pl.multiple_of(16 * part, 16)
    halves = [held[:, x, pl.ds(y_at, 16), :].astype(F32) for x in range(2)]
    for half in range(2):
        rows = jnp.concatenate(
            [block[:, 8 * half : 8 * half + 8].reshape(512, 128) for block in halves], 1
        ).astype(BF16)
        field_rows[part, :, half * 256 : half * 256 + 256] = rows
        got = jnp.dot(kron[...], rows, preferred_element_type=F32)
        added = bias_rows[...]
        local[:, pl.ds(pl.multiple_of(y_at + 8 * half, 8), 8), :] = got.reshape(
            64, 8, 256
        ) + jnp.concatenate([added, added], 2)


def scale_rows(grp, direction_ref, shift_ref):
    number = grp + 1
    gray_code = number ^ (number >> 1)
    bits = shift_ref[...]
    for bit_pos in range(N_GRP.bit_length()):
        bits = bits ^ (direction_ref[bit_pos : bit_pos + 1, :] * ((gray_code >> bit_pos) & 1))
    scale = 0.5 + bits.astype(F32) * 2.0 ** (-BITS)
    return jnp.broadcast_to(jnp.concatenate([scale, scale], 1), (8, 128))


def fill_kron(wl_ref, scale_row, kron):
    local = (wl_ref[...].astype(F32) * scale_row[0:1, 0:64]).astype(BF16)
    pick = (
        lax.broadcasted_iota(jnp.int32, (64, 512), 0)
        == lax.broadcasted_iota(jnp.int32, (64, 512), 1) // 8
    )
    wide = jnp.dot(local, pick.astype(F32).astype(BF16), preferred_element_type=F32).astype(BF16)
    same = (
        lax.broadcasted_iota(jnp.int32, (64, 512), 0) % 8
        == lax.broadcasted_iota(jnp.int32, (64, 512), 1) % 8
    )
    row_ids = lax.broadcasted_iota(jnp.int32, (64, 64), 0) // 8
    col_ids = lax.broadcasted_iota(jnp.int32, (64, 64), 1)
    for octet in range(8):
        rows_of = (row_ids + 8 * octet == col_ids).astype(F32).astype(BF16)
        tall = jnp.dot(rows_of, wide, preferred_element_type=F32)
        kron[octet * 64 : octet * 64 + 64, :] = jnp.where(same, tall, 0.0).astype(BF16)


def fill_along_z(landed, ez_ref, along_z):
    for quarter in range(4):
        rows = landed[quarter * 16 : quarter * 16 + 16].astype(F32).reshape(128, 128)
        turn = rows.T
        per_c = jnp.concatenate(
            [
                jnp.concatenate(
                    [turn[0:64, jy * 32 : jy * 32 + 32], turn[64:128, jy * 32 : jy * 32 + 32]], 1
                )
                for jy in range(4)
            ],
            0,
        ).astype(BF16)
        got = jnp.dot(per_c, ez_ref[...], preferred_element_type=F32)
        for jy in range(4):
            for cs in range(2):
                for x in range(2):
                    start = x * 2048 + cs * 16 + quarter * 4 + jy
                    lane = cs * 256 + x * 128
                    along_z[pl.ds(start, 64, stride=32), :] = got[
                        jy * 64 : jy * 64 + 64, lane : lane + 128
                    ]


def synthesis(group, along_z, local, ey_ref, pre_act):
    rows = jnp.concatenate(
        [
            along_z[pl.ds(x * 2048 + 256 * group + 64 * pair, 64), :].astype(BF16)
            for pair in range(4)
            for x in range(2)
        ],
        1,
    )
    got = jnp.dot(ey_ref[...], rows, preferred_element_type=F32)
    for pair in range(4):
        for c2 in range(2):
            at = slice(c2 * 128, c2 * 128 + 128)
            lanes = slice(pair * 256, pair * 256 + 256)
            pre_act[at, lanes] = (
                got[at, lanes] + local[8 * group + 2 * pair + c2]
            ).astype(BF16)


def activation(group, pre_act, cotan_in, out_held, cotan_pre):
    for pair in range(4):
        for c2 in range(2):
            for x in range(2):
                channel = 8 * group + 2 * pair + c2
                at = slice(c2 * 128, c2 * 128 + 128)
                lanes = slice(pair * 256 + x * 128, pair * 256 + x * 128 + 128)
                pre = pre_act[at, lanes]
                square = pre * pre
                inner = pre * (1.0 + GELU_A * square)
                tanh = jnp.tanh(inner.astype(F32) * GELU_K)
                above = 1.0 + tanh
                bell = (above * (1.0 - tanh)).astype(BF16)
                above = above.astype(BF16)
                out_held[channel, x] = (0.5 * pre) * above
                slope = above + bell * (pre * (GELU_K + (3.0 * GELU_K * GELU_A) * square))
                cotan_pre[at, lanes] = slope * cotan_in[channel, x]


def gradient_modes(group, cotan_pre, ty_ref, cotan_rows, along_y):
    got = jnp.dot(ty_ref[...], cotan_pre[...], preferred_element_type=F32)
    for pair in range(4):
        store_along_y(along_y, got[:, pair * 256 : pair * 256 + 256], 8 * group + 2 * pair)
    for pair in range(4):
        for x in range(2):
            lanes = slice(pair * 256 + x * 128, pair * 256 + x * 128 + 128)
            wide = cotan_pre[:, lanes].astype(F32)
            for y8 in range(16):
                block = jnp.concatenate(
                    [wide[c2 * 128 + 8 * y8 : c2 * 128 + 8 * y8 + 8] for c2 in range(2)], 0
                )
                lane = (y8 % 2) * 256 + x * 128
                cotan_rows[
                    y8 // 2, pl.ds(64 * group + 16 * pair, 16), lane : lane + 128
                ] = block.astype(BF16)


def local_grad(grad):
    same = (
        lax.broadcasted_iota(jnp.int32, (256, 512), 0) % 8
        == lax.broadcasted_iota(jnp.int32, (256, 512), 1) % 8
    )
    kept = jnp.where(same, grad, 0.0)
    high = kept.astype(BF16)
    low = (kept - high.astype(F32)).astype(BF16)
    pick = (
        lax.broadcasted_iota(jnp.int32, (512, 64), 0) // 8
        == lax.broadcasted_iota(jnp.int32, (512, 64), 1)
    )
    pick = pick.astype(F32).astype(BF16)
    got = jnp.dot(high, pick, preferred_element_type=F32) + jnp.dot(
        low, pick, preferred_element_type=F32
    )
    return jnp.sum(got.reshape(32, 8, 64), axis=1)


def fill_terms(shifted_modes, terms):
    turn = shifted_modes[...].T
    columns = jnp.concatenate([turn[0:64], turn[64:128]], 1)
    mode = lax.broadcasted_iota(jnp.int32, (64, 128), 1) % 16
    for k in range(16):
        terms[k * 64 : k * 64 + 64, :] = jnp.where(mode == k, columns, 0.0).astype(BF16)


def weight_terms(gathered_g, terms, d_spec):
    rows = gathered_g[...].reshape(64, 128)
    both = jnp.concatenate([rows, turned(rows.astype(F32), 1.0, -1.0).astype(BF16)], 0)
    got = jnp.dot(terms[...], both, preferred_element_type=F32)
    d_spec[...] = got.reshape(16, 64, 128)


def layer_kernel(
    field, cotan, w_hbm, wl_hbm, direction_hbm, shift_hbm, bias_ref,
    ty_hbm, ztf_hbm, ztb_hbm, tx_hbm, txb_hbm, ey_hbm, ez_hbm,
    out_hbm, spec_hbm, sums_out,
    ty_ref, ztf_ref, ztb_ref, tx_ref, txb_ref, ey_ref, ez_ref, w_ref, wl_ref, direction_ref, shift_ref, scale_ref,
    held, cotan_in, out_held, field_rows, cotan_rows, local, along_y, along_z, kron, w_two,
    d_spec, terms, modes_z, grad, pre_even, pre_odd, cotan_even, cotan_odd, bias_rows,
    slab_modes, pencil, mixed, gathered, back, landed, slab_g, pencil_g, mixed_g, gathered_g,
    all_modes, shifted_modes, scale_own, scale_all, own_sums, first, second, second_own, third,
    field_sems, cotan_sems, table_sems, out_sems, send_sems, recv_sems,
):
    me = lax.axis_index("slab")
    grp = lax.axis_index("grp")
    low = lax.rem(me, N_LOW)
    z = me // N_LOW
    barrier = pltpu.get_barrier_semaphore()
    small = [
        (ty_hbm, ty_ref), (ztf_hbm, ztf_ref), (direction_hbm, direction_ref), (wl_hbm, wl_ref),
        (w_hbm, w_ref), (tx_hbm, tx_ref), (txb_hbm, txb_ref), (ey_hbm, ey_ref),
        (ez_hbm, ez_ref), (ztb_hbm, ztb_ref), (shift_hbm, shift_ref),
    ]
    copies = [
        pltpu.make_async_copy(source, target, table_sems.at[at])
        for at, (source, target) in enumerate(small)
    ]
    for copy in copies[:2]:
        copy.start()
    fetch_field(field, held, field_sems)
    for copy in copies[2:]:
        copy.start()
    calls = greetings(barrier, me, grp, low, z)

    for call in calls[:15]:
        call()
    copies[0].wait()

    for part in range(8):
        for call in calls[15 * part + 15 : 15 * part + 30]:
            call()
        wait_field(field, held, field_sems, part)
        rows = jnp.concatenate(
            [
                jnp.concatenate([held[8 * part + 2 * pair + c2, x] for c2 in range(2)], 0)
                for pair in range(4)
                for x in range(2)
            ],
            1,
        )
        got = jnp.dot(ty_ref[...], rows, preferred_element_type=F32)
        for pair in range(4):
            store_along_y(along_y, got[:, pair * 256 : pair * 256 + 256], 8 * part + 2 * pair)
        if part == 3:
            copies[1].wait()
            along_z_half(0, along_y, ztf_ref, modes_z)
    along_z_half(1, along_y, ztf_ref, modes_z)
    join_halves(modes_z, slab_modes)
    copies[2].wait()
    copies[10].wait()
    scale_ref[...] = scale_rows(grp, direction_ref, shift_ref)
    scale_own[grp] = scale_ref[...]
    scale_all[grp] = scale_ref[...]
    pl.semaphore_wait(barrier, N_SLAB - 1 + N_GRP - 1 + (N_GRP - 1) * (N_Z - 1))
    send_all(slab_modes, pencil, send_sems.at[0], recv_sems.at[0], me)
    send_grp(scale_own, scale_all, send_sems.at[1], recv_sems.at[1], grp, False)
    fetch_field(cotan, cotan_in, cotan_sems)

    copies[3].wait()
    copies[4].wait()
    for k in range(16):
        block = w_ref[k].astype(F32)
        w_two[k * 128 : k * 128 + 64, :] = w_ref[k]
        w_two[k * 128 + 64 : k * 128 + 128, :] = turned(block, -1.0, 1.0).astype(BF16)
    fill_kron(wl_ref, scale_ref[...], kron)
    for channel in range(CH):
        bias_rows[channel] = jnp.full((8, 128), bias_ref[channel], F32)

    def local_some(part, carry):
        local_step(part, held, kron, bias_rows, field_rows, local)
        return carry

    lax.fori_loop(0, 1, local_some, 0)
    pltpu.make_async_remote_copy(
        src_ref=scale_own.at[pl.ds(0, N_GRP - 1)],
        dst_ref=scale_all.at[pl.ds(0, N_GRP - 1)],
        send_sem=send_sems.at[1],
        recv_sem=recv_sems.at[1],
        device_id={"slab": me},
        device_id_type=MESH,
    ).wait()
    copies[5].wait()
    copies[6].wait()
    wait_blocks(slab_modes, pencil, send_sems.at[0], recv_sems.at[0], N_SLAB - 1, me)

    all_modes[...] = x_modes(pencil, tx_ref) * (1.0 / math.sqrt(NX * NY * NZ))
    own = all_modes[pl.ds(pl.multiple_of(16 * grp, 16), 16), :]
    shifted = jnp.concatenate([own * scale_all[s, 0:1, :] for s in range(N_GRP)], 0)
    shifted_modes[...] = shifted
    row_mode = lax.broadcasted_iota(jnp.int32, (64, 128), 0) % 16
    spread = jnp.concatenate(
        [jnp.where(row_mode == k, shifted, 0.0).astype(BF16) for k in range(16)], 1
    )
    mixed[...] = (
        jnp.dot(spread, w_two[...], preferred_element_type=F32).astype(BF16).reshape(4, 16, 128)
    )
    send_grp(mixed, gathered, send_sems.at[2], recv_sems.at[2], grp, True)
    gathered[pl.ds(grp, 1)] = mixed[pl.ds(grp, 1)]
    lax.fori_loop(1, 5, local_some, 0)
    wait_blocks(mixed, gathered, send_sems.at[2], recv_sems.at[2], N_GRP - 1, me)
    full = gathered[...].reshape(64, 128)
    both = jnp.concatenate([full, turned(full.astype(F32), -1.0, 1.0).astype(BF16)], 0)
    back[...] = (
        jnp.dot(txb_ref[...], both, preferred_element_type=F32).reshape(64, 8, 128).astype(BF16)
    )
    send_all(back, landed, send_sems.at[3], recv_sems.at[3], me)
    lax.fori_loop(5, 8, local_some, 0)
    fill_terms(shifted_modes, terms)
    for copy in copies[7:10]:
        copy.wait()
    for part in range(8):
        wait_field(cotan, cotan_in, cotan_sems, part)
    wait_blocks(back, landed, send_sems.at[3], recv_sems.at[3], N_SLAB - 1, me)

    fill_along_z(landed, ez_ref, along_z)

    slots = ((pre_even, cotan_even), (pre_odd, cotan_odd))
    for step in range(10):
        if step < 8:
            synthesis(step, along_z, local, ey_ref, slots[step % 2][0])
        if 0 < step < 9:
            pre_act, cotan_pre = slots[(step - 1) % 2]
            activation(step - 1, pre_act, cotan_in, out_held, cotan_pre)
            rows = pl.ds(8 * (step - 1), 8)
            pltpu.make_async_copy(
                out_held.at[rows], out_hbm.at[rows], out_sems.at[step - 1]
            ).start()
        if step > 1:
            gradient_modes(
                step - 2, slots[step % 2][1], ty_ref, cotan_rows, along_y
            )
        if step == 5:
            along_z_half(0, along_y, ztb_ref, modes_z)
            grad[...] = jnp.zeros_like(grad)
        if step > 5:
            for part in (2 * step - 12, 2 * step - 11):
                grad[...] += nt_dot(cotan_rows[part, 0:256, :], field_rows[part])

    d_top = local_grad(grad[...])
    bottom = jnp.zeros((256, 512), F32)
    for part in range(8):
        bottom = bottom + nt_dot(cotan_rows[part, 256:512, :], field_rows[part])
    d_local = jnp.concatenate([d_top, local_grad(bottom)], 0)
    d_local = d_local * (scale_ref[0:1, 0:64] * GRAD_SCALE)
    lanes = along_y[0:64, :] + along_y[1024:1088, :]
    d_bias = nt_dot(jnp.full((8, 128), GRAD_SCALE, F32), lanes, lax.Precision.HIGHEST)
    side = jnp.concatenate([d_bias, jnp.zeros((56, 64), F32)], 0)
    own_sums[...] = jnp.concatenate([d_local, side], 1).reshape(8, 8, 128)

    def scatter(step, carry):
        other = lax.rem(low + step, N_LOW)
        pltpu.make_async_remote_copy(
            src_ref=own_sums.at[other],
            dst_ref=first.at[low],
            send_sem=send_sems.at[4],
            recv_sem=recv_sems.at[4],
            device_id={"slab": z * N_LOW + other},
            device_id_type=MESH,
        ).start()
        return carry

    lax.fori_loop(1, N_LOW, scatter, 0)
    first[pl.ds(low, 1)] = own_sums[pl.ds(low, 1)]
    along_z_half(1, along_y, ztb_ref, modes_z)
    join_halves(modes_z, slab_g)
    send_all(slab_g, pencil_g, send_sems.at[5], recv_sems.at[5], me)
    wait_blocks(own_sums, first, send_sems.at[4], recv_sems.at[4], N_LOW - 1, me)
    part_sum = jnp.sum(first[...], axis=0, keepdims=True)
    mine = grp * N_Z + z
    second[pl.ds(mine, 1)] = part_sum
    second_own[...] = part_sum
    for g_step in (2, 1, 3, 0):

        def spread_sum(step, carry):
            pltpu.make_async_remote_copy(
                src_ref=second_own.at[0],
                dst_ref=second.at[mine],
                send_sem=send_sems.at[6],
                recv_sem=recv_sems.at[6],
                device_id={
                    "grp": lax.rem(grp + g_step, N_GRP),
                    "slab": lax.rem(z + step, N_Z) * N_LOW + low,
                },
                device_id_type=MESH,
            ).start()
            return carry

        lax.fori_loop(1 if g_step == 0 else 0, N_Z, spread_sum, 0)
    wait_blocks(slab_g, pencil_g, send_sems.at[5], recv_sems.at[5], N_SLAB - 1, me)
    mixed_g[...] = x_modes(pencil_g, tx_ref).astype(BF16).reshape(4, 16, 128)
    send_grp(mixed_g, gathered_g, send_sems.at[7], recv_sems.at[7], grp, True)
    gathered_g[pl.ds(grp, 1)] = mixed_g[pl.ds(grp, 1)]
    wait_blocks(second, second, send_sems.at[6], recv_sems.at[6], N_GRP * N_Z - 1, me)
    third[...] = jnp.sum(second[...], axis=0, keepdims=True)
    own_copy = pltpu.make_async_copy(third.at[0], sums_out.at[low], out_sems.at[9])
    own_copy.start()

    def collect(step, carry):
        pltpu.make_async_remote_copy(
            src_ref=third.at[0],
            dst_ref=sums_out.at[low],
            send_sem=send_sems.at[8],
            recv_sem=recv_sems.at[8],
            device_id={"slab": z * N_LOW + lax.rem(low + step, N_LOW)},
            device_id_type=MESH,
        ).start()
        return carry

    lax.fori_loop(1, N_LOW, collect, 0)
    wait_blocks(mixed_g, gathered_g, send_sems.at[7], recv_sems.at[7], N_GRP - 1, me)
    weight_terms(gathered_g, terms, d_spec)
    spec_copy = pltpu.make_async_copy(d_spec, spec_hbm, out_sems.at[8])
    spec_copy.start()
    for part in range(8):
        rows = pl.ds(8 * part, 8)
        pltpu.make_async_copy(out_held.at[rows], out_hbm.at[rows], out_sems.at[part]).wait()
    wait_blocks(sums_out, sums_out, send_sems.at[8], recv_sems.at[8], N_LOW - 1, me)
    own_copy.wait()
    spec_copy.wait()


def layer_call(field, cotangent, w_spec, w_local, direction, shift, bias):
    hbm = pl.BlockSpec(memory_space=pl.ANY)
    tables = (
        table_ty(), table_zt(False), table_zt(True), table_tx(),
        np.ascontiguousarray(table_tx().T), table_ey(), table_ez(),
    )
    cells = (64, 2, 128, 128)
    blocks = pltpu.VMEM((64, 8, 128), BF16)
    quads = pltpu.VMEM((4, 16, 128), BF16)
    return pl.pallas_call(
        layer_kernel,
        out_shape=(
            jax.ShapeDtypeStruct(cells, BF16),
            jax.ShapeDtypeStruct((16, 64, 128), F32),
            jax.ShapeDtypeStruct((8, 8, 128), F32),
        ),
        in_specs=[hbm] * 6 + [pl.BlockSpec(memory_space=pltpu.SMEM)] + [hbm] * 7,
        out_specs=(hbm,) * 3,
        scratch_shapes=[pltpu.VMEM(table.shape, BF16) for table in tables]
        + [
            pltpu.VMEM((16, 64, 128), BF16),
            pltpu.VMEM((64, 64), BF16),
            pltpu.VMEM((BITS, 64), jnp.int32),
            pltpu.VMEM((1, 64), jnp.int32),
            pltpu.VMEM((8, 128), F32),
            pltpu.VMEM(cells, BF16),
            pltpu.VMEM(cells, BF16),
            pltpu.VMEM(cells, BF16),
            pltpu.VMEM((8, 512, 512), BF16),
            pltpu.VMEM((8, 512, 512), BF16),
            pltpu.VMEM((64, 128, 256), F32),
            pltpu.VMEM((4096, 128), F32),
            pltpu.VMEM((4096, 128), F32),
            pltpu.VMEM((512, 512), BF16),
            pltpu.VMEM((2048, 128), BF16),
            pltpu.VMEM((16, 64, 128), F32),
            pltpu.VMEM((1024, 128), BF16),
            pltpu.VMEM((2, 2, 64, 256), F32),
            pltpu.VMEM((256, 512), F32),
            pltpu.VMEM((256, 1024), BF16),
            pltpu.VMEM((256, 1024), BF16),
            pltpu.VMEM((256, 1024), BF16),
            pltpu.VMEM((256, 1024), BF16),
            pltpu.VMEM((64, 8, 128), F32),
            blocks, blocks, quads, quads, blocks, blocks, blocks, blocks, quads, quads,
            pltpu.VMEM((64, 128), F32),
            pltpu.VMEM((64, 128), F32),
            pltpu.VMEM((4, 8, 128), F32),
            pltpu.VMEM((4, 8, 128), F32),
            pltpu.VMEM((8, 8, 128), F32),
            pltpu.VMEM((8, 8, 128), F32),
            pltpu.VMEM((32, 8, 128), F32),
            pltpu.VMEM((1, 8, 128), F32),
            pltpu.VMEM((1, 8, 128), F32),
            pltpu.SemaphoreType.DMA((8,)),
            pltpu.SemaphoreType.DMA((8,)),
            pltpu.SemaphoreType.DMA((11,)),
            pltpu.SemaphoreType.DMA((10,)),
            pltpu.SemaphoreType.DMA((9,)),
            pltpu.SemaphoreType.DMA((9,)),
        ],
        compiler_params=pltpu.CompilerParams(
            collective_id=0, has_side_effects=True, vmem_limit_bytes=58 * MIB
        ),
    )(field, cotangent, w_spec, w_local, direction, shift, bias, *tables)


def results_kernel(
    out_hbm, spec_hbm, sums_hbm,
    output, spec_out, d_local, d_bias,
    held, spec_held, sums_ref, in_sems, out_sems,
):
    moves = []
    for part in range(8):
        rows = pl.ds(8 * part, 8)
        moves.append((out_hbm.at[rows], held.at[rows], output.at[rows]))
    for part in range(2):
        rows = pl.ds(8 * part, 8)
        moves.append((spec_hbm.at[rows], spec_held.at[rows], spec_out.at[rows]))
    ins = [
        pltpu.make_async_copy(source, middle, in_sems.at[at])
        for at, (source, middle, _) in enumerate(moves)
    ]
    outs = [
        pltpu.make_async_copy(middle, target, out_sems.at[at])
        for at, (_, middle, target) in enumerate(moves)
    ]
    sums_copy = pltpu.make_async_copy(sums_hbm, sums_ref, in_sems.at[10])
    for copy in ins:
        copy.start()
    sums_copy.start()
    for before, after in zip(ins, outs):
        before.wait()
        after.start()
    sums_copy.wait()
    sums = sums_ref[...].reshape(64, 128)
    d_local[...] = sums[:, 0:64]
    d_bias[...] = sums[0:1, 64:128]
    for copy in outs:
        copy.wait()


def results_call(out, d_spec, sums):
    vmem = pl.BlockSpec(memory_space=pltpu.VMEM)
    hbm = pl.BlockSpec(memory_space=pl.ANY)
    return pl.pallas_call(
        results_kernel,
        out_shape=(
            jax.ShapeDtypeStruct(out.shape, BF16),
            jax.ShapeDtypeStruct(d_spec.shape, F32),
            jax.ShapeDtypeStruct((64, 64), F32),
            jax.ShapeDtypeStruct((1, 64), F32),
        ),
        in_specs=[hbm] * 3,
        out_specs=(hbm, hbm, vmem, vmem),
        scratch_shapes=[
            pltpu.VMEM(out.shape, BF16),
            pltpu.VMEM(d_spec.shape, F32),
            pltpu.VMEM((8, 8, 128), F32),
            pltpu.SemaphoreType.DMA((11,)),
            pltpu.SemaphoreType.DMA((10,)),
        ],
        compiler_params=pltpu.CompilerParams(vmem_limit_bytes=58 * MIB),
    )(out, d_spec, sums)


def shards(base_field, cotangent, w_spec, w_local, bias, direction, shift):
    out, d_spec, sums = layer_call(
        base_field, cotangent[0], w_spec.reshape(16, 64, 128), w_local, direction.T, shift, bias
    )
    output, d_spec, d_local, d_bias = results_call(out, d_spec, sums)
    return (output[None], d_spec.reshape(4, 4, 64, 128), d_local, d_bias.reshape(64))


def solution(mesh):
    return jax.shard_map(
        shards,
        mesh=mesh,
        in_specs=(
            P(None, "slab", None, None),
            P("grp", None, "slab", None, None),
            P("grp", "slab", None, None),
            P(),
            P(),
            P(),
            P("grp", None),
        ),
        out_specs=(P("grp", None, "slab", None, None), P("grp", "slab", None, None), P(), P()),
        check_vma=False,
    )
```

```python
import functools
import math

import jax
import jax.numpy as jnp
import ml_dtypes
import numpy as np
from jax import lax
from jax.experimental import pallas as pl
from jax.experimental.pallas import tpu as pltpu
from jax.sharding import PartitionSpec as P

CH = 64
NX = 128
NY = 128
NZ = 128
MODES = 16
BITS = 30
N_GRP = 4
N_SLAB = 64
N_LOW = 8
N_Z = 8
MESH = pl.DeviceIdType.MESH
F32 = jnp.float32
BF16 = jnp.bfloat16
MIB = 1024 * 1024
GELU_K = math.sqrt(2.0 / math.pi)
GELU_A = 0.044715
GRAD_SCALE = 0.5 / math.sqrt(N_GRP * NX * NY * NZ)


def waves(length, half):
    ids = np.arange(MODES)
    if not half:
        ids = np.where(ids < MODES // 2, ids, length - MODES + ids)
    angles = 2.0 * math.pi / length * (ids[:, None] * np.arange(length)[None, :] % length)
    return np.cos(angles), np.sin(angles)


def as_bf16(table):
    return np.asarray(table, np.float32).astype(ml_dtypes.bfloat16)


def table_ty():
    cos_y, sin_y = waves(NY, False)
    out = np.zeros((2, 2, MODES, 2, NY))
    for c2 in range(2):
        out[0, c2, :, c2] = cos_y
        out[1, c2, :, c2] = sin_y
    return as_bf16(out.reshape(64, 256))


def weights_z(backward):
    return np.where(np.arange(MODES) == 0, 1.0, 2.0 if backward else 1.0)[:, None]


def table_zt(backward):
    cos_z, sin_z = waves(NZ, True)
    weight = weights_z(backward)
    if backward:
        weight = weight * GRAD_SCALE
    cos_z = (weight * cos_z).reshape(4, 4, NZ)
    sin_z = (weight * sin_z).reshape(4, 4, NZ)
    out = np.zeros((2, 4, 2, 4, 2, 2, NZ))
    for x in range(2):
        out[0, :, x, :, 0, x] = cos_z
        out[0, :, x, :, 1, x] = -sin_z
        out[1, :, x, :, 0, x] = -sin_z
        out[1, :, x, :, 1, x] = -cos_z
    return as_bf16(out.reshape(64, 512))


def table_tx():
    cos_x, sin_x = waves(NX, False)
    out = np.zeros((2, MODES, 4, NX, 4))
    for m in range(4):
        out[0, :, m, :, m] = cos_x
        out[1, :, m, :, m] = sin_x
    return as_bf16(out.reshape(128, 512))


def table_ey():
    cos_y, sin_y = waves(NY, False)
    out = np.zeros((2, NY, 2, 2, MODES))
    for c2 in range(2):
        out[c2, :, c2, 0] = cos_y.T
        out[c2, :, c2, 1] = -sin_y.T
    return as_bf16(out.reshape(256, 64))


def table_ez():
    cos_z, sin_z = waves(NZ, True)
    weight = weights_z(True) / math.sqrt(MODES**3)
    cos_z = (weight * cos_z).reshape(4, 4, NZ)
    sin_z = (weight * sin_z).reshape(4, 4, NZ)
    out = np.zeros((2, 4, 2, 4, 2, 2, NZ))
    for x in range(2):
        out[0, :, x, :, 0, x] = cos_z
        out[1, :, x, :, 0, x] = -sin_z
        out[0, :, x, :, 1, x] = sin_z
        out[1, :, x, :, 1, x] = cos_z
    return as_bf16(out.reshape(64, 512))


def lane_sign(rows, first, second):
    lane = lax.broadcasted_iota(jnp.int32, (rows, 128), 1)
    return jnp.where(lane < 64, first, second).astype(F32)


def turned(rows, first, second):
    return pltpu.roll(rows, 64, 1) * lane_sign(rows.shape[0], first, second)


def nt_dot(left, right, precision=None):
    return lax.dot_general(
        left, right, (((1,), (1,)), ((), ())), preferred_element_type=F32, precision=precision
    )


def fetch_field(field, held, sems):
    for part in range(8):
        rows = pl.ds(8 * part, 8)
        pltpu.make_async_copy(field.at[rows], held.at[rows], sems.at[part]).start()


def wait_field(field, held, sems, part):
    rows = pl.ds(8 * part, 8)
    pltpu.make_async_copy(field.at[rows], held.at[rows], sems.at[part]).wait()


def store_along_y(along_y, got, first):
    for cs in range(2):
        for c2 in range(2):
            at = cs * 32 + c2 * 16
            for x in range(2):
                start = (2 * cs + x) * 1024 + first + c2
                along_y[pl.ds(start, 16, stride=64), :] = got[
                    at : at + 16, x * 128 : x * 128 + 128
                ]


def along_z_half(half, along_y, zt_ref, modes_z):
    for part in range(2):
        rows = jnp.concatenate(
            [
                jnp.concatenate(
                    [
                        along_y[
                            cs_x * 1024 + jy * 64 + half * 32 : cs_x * 1024 + jy * 64 + half * 32 + 32,
                            :,
                        ]
                        for jy in range(part * 8, part * 8 + 8)
                    ],
                    0,
                ).astype(BF16)
                for cs_x in range(4)
            ],
            1,
        )
        modes_z[half, part] = nt_dot(zt_ref[...], rows)


def join_halves(modes_z, slab_modes):
    for jy in range(16):
        lanes = slice((jy % 8) * 32, (jy % 8) * 32 + 32)
        block = jnp.concatenate(
            [
                modes_z[half, jy // 8, re * 32 : re * 32 + 32, lanes]
                for re in range(2)
                for half in range(2)
            ],
            1,
        )
        slab_modes[jy * 4 : jy * 4 + 4] = block.reshape(4, 8, 128).astype(BF16)


def greetings(barrier, me, grp, low, z):
    def tell(device):
        pl.semaphore_signal(barrier, inc=1, device_id=device, device_id_type=MESH)

    calls = []
    for dz in (4, 3, 5, 2, 6, 1, 7, 0):
        other_z = lax.rem(z + dz, N_Z) * N_LOW
        for g_step in (2, 1, 3):
            calls.append(
                functools.partial(
                    tell, {"grp": lax.rem(grp + g_step, N_GRP), "slab": other_z + low}
                )
            )
        for step in (4, 5, 2, 3, 6, 7, 1, 0):
            if dz or step:
                calls.append(
                    functools.partial(tell, {"slab": other_z + lax.rem(low + step, N_LOW)})
                )
    return calls


def send_all(source, target, send_sem, recv_sem, me):
    low = lax.rem(me, N_LOW)
    z = me // N_LOW
    for dz in (4, 3, 5, 2, 6, 1, 7, 0):

        def go(step, carry):
            other = lax.rem(z + dz, N_Z) * N_LOW + lax.rem(low + step, N_LOW)
            pltpu.make_async_remote_copy(
                src_ref=source.at[other],
                dst_ref=target.at[me],
                send_sem=send_sem,
                recv_sem=recv_sem,
                device_id={"slab": other},
                device_id_type=MESH,
            ).start()
            return carry

        lax.fori_loop(1 if dz == 0 else 0, N_LOW, go, 0)
    target[pl.ds(me, 1)] = source[pl.ds(me, 1)]


def wait_blocks(source, target, send_sem, recv_sem, count, me):
    pltpu.make_async_remote_copy(
        src_ref=source.at[pl.ds(0, count)],
        dst_ref=target.at[pl.ds(0, count)],
        send_sem=send_sem,
        recv_sem=recv_sem,
        device_id={"slab": me},
        device_id_type=MESH,
    ).wait()


def send_grp(source, target, send_sem, recv_sem, grp, by_target):
    for step in (2, 1, 3):
        other = lax.rem(grp + step, N_GRP)
        pltpu.make_async_remote_copy(
            src_ref=source.at[other] if by_target else source.at[grp],
            dst_ref=target.at[grp],
            send_sem=send_sem,
            recv_sem=recv_sem,
            device_id={"grp": other},
            device_id_type=MESH,
        ).start()


def x_modes(pencil, tx_ref):
    rows = pencil[...].astype(F32).reshape(512, 128).astype(BF16)
    both = jnp.dot(tx_ref[...], rows, preferred_element_type=F32)
    return both[:64] + turned(both[64:], 1.0, -1.0)


def local_step(part, held, kron, bias_rows, field_rows, local):
    y_at = pl.multiple_of(16 * part, 16)
    halves = [held[:, x, pl.ds(y_at, 16), :].astype(F32) for x in range(2)]
    for half in range(2):
        rows = jnp.concatenate(
            [block[:, 8 * half : 8 * half + 8].reshape(512, 128) for block in halves], 1
        ).astype(BF16)
        field_rows[part, :, half * 256 : half * 256 + 256] = rows
        got = jnp.dot(kron[...], rows, preferred_element_type=F32)
        added = bias_rows[...]
        local[:, pl.ds(pl.multiple_of(y_at + 8 * half, 8), 8), :] = got.reshape(
            64, 8, 256
        ) + jnp.concatenate([added, added], 2)


def scale_rows(grp, direction_ref, shift_ref):
    number = grp + 1
    gray_code = number ^ (number >> 1)
    bits = shift_ref[...]
    for bit_pos in range(N_GRP.bit_length()):
        bits = bits ^ (direction_ref[bit_pos : bit_pos + 1, :] * ((gray_code >> bit_pos) & 1))
    scale = 0.5 + bits.astype(F32) * 2.0 ** (-BITS)
    return jnp.broadcast_to(jnp.concatenate([scale, scale], 1), (8, 128))


def fill_kron(wl_ref, scale_row, kron):
    local = (wl_ref[...].astype(F32) * scale_row[0:1, 0:64]).astype(BF16)
    pick = (
        lax.broadcasted_iota(jnp.int32, (64, 512), 0)
        == lax.broadcasted_iota(jnp.int32, (64, 512), 1) // 8
    )
    wide = jnp.dot(local, pick.astype(F32).astype(BF16), preferred_element_type=F32).astype(BF16)
    same = (
        lax.broadcasted_iota(jnp.int32, (64, 512), 0) % 8
        == lax.broadcasted_iota(jnp.int32, (64, 512), 1) % 8
    )
    row_ids = lax.broadcasted_iota(jnp.int32, (64, 64), 0) // 8
    col_ids = lax.broadcasted_iota(jnp.int32, (64, 64), 1)
    for octet in range(8):
        rows_of = (row_ids + 8 * octet == col_ids).astype(F32).astype(BF16)
        tall = jnp.dot(rows_of, wide, preferred_element_type=F32)
        kron[octet * 64 : octet * 64 + 64, :] = jnp.where(same, tall, 0.0).astype(BF16)


def fill_along_z(landed, ez_ref, along_z):
    for quarter in range(4):
        rows = landed[quarter * 16 : quarter * 16 + 16].astype(F32).reshape(128, 128)
        turn = rows.T
        per_c = jnp.concatenate(
            [
                jnp.concatenate(
                    [turn[0:64, jy * 32 : jy * 32 + 32], turn[64:128, jy * 32 : jy * 32 + 32]], 1
                )
                for jy in range(4)
            ],
            0,
        ).astype(BF16)
        got = jnp.dot(per_c, ez_ref[...], preferred_element_type=F32)
        for jy in range(4):
            for cs in range(2):
                for x in range(2):
                    start = x * 2048 + cs * 16 + quarter * 4 + jy
                    lane = cs * 256 + x * 128
                    along_z[pl.ds(start, 64, stride=32), :] = got[
                        jy * 64 : jy * 64 + 64, lane : lane + 128
                    ]


def synthesis(group, along_z, local, ey_ref, pre_act):
    rows = jnp.concatenate(
        [
            along_z[pl.ds(x * 2048 + 256 * group + 64 * pair, 64), :].astype(BF16)
            for pair in range(4)
            for x in range(2)
        ],
        1,
    )
    got = jnp.dot(ey_ref[...], rows, preferred_element_type=F32)
    for pair in range(4):
        for c2 in range(2):
            at = slice(c2 * 128, c2 * 128 + 128)
            lanes = slice(pair * 256, pair * 256 + 256)
            pre_act[at, lanes] = (
                got[at, lanes] + local[8 * group + 2 * pair + c2]
            ).astype(BF16)


def activation(group, pre_act, cotan_in, out_held, cotan_pre):
    for pair in range(4):
        for c2 in range(2):
            for x in range(2):
                channel = 8 * group + 2 * pair + c2
                at = slice(c2 * 128, c2 * 128 + 128)
                lanes = slice(pair * 256 + x * 128, pair * 256 + x * 128 + 128)
                pre = pre_act[at, lanes]
                square = pre * pre
                inner = pre * (1.0 + GELU_A * square)
                tanh = jnp.tanh(inner.astype(F32) * GELU_K)
                above = 1.0 + tanh
                bell = (above * (1.0 - tanh)).astype(BF16)
                above = above.astype(BF16)
                out_held[channel, x] = (0.5 * pre) * above
                slope = above + bell * (pre * (GELU_K + (3.0 * GELU_K * GELU_A) * square))
                cotan_pre[at, lanes] = slope * cotan_in[channel, x]


def gradient_modes(group, cotan_pre, ty_ref, cotan_rows, along_y):
    got = jnp.dot(ty_ref[...], cotan_pre[...], preferred_element_type=F32)
    for pair in range(4):
        store_along_y(along_y, got[:, pair * 256 : pair * 256 + 256], 8 * group + 2 * pair)
    for pair in range(4):
        for x in range(2):
            lanes = slice(pair * 256 + x * 128, pair * 256 + x * 128 + 128)
            wide = cotan_pre[:, lanes].astype(F32)
            for y8 in range(16):
                block = jnp.concatenate(
                    [wide[c2 * 128 + 8 * y8 : c2 * 128 + 8 * y8 + 8] for c2 in range(2)], 0
                )
                lane = (y8 % 2) * 256 + x * 128
                cotan_rows[
                    y8 // 2, pl.ds(64 * group + 16 * pair, 16), lane : lane + 128
                ] = block.astype(BF16)


def local_grad(grad):
    same = (
        lax.broadcasted_iota(jnp.int32, (256, 512), 0) % 8
        == lax.broadcasted_iota(jnp.int32, (256, 512), 1) % 8
    )
    kept = jnp.where(same, grad, 0.0)
    high = kept.astype(BF16)
    low = (kept - high.astype(F32)).astype(BF16)
    pick = (
        lax.broadcasted_iota(jnp.int32, (512, 64), 0) // 8
        == lax.broadcasted_iota(jnp.int32, (512, 64), 1)
    )
    pick = pick.astype(F32).astype(BF16)
    got = jnp.dot(high, pick, preferred_element_type=F32) + jnp.dot(
        low, pick, preferred_element_type=F32
    )
    return jnp.sum(got.reshape(32, 8, 64), axis=1)


def fill_terms(shifted_modes, terms):
    turn = shifted_modes[...].T
    columns = jnp.concatenate([turn[0:64], turn[64:128]], 1)
    mode = lax.broadcasted_iota(jnp.int32, (64, 128), 1) % 16
    for k in range(16):
        terms[k * 64 : k * 64 + 64, :] = jnp.where(mode == k, columns, 0.0).astype(BF16)


def weight_terms(gathered_g, terms, d_spec):
    rows = gathered_g[...].reshape(64, 128)
    both = jnp.concatenate([rows, turned(rows.astype(F32), 1.0, -1.0).astype(BF16)], 0)
    got = jnp.dot(terms[...], both, preferred_element_type=F32)
    d_spec[...] = got.reshape(16, 64, 128)


def layer_kernel(
    field, cotan, w_hbm, wl_hbm, direction_hbm, shift_hbm, bias_ref,
    ty_hbm, ztf_hbm, ztb_hbm, tx_hbm, txb_hbm, ey_hbm, ez_hbm,
    out_hbm, spec_hbm, sums_out,
    ty_ref, ztf_ref, ztb_ref, tx_ref, txb_ref, ey_ref, ez_ref, w_ref, wl_ref, direction_ref, shift_ref, scale_ref,
    held, cotan_in, out_held, field_rows, cotan_rows, local, along_y, along_z, kron, w_two,
    d_spec, terms, modes_z, grad, pre_even, pre_odd, cotan_even, cotan_odd, bias_rows,
    slab_modes, pencil, mixed, gathered, back, landed, slab_g, pencil_g, mixed_g, gathered_g,
    all_modes, shifted_modes, scale_own, scale_all, own_sums, first, second, second_own, third,
    field_sems, cotan_sems, table_sems, out_sems, send_sems, recv_sems,
):
    me = lax.axis_index("slab")
    grp = lax.axis_index("grp")
    low = lax.rem(me, N_LOW)
    z = me // N_LOW
    barrier = pltpu.get_barrier_semaphore()
    small = [
        (ty_hbm, ty_ref), (ztf_hbm, ztf_ref), (direction_hbm, direction_ref), (wl_hbm, wl_ref),
        (w_hbm, w_ref), (tx_hbm, tx_ref), (txb_hbm, txb_ref), (ey_hbm, ey_ref),
        (ez_hbm, ez_ref), (ztb_hbm, ztb_ref), (shift_hbm, shift_ref),
    ]
    copies = [
        pltpu.make_async_copy(source, target, table_sems.at[at])
        for at, (source, target) in enumerate(small)
    ]
    for copy in copies[:2]:
        copy.start()
    fetch_field(field, held, field_sems)
    for copy in copies[2:]:
        copy.start()
    calls = greetings(barrier, me, grp, low, z)

    for call in calls[:15]:
        call()
    copies[0].wait()

    for part in range(8):
        for call in calls[15 * part + 15 : 15 * part + 30]:
            call()
        wait_field(field, held, field_sems, part)
        rows = jnp.concatenate(
            [
                jnp.concatenate([held[8 * part + 2 * pair + c2, x] for c2 in range(2)], 0)
                for pair in range(4)
                for x in range(2)
            ],
            1,
        )
        got = jnp.dot(ty_ref[...], rows, preferred_element_type=F32)
        for pair in range(4):
            store_along_y(along_y, got[:, pair * 256 : pair * 256 + 256], 8 * part + 2 * pair)
        if part == 3:
            copies[1].wait()
            along_z_half(0, along_y, ztf_ref, modes_z)
    along_z_half(1, along_y, ztf_ref, modes_z)
    join_halves(modes_z, slab_modes)
    copies[2].wait()
    copies[10].wait()
    scale_ref[...] = scale_rows(grp, direction_ref, shift_ref)
    scale_own[grp] = scale_ref[...]
    scale_all[grp] = scale_ref[...]
    pl.semaphore_wait(barrier, N_SLAB - 1 + N_GRP - 1 + (N_GRP - 1) * (N_Z - 1))
    send_all(slab_modes, pencil, send_sems.at[0], recv_sems.at[0], me)
    send_grp(scale_own, scale_all, send_sems.at[1], recv_sems.at[1], grp, False)
    fetch_field(cotan, cotan_in, cotan_sems)

    copies[3].wait()
    copies[4].wait()
    for k in range(16):
        block = w_ref[k].astype(F32)
        w_two[k * 128 : k * 128 + 64, :] = w_ref[k]
        w_two[k * 128 + 64 : k * 128 + 128, :] = turned(block, -1.0, 1.0).astype(BF16)
    fill_kron(wl_ref, scale_ref[...], kron)
    for channel in range(CH):
        bias_rows[channel] = jnp.full((8, 128), bias_ref[channel], F32)

    def local_some(part, carry):
        local_step(part, held, kron, bias_rows, field_rows, local)
        return carry

    lax.fori_loop(0, 1, local_some, 0)
    pltpu.make_async_remote_copy(
        src_ref=scale_own.at[pl.ds(0, N_GRP - 1)],
        dst_ref=scale_all.at[pl.ds(0, N_GRP - 1)],
        send_sem=send_sems.at[1],
        recv_sem=recv_sems.at[1],
        device_id={"slab": me},
        device_id_type=MESH,
    ).wait()
    copies[5].wait()
    copies[6].wait()
    wait_blocks(slab_modes, pencil, send_sems.at[0], recv_sems.at[0], N_SLAB - 1, me)

    all_modes[...] = x_modes(pencil, tx_ref) * (1.0 / math.sqrt(NX * NY * NZ))
    own = all_modes[pl.ds(pl.multiple_of(16 * grp, 16), 16), :]
    shifted = jnp.concatenate([own * scale_all[s, 0:1, :] for s in range(N_GRP)], 0)
    shifted_modes[...] = shifted
    row_mode = lax.broadcasted_iota(jnp.int32, (64, 128), 0) % 16
    spread = jnp.concatenate(
        [jnp.where(row_mode == k, shifted, 0.0).astype(BF16) for k in range(16)], 1
    )
    mixed[...] = (
        jnp.dot(spread, w_two[...], preferred_element_type=F32).astype(BF16).reshape(4, 16, 128)
    )
    send_grp(mixed, gathered, send_sems.at[2], recv_sems.at[2], grp, True)
    gathered[pl.ds(grp, 1)] = mixed[pl.ds(grp, 1)]
    lax.fori_loop(1, 5, local_some, 0)
    wait_blocks(mixed, gathered, send_sems.at[2], recv_sems.at[2], N_GRP - 1, me)
    full = gathered[...].reshape(64, 128)
    both = jnp.concatenate([full, turned(full.astype(F32), -1.0, 1.0).astype(BF16)], 0)
    back[...] = (
        jnp.dot(txb_ref[...], both, preferred_element_type=F32).reshape(64, 8, 128).astype(BF16)
    )
    send_all(back, landed, send_sems.at[3], recv_sems.at[3], me)
    lax.fori_loop(5, 8, local_some, 0)
    fill_terms(shifted_modes, terms)
    for copy in copies[7:10]:
        copy.wait()
    for part in range(8):
        wait_field(cotan, cotan_in, cotan_sems, part)
    wait_blocks(back, landed, send_sems.at[3], recv_sems.at[3], N_SLAB - 1, me)

    fill_along_z(landed, ez_ref, along_z)

    slots = ((pre_even, cotan_even), (pre_odd, cotan_odd))
    for step in range(10):
        if step < 8:
            synthesis(step, along_z, local, ey_ref, slots[step % 2][0])
        if 0 < step < 9:
            pre_act, cotan_pre = slots[(step - 1) % 2]
            activation(step - 1, pre_act, cotan_in, out_held, cotan_pre)
            rows = pl.ds(8 * (step - 1), 8)
            pltpu.make_async_copy(
                out_held.at[rows], out_hbm.at[rows], out_sems.at[step - 1]
            ).start()
        if step > 1:
            gradient_modes(
                step - 2, slots[step % 2][1], ty_ref, cotan_rows, along_y
            )
        if step == 5:
            along_z_half(0, along_y, ztb_ref, modes_z)
            grad[...] = jnp.zeros_like(grad)
        if step > 5:
            for part in (2 * step - 12, 2 * step - 11):
                grad[...] += nt_dot(cotan_rows[part, 0:256, :], field_rows[part])

    d_top = local_grad(grad[...])
    bottom = jnp.zeros((256, 512), F32)
    for part in range(8):
        bottom = bottom + nt_dot(cotan_rows[part, 256:512, :], field_rows[part])
    d_local = jnp.concatenate([d_top, local_grad(bottom)], 0)
    d_local = d_local * (scale_ref[0:1, 0:64] * GRAD_SCALE)
    lanes = along_y[0:64, :] + along_y[1024:1088, :]
    d_bias = nt_dot(jnp.full((8, 128), GRAD_SCALE, F32), lanes, lax.Precision.HIGHEST)
    side = jnp.concatenate([d_bias, jnp.zeros((56, 64), F32)], 0)
    own_sums[...] = jnp.concatenate([d_local, side], 1).reshape(8, 8, 128)

    def scatter(step, carry):
        other = lax.rem(low + step, N_LOW)
        pltpu.make_async_remote_copy(
            src_ref=own_sums.at[other],
            dst_ref=first.at[low],
            send_sem=send_sems.at[4],
            recv_sem=recv_sems.at[4],
            device_id={"slab": z * N_LOW + other},
            device_id_type=MESH,
        ).start()
        return carry

    lax.fori_loop(1, N_LOW, scatter, 0)
    first[pl.ds(low, 1)] = own_sums[pl.ds(low, 1)]
    along_z_half(1, along_y, ztb_ref, modes_z)
    join_halves(modes_z, slab_g)
    send_all(slab_g, pencil_g, send_sems.at[5], recv_sems.at[5], me)
    wait_blocks(own_sums, first, send_sems.at[4], recv_sems.at[4], N_LOW - 1, me)
    part_sum = jnp.sum(first[...], axis=0, keepdims=True)
    mine = grp * N_Z + z
    second[pl.ds(mine, 1)] = part_sum
    second_own[...] = part_sum
    for g_step in (2, 1, 3, 0):

        def spread_sum(step, carry):
            pltpu.make_async_remote_copy(
                src_ref=second_own.at[0],
                dst_ref=second.at[mine],
                send_sem=send_sems.at[6],
                recv_sem=recv_sems.at[6],
                device_id={
                    "grp": lax.rem(grp + g_step, N_GRP),
                    "slab": lax.rem(z + step, N_Z) * N_LOW + low,
                },
                device_id_type=MESH,
            ).start()
            return carry

        lax.fori_loop(1 if g_step == 0 else 0, N_Z, spread_sum, 0)
    wait_blocks(slab_g, pencil_g, send_sems.at[5], recv_sems.at[5], N_SLAB - 1, me)
    mixed_g[...] = x_modes(pencil_g, tx_ref).astype(BF16).reshape(4, 16, 128)
    send_grp(mixed_g, gathered_g, send_sems.at[7], recv_sems.at[7], grp, True)
    gathered_g[pl.ds(grp, 1)] = mixed_g[pl.ds(grp, 1)]
    wait_blocks(second, second, send_sems.at[6], recv_sems.at[6], N_GRP * N_Z - 1, me)
    third[...] = jnp.sum(second[...], axis=0, keepdims=True)
    own_copy = pltpu.make_async_copy(third.at[0], sums_out.at[low], out_sems.at[9])
    own_copy.start()

    def collect(step, carry):
        pltpu.make_async_remote_copy(
            src_ref=third.at[0],
            dst_ref=sums_out.at[low],
            send_sem=send_sems.at[8],
            recv_sem=recv_sems.at[8],
            device_id={"slab": z * N_LOW + lax.rem(low + step, N_LOW)},
            device_id_type=MESH,
        ).start()
        return carry

    lax.fori_loop(1, N_LOW, collect, 0)
    wait_blocks(mixed_g, gathered_g, send_sems.at[7], recv_sems.at[7], N_GRP - 1, me)
    weight_terms(gathered_g, terms, d_spec)
    spec_copy = pltpu.make_async_copy(d_spec, spec_hbm, out_sems.at[8])
    spec_copy.start()
    for part in range(8):
        rows = pl.ds(8 * part, 8)
        pltpu.make_async_copy(out_held.at[rows], out_hbm.at[rows], out_sems.at[part]).wait()
    wait_blocks(sums_out, sums_out, send_sems.at[8], recv_sems.at[8], N_LOW - 1, me)
    own_copy.wait()
    spec_copy.wait()


def layer_call(field, cotangent, w_spec, w_local, direction, shift, bias):
    hbm = pl.BlockSpec(memory_space=pl.ANY)
    tables = (
        table_ty(), table_zt(False), table_zt(True), table_tx(),
        np.ascontiguousarray(table_tx().T), table_ey(), table_ez(),
    )
    cells = (64, 2, 128, 128)
    blocks = pltpu.VMEM((64, 8, 128), BF16)
    quads = pltpu.VMEM((4, 16, 128), BF16)
    return pl.pallas_call(
        layer_kernel,
        out_shape=(
            jax.ShapeDtypeStruct(cells, BF16),
            jax.ShapeDtypeStruct((16, 64, 128), F32),
            jax.ShapeDtypeStruct((8, 8, 128), F32),
        ),
        in_specs=[hbm] * 6 + [pl.BlockSpec(memory_space=pltpu.SMEM)] + [hbm] * 7,
        out_specs=(hbm,) * 3,
        scratch_shapes=[pltpu.VMEM(table.shape, BF16) for table in tables]
        + [
            pltpu.VMEM((16, 64, 128), BF16),
            pltpu.VMEM((64, 64), BF16),
            pltpu.VMEM((BITS, 64), jnp.int32),
            pltpu.VMEM((1, 64), jnp.int32),
            pltpu.VMEM((8, 128), F32),
            pltpu.VMEM(cells, BF16),
            pltpu.VMEM(cells, BF16),
            pltpu.VMEM(cells, BF16),
            pltpu.VMEM((8, 512, 512), BF16),
            pltpu.VMEM((8, 512, 512), BF16),
            pltpu.VMEM((64, 128, 256), F32),
            pltpu.VMEM((4096, 128), F32),
            pltpu.VMEM((4096, 128), F32),
            pltpu.VMEM((512, 512), BF16),
            pltpu.VMEM((2048, 128), BF16),
            pltpu.VMEM((16, 64, 128), F32),
            pltpu.VMEM((1024, 128), BF16),
            pltpu.VMEM((2, 2, 64, 256), F32),
            pltpu.VMEM((256, 512), F32),
            pltpu.VMEM((256, 1024), BF16),
            pltpu.VMEM((256, 1024), BF16),
            pltpu.VMEM((256, 1024), BF16),
            pltpu.VMEM((256, 1024), BF16),
            pltpu.VMEM((64, 8, 128), F32),
            blocks, blocks, quads, quads, blocks, blocks, blocks, blocks, quads, quads,
            pltpu.VMEM((64, 128), F32),
            pltpu.VMEM((64, 128), F32),
            pltpu.VMEM((4, 8, 128), F32),
            pltpu.VMEM((4, 8, 128), F32),
            pltpu.VMEM((8, 8, 128), F32),
            pltpu.VMEM((8, 8, 128), F32),
            pltpu.VMEM((32, 8, 128), F32),
            pltpu.VMEM((1, 8, 128), F32),
            pltpu.VMEM((1, 8, 128), F32),
            pltpu.SemaphoreType.DMA((8,)),
            pltpu.SemaphoreType.DMA((8,)),
            pltpu.SemaphoreType.DMA((11,)),
            pltpu.SemaphoreType.DMA((10,)),
            pltpu.SemaphoreType.DMA((9,)),
            pltpu.SemaphoreType.DMA((9,)),
        ],
        compiler_params=pltpu.CompilerParams(
            collective_id=0, has_side_effects=True, vmem_limit_bytes=58 * MIB
        ),
    )(field, cotangent, w_spec, w_local, direction, shift, bias, *tables)


def results_kernel(
    out_hbm, spec_hbm, sums_hbm,
    output, spec_out, d_local, d_bias,
    held, spec_held, sums_ref, in_sems, out_sems,
):
    moves = []
    for part in range(2):
        rows = pl.ds(8 * part, 8)
        moves.append((spec_hbm.at[rows], spec_held.at[rows], spec_out.at[rows]))
    for part in range(16):
        rows = pl.ds(4 * part, 4)
        moves.append((out_hbm.at[rows], held.at[rows], output.at[rows]))
    ins = [
        pltpu.make_async_copy(source, middle, in_sems.at[at])
        for at, (source, middle, _) in enumerate(moves)
    ]
    outs = [
        pltpu.make_async_copy(middle, target, out_sems.at[at])
        for at, (_, middle, target) in enumerate(moves)
    ]
    sums_copy = pltpu.make_async_copy(sums_hbm, sums_ref, in_sems.at[18])
    for copy in ins:
        copy.start()
    sums_copy.start()
    for before, after in zip(ins, outs):
        before.wait()
        after.start()
    sums_copy.wait()
    sums = sums_ref[...].reshape(64, 128)
    d_local[...] = sums[:, 0:64]
    d_bias[...] = sums[0:1, 64:128]
    for copy in outs:
        copy.wait()


def results_call(out, d_spec, sums):
    vmem = pl.BlockSpec(memory_space=pltpu.VMEM)
    hbm = pl.BlockSpec(memory_space=pl.ANY)
    return pl.pallas_call(
        results_kernel,
        out_shape=(
            jax.ShapeDtypeStruct(out.shape, BF16),
            jax.ShapeDtypeStruct(d_spec.shape, F32),
            jax.ShapeDtypeStruct((64, 64), F32),
            jax.ShapeDtypeStruct((1, 64), F32),
        ),
        in_specs=[hbm] * 3,
        out_specs=(hbm, hbm, vmem, vmem),
        scratch_shapes=[
            pltpu.VMEM(out.shape, BF16),
            pltpu.VMEM(d_spec.shape, F32),
            pltpu.VMEM((8, 8, 128), F32),
            pltpu.SemaphoreType.DMA((19,)),
            pltpu.SemaphoreType.DMA((18,)),
        ],
        compiler_params=pltpu.CompilerParams(vmem_limit_bytes=58 * MIB),
    )(out, d_spec, sums)


def shards(base_field, cotangent, w_spec, w_local, bias, direction, shift):
    out, d_spec, sums = layer_call(
        base_field, cotangent[0], w_spec.reshape(16, 64, 128), w_local, direction.T, shift, bias
    )
    output, d_spec, d_local, d_bias = results_call(out, d_spec, sums)
    return (output[None], d_spec.reshape(4, 4, 64, 128), d_local, d_bias.reshape(64))


def solution(mesh):
    return jax.shard_map(
        shards,
        mesh=mesh,
        in_specs=(
            P(None, "slab", None, None),
            P("grp", None, "slab", None, None),
            P("grp", "slab", None, None),
            P(),
            P(),
            P(),
            P("grp", None),
        ),
        out_specs=(P("grp", None, "slab", None, None), P("grp", "slab", None, None), P(), P()),
        check_vma=False,
    )
```
